256 devices in a mesh: band: 16 (over x, y), sector: 8 (over z), chan: 2 (over core).
Axes of the slice: x: 4, y: 4, z: 8, core: 2. Of those that a mesh axis runs over, the one named last changes fastest.
Arguments:
- obs_features: bfloat16 [131072, 256], P(('band', 'sector')), may hold values from -6 to 6
- obs_owner: int32 [131072, 1], P(('band', 'sector')), may hold values from 0 to 127; in each aligned block of 1024 rows (0 to 1023, 1024 to 2047, ...) at most 12 rows name the same one
- obs_node: int32 [131072], P(('band', 'sector')), may hold values from 0 to 1279
- obs_count: int32 [128], P(('band', 'sector')), may hold values from 3 to 8, as said below
- edge_senders: int32 [983040], P(('band', 'sector')), may hold values from 0 to 4159, as said below
- obs_in_w: bfloat16 [256, 256], replicated, may hold values from -0.375 to 0.375
- obs_in_b: float32 [256], replicated, may hold values from -3 to 3
- obs_out_w: bfloat16 [256, 256], replicated, may hold values from -0.375 to 0.375
- enc_w: bfloat16 [256, 1024], P(None, 'chan'), may hold values from -0.375 to 0.375
- enc_b: float32 [1024], P('chan'), may hold values from -3 to 3
- node_base: bfloat16 [163840, 1024], P(('band', 'sector'), 'chan'), may hold values from -6 to 6
- recv_w: bfloat16 [1024, 1024], P('chan'), may hold values from -0.1875 to 0.1875
- send_w: bfloat16 [1024, 1024], P('chan'), may hold values from -0.1875 to 0.1875
- edge_b: float32 [1024], P('chan'), may hold values from -3 to 3
- channel_scale: float32 [1024], P('chan'), may hold values from 0.25 to 2.75, as said below
- norm_gain: float32 [1024], P('chan'), may hold values from 0.1 to 1.9
Outputs:
- mesh_out: bfloat16 [163840, 1024], P(('band', 'sector'), 'chan')
The draws below stay inside these ranges and needn't reach their ends.
Inputs may be any that keep to these rules, and one draw needn't show every extreme that they name: `obs_owner`: among the 1024 observations of one device, each owner is named at most 12 times. `obs_count`: some device has all 8 pieces live in every draw. `edge_senders`: values under 1280 name the device's own nodes; larger ones name a boundary node of one of the eight neighbouring blocks; no edge of the first band reads the band before it, none of the last band the band after it, and the centre group is never named. `channel_scale`: positive.
All inputs are finite; a program needn't handle non-finite values.
Results may differ from the reference program's by a relative error of at most 0.0075.
Values may be sent and summed in bfloat16 or wider, within the bound.
A program may use at most 128 MiB of HBM per device.

```python
import math
import jax
import jax.numpy as jnp
import numpy as np
from jax import lax

E = 256
L = 1024
OBS_DEV = 1024
NODE_DEV = 1280
PIECES = 8
DEGREE = 6
BANDS = 16
SECTORS = 8
GEO = 128
CAP = 12
HALO = 320
EDGE_DEV = 7680
OBS = 131072
NODES = 163840


def draw_obs_count(key, part):
    key = jax.random.fold_in(key, 5)
    key_counts, key_full = jax.random.split(key)
    counts = jax.random.randint(key_counts, (GEO,), 3, PIECES + 1)
    full_device = jax.random.randint(key_full, (), 0, GEO)
    return jnp.where(jnp.arange(GEO) == full_device, PIECES, counts).astype(jnp.int32)


def draw_edge_senders(key, part):
    key = jax.random.fold_in(key, 11)
    key_own, key_pick, key_far, key_use = jax.random.split(key, 4)
    total = GEO * EDGE_DEV
    device = jnp.arange(total) // EDGE_DEV
    band_index = device // SECTORS
    own_node = jax.random.randint(key_own, (total,), 0, NODE_DEV)
    pick = jax.random.randint(key_pick, (total,), 0, 8)
    group = pick + (pick >= 4).astype(jnp.int32)
    row_part = group // 3
    col_part = group % 3
    row_part = jnp.where((band_index == 0) & (row_part == 0), 2, row_part)
    row_part = jnp.where((band_index == BANDS - 1) & (row_part == 2), 0, row_part)
    far_node = jax.random.randint(key_far, (total,), 0, HALO)
    remote = NODE_DEV + (row_part * 3 + col_part) * HALO + far_node
    use_own = jax.random.randint(key_use, (total,), 0, 5) < 3
    result = jnp.where(use_own, own_node, remote)
    result = result.at[0].set(NODE_DEV + 9 * HALO - 1)
    result = result.at[1].set(0)
    return result.astype(jnp.int32)


def draw_channel_scale(key, part):
    key = jax.random.fold_in(key, 7)
    ramp = jnp.exp(jnp.log(3.0) * jnp.arange(L, dtype=jnp.float32) / L)
    jitter = jnp.exp(jax.random.uniform(key, (L,), jnp.float32, -0.6, 0.6))
    return (0.5 * ramp * jitter).astype(jnp.float32)


def set_ends(values, stream_key, low, top_value):
    spot = [jax.random.randint(jax.random.fold_in(stream_key, axis), (), 0, length) for axis, length in enumerate(values.shape)]
    widest = values.shape.index(max(values.shape))
    next_to = spot[:widest] + [(spot[widest] + 1) % values.shape[widest]] + spot[widest + 1:]
    return values.at[tuple(spot)].set(low).at[tuple(next_to)].set(top_value)


def shard_levels(own_key, dims, pieces, smallest, top_value):
    level = 1.0
    for dim, shards_of in pieces:
        heights = jax.random.uniform(jax.random.fold_in(jax.random.fold_in(own_key, 6), dim), (shards_of,), jnp.float32, smallest / len(pieces), top_value / len(pieces))
        level = level * jnp.repeat(jnp.exp(heights), dims[dim] // shards_of).reshape((-1,) + (1,) * (len(dims) - 1 - dim))
    return level


def shared_out(own_key, own, number, rows, amount, top, bound, skew):
    order = jax.random.permutation(own_key, amount)
    packed, ordinary = load_shares(amount, rows * top, bound, skew, True), load_shares(amount, rows * top, bound, skew, False)
    places = jnp.arange(amount)

    def named(lengths, rotation):
        used = int((lengths > 0).sum())
        fixed = max(1, used // 4)
        passed = fixed + (places - fixed + rotation * (used - fixed)) % max(1, amount - fixed)
        return jnp.zeros((amount,), jnp.int32).at[order[jnp.where(places < fixed, places, passed)]].set(jnp.asarray(lengths, jnp.int32))

    lengths = jnp.where(number % 4 == 0, named(packed, number // 4), named(ordinary, number - number // 4 - 1))
    mixed = jax.random.permutation(jax.random.fold_in(own, 3), amount)
    giver, taker = mixed[0:amount // 2 * 2:2], mixed[1:amount // 2 * 2:2]
    room = jnp.minimum(lengths[giver] - 1, bound - lengths[taker]) // 2
    room = jnp.where((giver == order[0]) | (taker == order[0]) | (lengths[taker] == 0), 0, jnp.maximum(room, 0))
    passed = jax.random.randint(jax.random.fold_in(own, 4), (amount // 2,), 0, 1 << 20) % (room + 1)
    lengths = lengths.at[giver].add(-passed).at[taker].add(passed)
    labels = jnp.searchsorted(jnp.cumsum(lengths), jnp.arange(rows * top), side="right").astype(jnp.int32)
    table = labels.reshape(top, rows).T
    table = table[jax.random.permutation(jax.random.fold_in(own, 1), rows)]
    rotation = jax.random.randint(jax.random.fold_in(own, 2), (rows, 1), 0, top)
    return jnp.take_along_axis(table, (jnp.arange(top)[None, :] + rotation) % top, axis=1)


def load_shares(number_of, total, limit, skew, full):
    portions = [(1 << 20) // math.isqrt(grade ** skew) + 1 for grade in range(1, number_of + 1)]
    largest = limit if full else min(limit, max(-(-total // number_of), total * portions[0] // sum(portions)))
    least = 1 if total - largest >= number_of - 1 else 0
    given, rest = [largest] + [least] * (number_of - 1), total - largest - least * (number_of - 1)
    while rest > 0:
        movable = [i for i in range(1, number_of) if given[i] < largest] or [i for i in range(1, number_of) if given[i] < limit]
        pool, budget = sum([portions[i] for i in movable]), rest
        for i in movable:
            addition = min(limit - given[i], max(1, budget * portions[i] // pool), rest)
            given[i] = given[i] + addition
            rest = rest - addition
    return np.array(given)


def noise(rng, shape, deviation, bound, cuts=(), held_as=jnp.bfloat16):
    drawn = jax.random.normal(rng, shape, jnp.float32) * deviation
    if len(cuts) > 0:
        drawn = shard_levels(rng, shape, cuts, -0.22, 0.18) * drawn
    return jnp.clip(drawn, min=-bound, max=bound).astype(held_as)


def setup_inputs(seed: int = 0) -> dict:
    seeds = jax.random.split(jax.random.key(seed), 17)
    obs_features = noise(seeds[0], (OBS, E), 1.0, 6.0, ((0, 128),))
    obs_owner_keys = jax.random.split(jax.random.fold_in(seeds[1], 1), OBS // OBS_DEV)
    obs_owner_turns = jax.random.permutation(jax.random.fold_in(seeds[1], 3), OBS // OBS_DEV)
    obs_owner = jax.vmap(lambda own, number: shared_out(jax.random.fold_in(seeds[1], 2), own, number, OBS_DEV, GEO, 1, CAP, 1))(obs_owner_keys, obs_owner_turns).reshape((OBS, 1))
    obs_node = set_ends(jax.random.randint(seeds[2], (OBS,), 0, NODE_DEV), jax.random.fold_in(seeds[2], 1), 0, NODE_DEV - 1).astype(jnp.int32)
    obs_count = draw_obs_count(jax.random.fold_in(seeds[16], 71), 0)
    edge_senders = draw_edge_senders(jax.random.fold_in(seeds[16], 71), 0)
    obs_in_w = noise(seeds[5], (E, E), E ** -0.5, 0.375)
    obs_in_b = noise(seeds[6], (E,), 0.5, 3.0, (), jnp.float32)
    obs_out_w = noise(seeds[7], (E, E), E ** -0.5, 0.375)
    enc_w = noise(seeds[8], (E, L), E ** -0.5, 0.375, ((1, 2),))
    enc_b = noise(seeds[9], (L,), 0.5, 3.0, ((0, 2),), jnp.float32)
    node_base = noise(seeds[10], (NODES, L), 1.0, 6.0, ((0, 128), (1, 2)))
    recv_w = noise(seeds[11], (L, L), L ** -0.5, 0.1875, ((0, 2),))
    send_w = noise(seeds[12], (L, L), L ** -0.5, 0.1875, ((0, 2),))
    edge_b = noise(seeds[13], (L,), 0.5, 3.0, ((0, 2),), jnp.float32)
    channel_scale = draw_channel_scale(jax.random.fold_in(seeds[16], 71), 0)
    norm_gain = jnp.clip(1.0 + 0.18 * jax.random.normal(seeds[15], (L,), jnp.float32), 0.1, 1.9)
    return dict(obs_features=obs_features, obs_owner=obs_owner, obs_node=obs_node, obs_count=obs_count, edge_senders=edge_senders, obs_in_w=obs_in_w, obs_in_b=obs_in_b, obs_out_w=obs_out_w, enc_w=enc_w, enc_b=enc_b, node_base=node_base, recv_w=recv_w, send_w=send_w, edge_b=edge_b, channel_scale=channel_scale, norm_gain=norm_gain)


def global_senders(edge_senders):
    device = jnp.arange(GEO * EDGE_DEV, dtype=jnp.int32) // EDGE_DEV
    band_index = device // SECTORS
    sector_index = device % SECTORS
    own_node = device * NODE_DEV + edge_senders
    remain = jnp.maximum(edge_senders - NODE_DEV, 0)
    group = remain // HALO
    far_node = remain % HALO
    near_band = (band_index + group // 3 - 1) % BANDS
    near_sector = (sector_index + group % 3 - 1) % SECTORS
    remote = (near_band * SECTORS + near_sector) * NODE_DEV + far_node
    return jnp.where(edge_senders < NODE_DEV, own_node, remote).astype(jnp.int32)

def reference(obs_features, obs_owner, obs_node, obs_count, edge_senders, obs_in_w, obs_in_b, obs_out_w, enc_w, enc_b, node_base, recv_w, send_w, edge_b, channel_scale, norm_gain):
    node_total = GEO * NODE_DEV
    piece_rows = OBS_DEV // PIECES
    blocks = obs_features.reshape(GEO, OBS_DEV, E)
    owners = obs_owner[:, 0].reshape(GEO, OBS_DEV)
    node_ids = obs_node.reshape(GEO, OBS_DEV)

    def step(carry, item):
        total, count = carry
        block, owner, node_id, live_pieces = item
        hidden = jax.nn.silu(jnp.dot(block, obs_in_w, preferred_element_type=jnp.float32) + obs_in_b).astype(jnp.bfloat16)
        embedded = (block.astype(jnp.float32) + jnp.dot(hidden, obs_out_w, preferred_element_type=jnp.float32)).astype(jnp.bfloat16)
        message = jax.nn.silu(jnp.dot(embedded, enc_w, preferred_element_type=jnp.float32) + enc_b).astype(jnp.bfloat16)
        live = jnp.arange(OBS_DEV, dtype=jnp.int32) < live_pieces * piece_rows
        target = jnp.where(live, owner * NODE_DEV + node_id, node_total).astype(jnp.int32)
        total = total.at[target].add(message.astype(jnp.float32), mode='drop')
        count = count.at[target].add(jnp.ones((OBS_DEV,), jnp.float32), mode='drop')
        return ((total, count), None)
    start = (jnp.zeros((node_total, L), jnp.float32), jnp.zeros((node_total,), jnp.float32))
    (total, count), _ = lax.scan(step, start, (blocks, owners, node_ids, obs_count))
    latent = (node_base.astype(jnp.float32) + total / jnp.maximum(count, 1.0)[:, None]).astype(jnp.bfloat16)
    recv_proj = jnp.dot(latent, recv_w, preferred_element_type=jnp.float32).astype(jnp.bfloat16)
    send_proj = jnp.dot(latent, send_w, preferred_element_type=jnp.float32).astype(jnp.bfloat16)
    sources = global_senders(edge_senders).reshape(node_total, DEGREE)
    base = recv_proj.astype(jnp.float32) + edge_b
    agg = jnp.zeros((node_total, L), jnp.float32)
    for slot in range(DEGREE):
        agg = agg + jax.nn.silu(base + send_proj[sources[:, slot]].astype(jnp.float32))
    scaled = agg * channel_scale
    mean_square = lax.optimization_barrier(jnp.mean(scaled * scaled, axis=1))
    normed = scaled * lax.rsqrt(mean_square + 1e-05)[:, None] * norm_gain
    return (latent.astype(jnp.float32) + normed).astype(jnp.bfloat16)
```

```python
import functools

import jax
import jax.numpy as jnp
from jax import lax
from jax.experimental import pallas as pl
from jax.experimental.pallas import tpu as pltpu
from jax.sharding import PartitionSpec as P

PIECES = 8
DEGREE = 6
SLOTS = 16
ID_ROW = 12
GROUP = 8
LANES = 128
LOW = 64
PAD = 8
MESH = pl.DeviceIdType.MESH
F32 = jnp.float32
BF16 = jnp.bfloat16
STEP_ROWS = 256


def dot(a, b):
    return jnp.dot(a, b, preferred_element_type=F32)


def iota(shape, axis):
    return lax.broadcasted_iota(jnp.int32, shape, axis)


def half_silu(h):
    return h + h * jnp.tanh(h)


def kernel(
    bands,
    sectors,
    owner_ref,
    node_ref,
    count_ref,
    index_ref,
    obs_ref,
    in_w_ref,
    in_b_ref,
    out_w_ref,
    enc_w_ref,
    enc_b_ref,
    base_hbm,
    recv_hbm,
    send_hbm,
    edge_b_ref,
    scale_ref,
    gain_ref,
    out_hbm,
    send_buf,
    arrived,
    message,
    node_base,
    recv_w,
    send_w,
    picks,
    latent,
    table,
    recv_base,
    rim,
    halo,
    agg,
    part,
    part_in,
    out_buf,
    local_sem,
    weight_sem,
    weight_in_sem,
    send_sem,
    arrive_sem,
    pass_sem,
    pass_in_sem,
    latent_sem,
    latent_in_sem,
    halo_sem,
    halo_in_sem,
    part_sem,
    part_in_sem,
    out_sem,
):
    band = lax.axis_index("band")
    sector = lax.axis_index("sector")
    core = lax.axis_index("chan")
    other = 1 - core
    geo = bands * sectors
    pairs = geo // 2
    me = band * sectors + sector
    my_pair = me // 2
    parity = (me + core) % 2
    partner = (band, sector, other)
    rows = obs_ref.shape[0]
    node_rows, width = latent.shape[1:]
    tiles = width // LANES
    rim_rows = node_rows // 4
    groups = 2 * pairs // GROUP

    def device_of(block, core_of):
        return (block // sectors, block % sectors, core_of)

    def target_of(k):
        return 2 * ((my_pair + 1 + k) % pairs) + parity

    around = [(i, j) for i in (-1, 0, 1) for j in (-1, 0, 1) if (i, j) != (0, 0)]

    def neighbour(i, j):
        return ((band + i + bands) % bands, (sector + j + sectors) % sectors, core)

    local = [
        pltpu.make_async_copy(
            recv_hbm.at[:, pl.ds(pl.multiple_of(core * width, width), width)],
            recv_w.at[core],
            local_sem.at[0],
        ),
        pltpu.make_async_copy(
            send_hbm.at[:, pl.ds(pl.multiple_of(core * width, width), width)],
            send_w.at[core],
            local_sem.at[1],
        ),
        pltpu.make_async_copy(base_hbm, node_base, local_sem.at[2]),
    ]
    for copy in local:
        copy.start()

    barrier = pltpu.get_barrier_semaphore()

    def greet(k, carry):
        target = target_of(k)

        @pl.when(target != me)
        def _():
            pl.semaphore_signal(
                barrier, inc=1, device_id=device_of(target, core), device_id_type=MESH
            )

        return carry

    lax.fori_loop(0, pairs, greet, 0)
    for i, j in around:
        pl.semaphore_signal(barrier, inc=1, device_id=neighbour(i, j), device_id_type=MESH)
    pl.semaphore_signal(barrier, inc=1, device_id=partner, device_id_type=MESH)

    obs = obs_ref[...]
    hidden = half_silu(0.5 * (dot(obs, in_w_ref[...]) + in_b_ref[...])).astype(BF16)
    embedded = (obs.astype(F32) + dot(hidden, out_w_ref[...])).astype(BF16)
    owner = owner_ref[...]
    node = node_ref[...]
    live = iota((1, rows), 1) < count_ref[0] * (rows // PIECES)
    same = owner == iota((geo, rows), 0)
    upto = (iota((rows, rows), 0) <= iota((rows, rows), 1)).astype(F32).astype(BF16)
    ranks = dot(same.astype(F32).astype(BF16), upto)
    position = jnp.sum(jnp.where(same, ranks, 0.0), axis=0, keepdims=True).astype(jnp.int32) - 1
    pair = owner // 2
    valid = jnp.logical_and(live, owner % 2 == parity)
    step = (pair - my_pair - 1 + 2 * pairs) % pairs
    slot = jnp.where(valid, step * SLOTS + position, -1)
    lane = SLOTS * (step % GROUP) + position
    high = iota((2 * LANES, rows), 0) == lane
    low = iota((2 * LANES, rows), 0) == lane + LANES
    ids = jnp.where(
        high,
        (node // LOW + 1).astype(F32),
        jnp.where(low, (node % LOW).astype(F32), 0.0),
    ).astype(BF16)
    mine = (iota((pairs, rows), 0) == jnp.where(valid, step, -1)).astype(F32).astype(BF16)
    id_rows = lax.dot_general(
        mine, ids, (((1,), (1,)), ((), ())), preferred_element_type=F32
    ).astype(BF16)

    pl.semaphore_wait(barrier, pairs - 1 + core + len(around) + 1)

    weights = [
        pltpu.make_async_remote_copy(
            src_ref=source.at[:, pl.ds(pl.multiple_of(other * width, width), width)],
            dst_ref=target.at[core],
            send_sem=weight_sem.at[n],
            recv_sem=weight_in_sem.at[n],
            device_id=partner,
            device_id_type=MESH,
        )
        for n, (source, target) in enumerate(((send_hbm, send_w), (recv_hbm, recv_w)))
    ]

    def block_copy(k):
        return pltpu.make_async_remote_copy(
            src_ref=send_buf.at[k],
            dst_ref=arrived.at[core, k],
            send_sem=send_sem.at[k],
            recv_sem=arrive_sem.at[k],
            device_id=device_of(target_of(k), core),
            device_id_type=MESH,
        )

    def own_copy(k):
        return pltpu.make_async_copy(send_buf.at[k], arrived.at[core, k], local_sem.at[3])

    per_step = STEP_ROWS // SLOTS

    def pack(step_index, carry):
        first = pl.multiple_of(step_index * STEP_ROWS, STEP_ROWS)
        place = (slot == first + iota((STEP_ROWS, rows), 0)).astype(F32).astype(BF16)
        spread = (
            first + iota((STEP_ROWS, pairs), 0) == iota((STEP_ROWS, pairs), 1) * SLOTS + ID_ROW
        )
        block = dot(place, embedded) + dot(spread.astype(F32).astype(BF16), id_rows)
        send_buf[pl.ds(step_index * per_step, per_step)] = block.astype(BF16).reshape(
            per_step, SLOTS, -1
        )

        def send(n, inner):
            k = step_index * per_step + n

            @pl.when(target_of(k) != me)
            def _():
                block_copy(k).start()

            @pl.when(target_of(k) == me)
            def _():
                own_copy(k).start()

            return inner

        lax.fori_loop(0, per_step, send, 0)
        return carry

    lax.fori_loop(0, pairs // per_step, pack, 0)
    for copy in weights:
        copy.start()

    def pass_on(g, side):
        block = arrived.at[side, pl.ds(g * per_step, per_step)]
        return pltpu.make_async_remote_copy(
            src_ref=block,
            dst_ref=block,
            send_sem=pass_sem.at[g],
            recv_sem=pass_in_sem.at[g],
            device_id=partner,
            device_id_type=MESH,
        )

    def encode(side, g):
        block = arrived[side, pl.ds(g * per_step, per_step)].reshape(STEP_ROWS, -1)
        content = half_silu(0.5 * (dot(block, enc_w_ref[...]) + enc_b_ref[...])).astype(BF16)
        first = pl.multiple_of(side * (pairs * SLOTS) + g * STEP_ROWS, STEP_ROWS)
        message[pl.ds(first, STEP_ROWS), :] = content

    def receive(g, carry):
        def arrive(n, inner):
            k = g * per_step + n

            @pl.when(target_of(k) != me)
            def _():
                block_copy(k).wait_recv()

            @pl.when(target_of(k) == me)
            def _():
                own_copy(k).wait()

            return inner

        lax.fori_loop(0, per_step, arrive, 0)
        pass_on(g, core).start()
        encode(core, g)
        return carry

    lax.fori_loop(0, pairs // per_step, receive, 0)

    def receive_passed(g, carry):
        pass_on(g, other).wait_recv()
        encode(other, g)
        return carry

    lax.fori_loop(0, pairs // per_step, receive_passed, 0)

    slots = 2 * pairs * SLOTS
    at = iota((groups, slots), 1)
    chosen = jnp.logical_and(
        at // (GROUP * SLOTS) == iota((groups, slots), 0), at % SLOTS == ID_ROW
    )
    found = dot(chosen.astype(F32).astype(BF16), arrived[...].reshape(slots, -1))
    slot_ids = ((found[:, :LANES] - 1.0) * LOW + found[:, LANES:]).astype(jnp.int32)

    def rows_of(q):
        return pl.ds(pl.multiple_of(q * rim_rows, rim_rows), rim_rows)

    def latent_copy(q, side):
        block = latent.at[side, rows_of(q)]
        return pltpu.make_async_remote_copy(
            src_ref=block,
            dst_ref=block,
            send_sem=latent_sem.at[q],
            recv_sem=latent_in_sem.at[q],
            device_id=partner,
            device_id_type=MESH,
        )

    def make_latent(q):
        names = iota((rim_rows, LANES), 0) + q * rim_rows
        count = jnp.zeros((rim_rows, LANES), F32)
        for g in range(groups):
            hit = (names == slot_ids[g : g + 1, :]).astype(F32)
            count = count + hit
            picks[:, g * LANES : (g + 1) * LANES] = hit.astype(BF16)
        total = dot(picks[...], message[...])
        scale = 1.0 / jnp.maximum(jnp.sum(count, axis=1, keepdims=True), 1.0)
        latent[core, rows_of(q)] = (
            node_base[rows_of(q), :].astype(F32) + total * scale
        ).astype(BF16)
        latent_copy(q, core).start()

    def project(q, weight):
        return dot(latent[0, rows_of(q)], weight[0]) + dot(latent[1, rows_of(q)], weight[1])

    def project_send(q):
        value = 0.5 * project(q, send_w).astype(BF16).astype(F32)
        for t in range(tiles):
            table[pl.ds(PAD + q * (rim_rows * tiles) + t, rim_rows, stride=tiles), :] = value[
                :, t * LANES : (t + 1) * LANES
            ]

    def project_recv(q):
        value = 0.5 * (project(q, recv_w).astype(BF16).astype(F32) + edge_b_ref[...])
        for t in range(tiles):
            recv_base[pl.ds(q * (rim_rows * tiles) + t, rim_rows, stride=tiles), :] = value[
                :, t * LANES : (t + 1) * LANES
            ]

    local[2].wait()
    make_latent(0)
    local[1].wait()
    weights[0].wait_recv()
    latent_copy(0, other).wait_recv()
    project_send(0)
    rim[...] = table[pl.ds(PAD, rim_rows * tiles), :].astype(BF16)

    def halo_copy(n):
        i, j = around[n]
        return pltpu.make_async_remote_copy(
            src_ref=rim,
            dst_ref=halo.at[(1 - i) * 3 + 1 - j],
            send_sem=halo_sem.at[n],
            recv_sem=halo_in_sem.at[n],
            device_id=neighbour(i, j),
            device_id_type=MESH,
        )

    for n in range(len(around)):
        halo_copy(n).start()

    def later_latent(q, carry):
        make_latent(q)
        return carry

    lax.fori_loop(1, 4, later_latent, 0)
    local[0].wait()
    weights[1].wait_recv()
    project_recv(0)

    def later_project(q, carry):
        latent_copy(q, other).wait_recv()
        project_send(q)
        project_recv(q)
        return carry

    lax.fori_loop(1, 4, later_project, 0)

    for n, (i, j) in enumerate(around):
        halo_copy(n).wait_recv()
        group = (1 - i) * 3 + 1 - j
        first = PAD + (node_rows + group * rim_rows) * tiles
        table[pl.ds(first, rim_rows * tiles), :] = halo[group].astype(F32)

    upper = iota((2 * tiles, LANES), 0) < tiles

    def two_nodes(m):
        base = recv_base[pl.ds(pl.multiple_of(m * 2 * tiles, 2 * tiles), 2 * tiles), :]
        total = None
        for k in range(DEGREE):
            even = index_ref[2 * DEGREE * m + k]
            odd = index_ref[2 * DEGREE * m + DEGREE + k]
            sender = jnp.where(
                upper, table[pl.ds(even, 2 * tiles), :], table[pl.ds(odd, 2 * tiles), :]
            )
            term = half_silu(base + sender)
            total = term if total is None else total + term
        agg[pl.ds(pl.multiple_of(m * 2 * tiles, 2 * tiles), 2 * tiles), :] = total

    chunk = part.shape[1]
    chunks = node_rows // chunk
    unroll = 8

    def part_copy(n):
        return pltpu.make_async_remote_copy(
            src_ref=part.at[n],
            dst_ref=part_in.at[n],
            send_sem=part_sem.at[n],
            recv_sem=part_in_sem.at[n],
            device_id=partner,
            device_id_type=MESH,
        )

    def out_copy(n):
        span = pl.ds(pl.multiple_of(n * chunk, chunk), chunk)
        return pltpu.make_async_copy(out_buf.at[span], out_hbm.at[span], out_sem.at[n])

    def scaled(n, t):
        return (
            agg[pl.ds(n * (chunk * tiles) + t, chunk, stride=tiles), :]
            * scale_ref[:, t * LANES : (t + 1) * LANES]
        )

    def edges(n, carry):
        def some(m, inner):
            for u in range(unroll):
                two_nodes(n * (chunk // 2) + m * unroll + u)
            return inner

        lax.fori_loop(0, chunk // 2 // unroll, some, 0)
        square = jnp.zeros((chunk, LANES), F32)
        for t in range(tiles):
            value = scaled(n, t)
            square = square + value * value
        part[n] = square
        part_copy(n).start()
        return carry

    def finish(n, carry):
        part_copy(n).wait_recv()
        mean = jnp.sum(part[n] + part_in[n], axis=1, keepdims=True) / (2 * width)
        factor = lax.rsqrt(mean + 1e-05)
        span = pl.ds(pl.multiple_of(n * chunk, chunk), chunk)
        for t in range(tiles):
            lanes = slice(t * LANES, (t + 1) * LANES)
            normed = scaled(n, t) * factor * gain_ref[:, lanes]
            out_buf[span, lanes] = (latent[core, span, lanes].astype(F32) + normed).astype(BF16)
        out_copy(n).start()
        return carry

    def edges_and_finish(n, carry):
        edges(n, carry)
        return finish(n - 1, carry)

    edges(0, 0)
    lax.fori_loop(1, chunks, edges_and_finish, 0)
    finish(chunks - 1, 0)

    def drain_blocks(k, carry):
        @pl.when(target_of(k) != me)
        def _():
            block_copy(k).wait_send()

        return carry

    lax.fori_loop(0, pairs, drain_blocks, 0)

    def drain_passed(g, carry):
        pass_on(g, core).wait_send()
        return carry

    lax.fori_loop(0, pairs // per_step, drain_passed, 0)
    for copy in weights:
        copy.wait_send()
    for q in range(4):
        latent_copy(q, core).wait_send()
    for n in range(len(around)):
        halo_copy(n).wait_send()
    for n in range(chunks):
        part_copy(n).wait_send()
        out_copy(n).wait()


def local(
    obs_features,
    obs_owner,
    obs_node,
    obs_count,
    edge_senders,
    obs_in_w,
    obs_in_b,
    obs_out_w,
    enc_w,
    enc_b,
    node_base,
    recv_w,
    send_w,
    edge_b,
    channel_scale,
    norm_gain,
):
    bands = lax.axis_size("band")
    sectors = lax.axis_size("sector")
    geo = bands * sectors
    pairs = geo // 2
    rows, embed = obs_features.shape
    node_rows, width = node_base.shape
    tiles = width // LANES
    rim_rows = node_rows // 4
    chunk = node_rows // 5
    slots = geo * SLOTS
    place = jnp.arange(node_rows * DEGREE, dtype=jnp.int32) // DEGREE % 2
    index = edge_senders * tiles + PAD - tiles * place
    vmem = pl.BlockSpec(memory_space=pltpu.VMEM)
    smem = pl.BlockSpec(memory_space=pltpu.SMEM)
    hbm = pl.BlockSpec(memory_space=pl.ANY)
    dma = pltpu.SemaphoreType.DMA
    steps = pairs * SLOTS // STEP_ROWS
    return pl.pallas_call(
        functools.partial(kernel, bands, sectors),
        out_shape=jax.ShapeDtypeStruct((node_rows, width), BF16),
        in_specs=[vmem, vmem, smem, smem] + [vmem] * 6 + [hbm] * 3 + [vmem] * 3,
        out_specs=hbm,
        scratch_shapes=[
            pltpu.VMEM((pairs, SLOTS, embed), BF16),
            pltpu.VMEM((2, pairs, SLOTS, embed), BF16),
            pltpu.VMEM((slots, width), BF16),
            pltpu.VMEM((node_rows, width), BF16),
            pltpu.VMEM((2, width, width), BF16),
            pltpu.VMEM((2, width, width), BF16),
            pltpu.VMEM((rim_rows, slots), BF16),
            pltpu.VMEM((2, node_rows, width), BF16),
            pltpu.VMEM((2 * PAD + (node_rows + 9 * rim_rows) * tiles, LANES), F32),
            pltpu.VMEM((node_rows * tiles, LANES), F32),
            pltpu.VMEM((rim_rows * tiles, LANES), BF16),
            pltpu.VMEM((9, rim_rows * tiles, LANES), BF16),
            pltpu.VMEM((node_rows * tiles, LANES), F32),
            pltpu.VMEM((5, chunk, LANES), F32),
            pltpu.VMEM((5, chunk, LANES), F32),
            pltpu.VMEM((node_rows, width), BF16),
            dma((4,)),
            dma((2,)),
            dma((2,)),
            dma((pairs,)),
            dma((pairs,)),
            dma((steps,)),
            dma((steps,)),
            dma((4,)),
            dma((4,)),
            dma((8,)),
            dma((8,)),
            dma((5,)),
            dma((5,)),
            dma((5,)),
        ],
        compiler_params=pltpu.CompilerParams(
            collective_id=0, has_side_effects=True, vmem_limit_bytes=56 * 2**20
        ),
        name="encode_and_pass",
    )(
        obs_owner.reshape(1, rows),
        obs_node.reshape(1, rows),
        obs_count,
        index,
        obs_features,
        obs_in_w,
        obs_in_b.reshape(1, -1),
        obs_out_w,
        enc_w,
        enc_b.reshape(1, -1),
        node_base,
        recv_w,
        send_w,
        edge_b.reshape(1, -1),
        channel_scale.reshape(1, -1),
        norm_gain.reshape(1, -1),
    )


def solution(mesh):
    in_specs = (
        P(("band", "sector"), None),
        P(("band", "sector"), None),
        P(("band", "sector")),
        P(("band", "sector")),
        P(("band", "sector")),
        P(),
        P(),
        P(),
        P(None, "chan"),
        P("chan"),
        P(("band", "sector"), "chan"),
        P("chan", None),
        P("chan", None),
        P("chan"),
        P("chan"),
        P("chan"),
    )
    out_specs = P(("band", "sector"), "chan")
    return jax.shard_map(local, mesh=mesh, in_specs=in_specs, out_specs=out_specs, check_vma=False)
```

```python
import functools

import jax
import jax.numpy as jnp
from jax import lax
from jax.experimental import pallas as pl
from jax.experimental.pallas import tpu as pltpu
from jax.sharding import PartitionSpec as P

PIECES = 8
DEGREE = 6
SLOTS = 16
ID_ROW = 12
GROUP = 8
LANES = 128
LOW = 64
PAD = 8
MESH = pl.DeviceIdType.MESH
F32 = jnp.float32
BF16 = jnp.bfloat16
STEP_ROWS = 256


def dot(a, b):
    return jnp.dot(a, b, preferred_element_type=F32)


def iota(shape, axis):
    return lax.broadcasted_iota(jnp.int32, shape, axis)


def half_silu(h):
    return h + h * jnp.tanh(h)


def kernel(
    bands,
    sectors,
    owner_ref,
    node_ref,
    count_ref,
    index_ref,
    obs_ref,
    in_w_ref,
    in_b_ref,
    out_w_ref,
    enc_w_ref,
    enc_b_ref,
    base_hbm,
    recv_hbm,
    send_hbm,
    edge_b_ref,
    scale_ref,
    gain_ref,
    out_hbm,
    send_buf,
    arrived,
    message,
    node_base,
    recv_w,
    send_w,
    picks,
    latent,
    table,
    recv_base,
    rim,
    halo,
    agg,
    part,
    part_in,
    out_buf,
    local_sem,
    weight_sem,
    weight_in_sem,
    send_sem,
    arrive_sem,
    pass_sem,
    pass_in_sem,
    latent_sem,
    latent_in_sem,
    halo_sem,
    halo_in_sem,
    part_sem,
    part_in_sem,
    out_sem,
):
    band = lax.axis_index("band")
    sector = lax.axis_index("sector")
    core = lax.axis_index("chan")
    other = 1 - core
    geo = bands * sectors
    pairs = geo // 2
    me = band * sectors + sector
    my_pair = me // 2
    parity = (me + core) % 2
    partner = (band, sector, other)
    rows = obs_ref.shape[0]
    node_rows, width = latent.shape[1:]
    tiles = width // LANES
    rim_rows = node_rows // 4
    groups = 2 * pairs // GROUP

    def device_of(block, core_of):
        return (block // sectors, block % sectors, core_of)

    def target_of(k):
        return 2 * ((my_pair + 1 + k) % pairs) + parity

    around = [(i, j) for i in (-1, 0, 1) for j in (-1, 0, 1) if (i, j) != (0, 0)]

    def neighbour(i, j):
        return ((band + i + bands) % bands, (sector + j + sectors) % sectors, core)

    local = [
        pltpu.make_async_copy(
            recv_hbm.at[:, pl.ds(pl.multiple_of(core * width, width), width)],
            recv_w.at[core],
            local_sem.at[0],
        ),
        pltpu.make_async_copy(
            send_hbm.at[:, pl.ds(pl.multiple_of(core * width, width), width)],
            send_w.at[core],
            local_sem.at[1],
        ),
        pltpu.make_async_copy(base_hbm, node_base, local_sem.at[2]),
    ]
    for copy in local:
        copy.start()

    barrier = pltpu.get_barrier_semaphore()

    def greet(k, carry):
        target = target_of(k)

        @pl.when(target != me)
        def _():
            pl.semaphore_signal(
                barrier, inc=1, device_id=device_of(target, core), device_id_type=MESH
            )

        return carry

    lax.fori_loop(0, pairs, greet, 0)
    for i, j in around:
        pl.semaphore_signal(barrier, inc=1, device_id=neighbour(i, j), device_id_type=MESH)
    pl.semaphore_signal(barrier, inc=1, device_id=partner, device_id_type=MESH)

    obs = obs_ref[...]
    hidden = half_silu(0.5 * (dot(obs, in_w_ref[...]) + in_b_ref[...])).astype(BF16)
    embedded = (obs.astype(F32) + dot(hidden, out_w_ref[...])).astype(BF16)
    owner = owner_ref[...]
    node = node_ref[...]
    live = iota((1, rows), 1) < count_ref[0] * (rows // PIECES)
    same = owner == iota((geo, rows), 0)
    upto = (iota((rows, rows), 0) <= iota((rows, rows), 1)).astype(F32).astype(BF16)
    ranks = dot(same.astype(F32).astype(BF16), upto)
    position = jnp.sum(jnp.where(same, ranks, 0.0), axis=0, keepdims=True).astype(jnp.int32) - 1
    pair = owner // 2
    valid = jnp.logical_and(live, owner % 2 == parity)
    step = (pair - my_pair - 1 + 2 * pairs) % pairs
    slot = jnp.where(valid, step * SLOTS + position, -1)
    lane = SLOTS * (step % GROUP) + position
    high = iota((2 * LANES, rows), 0) == lane
    low = iota((2 * LANES, rows), 0) == lane + LANES
    ids = jnp.where(
        high,
        (node // LOW + 1).astype(F32),
        jnp.where(low, (node % LOW).astype(F32), 0.0),
    ).astype(BF16)
    mine = (iota((pairs, rows), 0) == jnp.where(valid, step, -1)).astype(F32).astype(BF16)
    id_rows = lax.dot_general(
        mine, ids, (((1,), (1,)), ((), ())), preferred_element_type=F32
    ).astype(BF16)

    pl.semaphore_wait(barrier, pairs - 1 + core + len(around) + 1)

    weights = [
        pltpu.make_async_remote_copy(
            src_ref=source.at[:, pl.ds(pl.multiple_of(other * width, width), width)],
            dst_ref=target.at[core],
            send_sem=weight_sem.at[n],
            recv_sem=weight_in_sem.at[n],
            device_id=partner,
            device_id_type=MESH,
        )
        for n, (source, target) in enumerate(((send_hbm, send_w), (recv_hbm, recv_w)))
    ]

    def block_copy(k):
        return pltpu.make_async_remote_copy(
            src_ref=send_buf.at[k],
            dst_ref=arrived.at[core, k],
            send_sem=send_sem.at[k],
            recv_sem=arrive_sem.at[k],
            device_id=device_of(target_of(k), core),
            device_id_type=MESH,
        )

    def own_copy(k):
        return pltpu.make_async_copy(send_buf.at[k], arrived.at[core, k], local_sem.at[3])

    per_step = STEP_ROWS // SLOTS

    def pack(step_index, carry):
        first = pl.multiple_of(step_index * STEP_ROWS, STEP_ROWS)
        place = (slot == first + iota((STEP_ROWS, rows), 0)).astype(F32).astype(BF16)
        spread = (
            first + iota((STEP_ROWS, pairs), 0) == iota((STEP_ROWS, pairs), 1) * SLOTS + ID_ROW
        )
        block = dot(place, embedded) + dot(spread.astype(F32).astype(BF16), id_rows)
        send_buf[pl.ds(step_index * per_step, per_step)] = block.astype(BF16).reshape(
            per_step, SLOTS, -1
        )

        def send(n, inner):
            k = step_index * per_step + n

            @pl.when(target_of(k) != me)
            def _():
                block_copy(k).start()

            @pl.when(target_of(k) == me)
            def _():
                own_copy(k).start()

            return inner

        lax.fori_loop(0, per_step, send, 0)
        return carry

    lax.fori_loop(0, pairs // per_step, pack, 0)
    for copy in weights:
        copy.start()

    def pass_on(g, side):
        block = arrived.at[side, pl.ds(g * per_step, per_step)]
        return pltpu.make_async_remote_copy(
            src_ref=block,
            dst_ref=block,
            send_sem=pass_sem.at[g],
            recv_sem=pass_in_sem.at[g],
            device_id=partner,
            device_id_type=MESH,
        )

    def encode(side, g):
        block = arrived[side, pl.ds(g * per_step, per_step)].reshape(STEP_ROWS, -1)
        content = half_silu(0.5 * (dot(block, enc_w_ref[...]) + enc_b_ref[...])).astype(BF16)
        first = pl.multiple_of(side * (pairs * SLOTS) + g * STEP_ROWS, STEP_ROWS)
        message[pl.ds(first, STEP_ROWS), :] = content

    def receive(g, carry):
        def arrive(n, inner):
            k = g * per_step + n

            @pl.when(target_of(k) != me)
            def _():
                block_copy(k).wait_recv()

            @pl.when(target_of(k) == me)
            def _():
                own_copy(k).wait()

            return inner

        lax.fori_loop(0, per_step, arrive, 0)
        pass_on(g, core).start()
        encode(core, g)
        return carry

    lax.fori_loop(0, pairs // per_step, receive, 0)

    def receive_passed(g, carry):
        pass_on(g, other).wait_recv()
        encode(other, g)
        return carry

    lax.fori_loop(0, pairs // per_step, receive_passed, 0)

    slots = 2 * pairs * SLOTS
    at = iota((groups, slots), 1)
    chosen = jnp.logical_and(
        at // (GROUP * SLOTS) == iota((groups, slots), 0), at % SLOTS == ID_ROW
    )
    found = dot(chosen.astype(F32).astype(BF16), arrived[...].reshape(slots, -1))
    slot_ids = ((found[:, :LANES] - 1.0) * LOW + found[:, LANES:]).astype(jnp.int32)

    def rows_of(q):
        return pl.ds(pl.multiple_of(q * rim_rows, rim_rows), rim_rows)

    def latent_copy(q, side):
        block = latent.at[side, rows_of(q)]
        return pltpu.make_async_remote_copy(
            src_ref=block,
            dst_ref=block,
            send_sem=latent_sem.at[q],
            recv_sem=latent_in_sem.at[q],
            device_id=partner,
            device_id_type=MESH,
        )

    def make_latent(q):
        names = iota((rim_rows, LANES), 0) + q * rim_rows
        count = jnp.zeros((rim_rows, LANES), F32)
        for g in range(groups):
            hit = (names == slot_ids[g : g + 1, :]).astype(F32)
            count = count + hit
            picks[:, g * LANES : (g + 1) * LANES] = hit.astype(BF16)
        total = dot(picks[...], message[...])
        scale = 1.0 / jnp.maximum(jnp.sum(count, axis=1, keepdims=True), 1.0)
        latent[core, rows_of(q)] = (
            node_base[rows_of(q), :].astype(F32) + total * scale
        ).astype(BF16)
        latent_copy(q, core).start()

    def project(q, weight):
        return dot(latent[0, rows_of(q)], weight[0]) + dot(latent[1, rows_of(q)], weight[1])

    def project_send(q):
        value = 0.5 * project(q, send_w).astype(BF16).astype(F32)
        for t in range(tiles):
            table[pl.ds(PAD + q * (rim_rows * tiles) + t, rim_rows, stride=tiles), :] = value[
                :, t * LANES : (t + 1) * LANES
            ]

    def project_recv(q):
        value = 0.5 * (project(q, recv_w).astype(BF16).astype(F32) + edge_b_ref[...])
        for t in range(tiles):
            recv_base[pl.ds(q * (rim_rows * tiles) + t, rim_rows, stride=tiles), :] = value[
                :, t * LANES : (t + 1) * LANES
            ]

    local[2].wait()
    make_latent(0)
    local[1].wait()
    weights[0].wait_recv()
    latent_copy(0, other).wait_recv()
    project_send(0)
    rim[...] = table[pl.ds(PAD, rim_rows * tiles), :].astype(BF16)

    half_rows = rim_rows * tiles // 2
    sides = [(0, 1), (0, -1), (1, 0), (-1, 0)]
    turns = [(d, e) for d in sides for e in sides if (d[0] == 0) != (e[0] == 0)]

    def group_of(i, j):
        return (1 - i) * 3 + 1 - j

    def half_of(n):
        return pl.ds(n * half_rows, half_rows)

    def halo_copy(half, d):
        n = half * 4 + sides.index(d)
        return pltpu.make_async_remote_copy(
            src_ref=rim.at[half_of(half)],
            dst_ref=halo.at[group_of(*d), half_of(half)],
            send_sem=halo_sem.at[n],
            recv_sem=halo_in_sem.at[n],
            device_id=neighbour(*d),
            device_id_type=MESH,
        )

    def corner_copy(d, e):
        half = 0 if d[0] == 0 else 1
        n = 8 + turns.index((d, e))
        return pltpu.make_async_remote_copy(
            src_ref=halo.at[group_of(*d), half_of(half)],
            dst_ref=halo.at[group_of(d[0] + e[0], d[1] + e[1]), half_of(half)],
            send_sem=halo_sem.at[n],
            recv_sem=halo_in_sem.at[n],
            device_id=neighbour(*e),
            device_id_type=MESH,
        )

    def widen(group, half):
        first = PAD + (node_rows + group * rim_rows) * tiles + half * half_rows
        table[pl.ds(first, half_rows), :] = halo[group, half_of(half)].astype(F32)

    for first in (True, False):
        for d in sides:
            halo_copy(0 if (d[0] == 0) == first else 1, d).start()

    make_latent(1)
    for d in sides:
        half = 0 if d[0] == 0 else 1
        halo_copy(half, d).wait_recv()
        for e in sides:
            if (d, e) in turns:
                corner_copy(d, e).start()

    def later_latent(q, carry):
        make_latent(q)
        return carry

    lax.fori_loop(2, 4, later_latent, 0)
    local[0].wait()
    weights[1].wait_recv()
    project_recv(0)

    def later_project(q, carry):
        latent_copy(q, other).wait_recv()
        project_send(q)
        project_recv(q)
        return carry

    lax.fori_loop(1, 4, later_project, 0)

    for d in sides:
        half = 0 if d[0] == 0 else 1
        widen(group_of(*d), half)
        halo_copy(1 - half, d).wait_recv()
        widen(group_of(*d), 1 - half)
    for d, e in turns:
        corner_copy(d, e).wait_recv()
        widen(group_of(d[0] + e[0], d[1] + e[1]), 0 if d[0] == 0 else 1)

    upper = iota((2 * tiles, LANES), 0) < tiles

    def two_nodes(m):
        base = recv_base[pl.ds(pl.multiple_of(m * 2 * tiles, 2 * tiles), 2 * tiles), :]
        total = None
        for k in range(DEGREE):
            even = index_ref[2 * DEGREE * m + k]
            odd = index_ref[2 * DEGREE * m + DEGREE + k]
            sender = jnp.where(
                upper, table[pl.ds(even, 2 * tiles), :], table[pl.ds(odd, 2 * tiles), :]
            )
            term = half_silu(base + sender)
            total = term if total is None else total + term
        agg[pl.ds(pl.multiple_of(m * 2 * tiles, 2 * tiles), 2 * tiles), :] = total

    chunk = part.shape[1]
    chunks = node_rows // chunk
    unroll = 8

    def part_copy(n):
        return pltpu.make_async_remote_copy(
            src_ref=part.at[n],
            dst_ref=part_in.at[n],
            send_sem=part_sem.at[n],
            recv_sem=part_in_sem.at[n],
            device_id=partner,
            device_id_type=MESH,
        )

    def out_copy(n):
        span = pl.ds(pl.multiple_of(n * chunk, chunk), chunk)
        return pltpu.make_async_copy(out_buf.at[span], out_hbm.at[span], out_sem.at[n])

    def scaled(n, t):
        return (
            agg[pl.ds(n * (chunk * tiles) + t, chunk, stride=tiles), :]
            * scale_ref[:, t * LANES : (t + 1) * LANES]
        )

    def edges(n, carry):
        def some(m, inner):
            for u in range(unroll):
                two_nodes(n * (chunk // 2) + m * unroll + u)
            return inner

        lax.fori_loop(0, chunk // 2 // unroll, some, 0)
        square = jnp.zeros((chunk, LANES), F32)
        for t in range(tiles):
            value = scaled(n, t)
            square = square + value * value
        part[n] = square
        part_copy(n).start()
        return carry

    def finish(n, carry):
        part_copy(n).wait_recv()
        mean = jnp.sum(part[n] + part_in[n], axis=1, keepdims=True) / (2 * width)
        factor = lax.rsqrt(mean + 1e-05)
        span = pl.ds(pl.multiple_of(n * chunk, chunk), chunk)
        for t in range(tiles):
            lanes = slice(t * LANES, (t + 1) * LANES)
            normed = scaled(n, t) * factor * gain_ref[:, lanes]
            out_buf[span, lanes] = (latent[core, span, lanes].astype(F32) + normed).astype(BF16)
        out_copy(n).start()
        return carry

    def edges_and_finish(n, carry):
        edges(n, carry)
        return finish(n - 1, carry)

    edges(0, 0)
    lax.fori_loop(1, chunks, edges_and_finish, 0)
    finish(chunks - 1, 0)

    def drain_blocks(k, carry):
        @pl.when(target_of(k) != me)
        def _():
            block_copy(k).wait_send()

        return carry

    lax.fori_loop(0, pairs, drain_blocks, 0)

    def drain_passed(g, carry):
        pass_on(g, core).wait_send()
        return carry

    lax.fori_loop(0, pairs // per_step, drain_passed, 0)
    for copy in weights:
        copy.wait_send()
    for q in range(4):
        latent_copy(q, core).wait_send()
    for d in sides:
        halo_copy(0, d).wait_send()
        halo_copy(1, d).wait_send()
    for d, e in turns:
        corner_copy(d, e).wait_send()
    for n in range(chunks):
        part_copy(n).wait_send()
        out_copy(n).wait()


def local(
    obs_features,
    obs_owner,
    obs_node,
    obs_count,
    edge_senders,
    obs_in_w,
    obs_in_b,
    obs_out_w,
    enc_w,
    enc_b,
    node_base,
    recv_w,
    send_w,
    edge_b,
    channel_scale,
    norm_gain,
):
    bands = lax.axis_size("band")
    sectors = lax.axis_size("sector")
    geo = bands * sectors
    pairs = geo // 2
    rows, embed = obs_features.shape
    node_rows, width = node_base.shape
    tiles = width // LANES
    rim_rows = node_rows // 4
    chunk = node_rows // 5
    slots = geo * SLOTS
    place = jnp.arange(node_rows * DEGREE, dtype=jnp.int32) // DEGREE % 2
    index = edge_senders * tiles + PAD - tiles * place
    vmem = pl.BlockSpec(memory_space=pltpu.VMEM)
    smem = pl.BlockSpec(memory_space=pltpu.SMEM)
    hbm = pl.BlockSpec(memory_space=pl.ANY)
    dma = pltpu.SemaphoreType.DMA
    steps = pairs * SLOTS // STEP_ROWS
    return pl.pallas_call(
        functools.partial(kernel, bands, sectors),
        out_shape=jax.ShapeDtypeStruct((node_rows, width), BF16),
        in_specs=[vmem, vmem, smem, smem] + [vmem] * 6 + [hbm] * 3 + [vmem] * 3,
        out_specs=hbm,
        scratch_shapes=[
            pltpu.VMEM((pairs, SLOTS, embed), BF16),
            pltpu.VMEM((2, pairs, SLOTS, embed), BF16),
            pltpu.VMEM((slots, width), BF16),
            pltpu.VMEM((node_rows, width), BF16),
            pltpu.VMEM((2, width, width), BF16),
            pltpu.VMEM((2, width, width), BF16),
            pltpu.VMEM((rim_rows, slots), BF16),
            pltpu.VMEM((2, node_rows, width), BF16),
            pltpu.VMEM((2 * PAD + (node_rows + 9 * rim_rows) * tiles, LANES), F32),
            pltpu.VMEM((node_rows * tiles, LANES), F32),
            pltpu.VMEM((rim_rows * tiles, LANES), BF16),
            pltpu.VMEM((9, rim_rows * tiles, LANES), BF16),
            pltpu.VMEM((node_rows * tiles, LANES), F32),
            pltpu.VMEM((5, chunk, LANES), F32),
            pltpu.VMEM((5, chunk, LANES), F32),
            pltpu.VMEM((node_rows, width), BF16),
            dma((4,)),
            dma((2,)),
            dma((2,)),
            dma((pairs,)),
            dma((pairs,)),
            dma((steps,)),
            dma((steps,)),
            dma((4,)),
            dma((4,)),
            dma((16,)),
            dma((16,)),
            dma((5,)),
            dma((5,)),
            dma((5,)),
        ],
        compiler_params=pltpu.CompilerParams(
            collective_id=0, has_side_effects=True, vmem_limit_bytes=56 * 2**20
        ),
        name="encode_and_pass",
    )(
        obs_owner.reshape(1, rows),
        obs_node.reshape(1, rows),
        obs_count,
        index,
        obs_features,
        obs_in_w,
        obs_in_b.reshape(1, -1),
        obs_out_w,
        enc_w,
        enc_b.reshape(1, -1),
        node_base,
        recv_w,
        send_w,
        edge_b.reshape(1, -1),
        channel_scale.reshape(1, -1),
        norm_gain.reshape(1, -1),
    )


def solution(mesh):
    in_specs = (
        P(("band", "sector"), None),
        P(("band", "sector"), None),
        P(("band", "sector")),
        P(("band", "sector")),
        P(("band", "sector")),
        P(),
        P(),
        P(),
        P(None, "chan"),
        P("chan"),
        P(("band", "sector"), "chan"),
        P("chan", None),
        P("chan", None),
        P("chan"),
        P("chan"),
        P("chan"),
    )
    out_specs = P(("band", "sector"), "chan")
    return jax.shard_map(local, mesh=mesh, in_specs=in_specs, out_specs=out_specs, check_vma=False)
```

```python
import functools

import jax
import jax.numpy as jnp
from jax import lax
from jax.experimental import pallas as pl
from jax.experimental.pallas import tpu as pltpu
from jax.sharding import PartitionSpec as P

PIECES = 8
DEGREE = 6
SLOTS = 16
ID_ROW = 12
GROUP = 8
LANES = 128
LOW = 64
SKEW = 4
PARTS = 4
STEPS = 4
MESH = pl.DeviceIdType.MESH
F32 = jnp.float32
BF16 = jnp.bfloat16


def dot(a, b):
    return jnp.dot(a, b, preferred_element_type=F32)


def iota(shape, axis):
    return lax.broadcasted_iota(jnp.int32, shape, axis)


def half_silu(h):
    return h + h * jnp.tanh(h)


def kernel(
    bands,
    sectors,
    owner_ref,
    node_ref,
    count_ref,
    sender_ref,
    in_b_ref,
    enc_b_ref,
    edge_b_ref,
    scale_ref,
    gain_ref,
    obs_hbm,
    in_w_hbm,
    out_w_hbm,
    enc_w_hbm,
    base_hbm,
    recv_hbm,
    send_hbm,
    out_hbm,
    obs_ref,
    in_w_ref,
    out_w_ref,
    enc_w_ref,
    vectors,
    send_buf,
    arrived,
    message,
    node_base,
    recv_w,
    send_w,
    picks,
    latent,
    latent_in,
    table,
    recv_base,
    sent,
    sent_in,
    halo,
    agg,
    out_buf,
    local_sem,
    weight_sem,
    weight_in_sem,
    send_sem,
    arrive_sem,
    pass_sem,
    pass_in_sem,
    latent_sem,
    latent_in_sem,
    sent_sem,
    sent_in_sem,
    halo_sem,
    halo_in_sem,
    share_sem,
    share_in_sem,
    out_sem,
    out_send_sem,
    out_in_sem,
):
    band = lax.axis_index("band")
    sector = lax.axis_index("sector")
    core = lax.axis_index("chan")
    other = 1 - core
    geo = bands * sectors
    columns = sectors // 2
    pairs = bands * columns
    partner = (band, sector, other)
    rows = obs_ref.shape[0]
    node_rows, width = node_base.shape
    tiles = 2 * width // LANES
    run = node_rows // PARTS
    mine_rows = run // 2
    piece = mine_rows // 2
    table_rows = table.shape[0] // tiles
    base_rows = recv_base.shape[0] // tiles
    groups = geo // GROUP
    per_step = pairs // STEPS

    def local_copy(n, source, target):
        return pltpu.make_async_copy(source, target, local_sem.at[n])

    first_copies = [
        local_copy(0, obs_hbm, obs_ref),
        local_copy(1, in_w_hbm, in_w_ref),
        local_copy(2, out_w_hbm, out_w_ref),
    ]
    enc_copy = local_copy(3, enc_w_hbm, enc_w_ref)
    base_copy = local_copy(4, base_hbm, node_base)
    send_w_copy = local_copy(5, send_hbm, send_w.at[core])
    recv_w_copy = local_copy(6, recv_hbm, recv_w.at[core])
    for copy in first_copies + [enc_copy, base_copy, send_w_copy, recv_w_copy]:
        copy.start()

    sides = [(0, 1), (0, -1), (1, 0), (-1, 0)]

    def neighbour(i, j):
        return (
            lax.rem(band + (i + bands), bands),
            lax.rem(sector + (j + sectors), sectors),
            core,
        )

    to_sector = [lax.rem(sector + (2 * n + core), sectors) for n in range(columns)]
    barrier = pltpu.get_barrier_semaphore()

    def greet(device):
        pl.semaphore_signal(barrier, inc=1, device_id=device, device_id_type=MESH)

    greet(partner)
    for d in sides:
        greet(neighbour(*d))
    for i in range(bands):
        to_band = lax.rem(band + i, bands)
        for n in range(columns):
            if i == 0 and n == 0:

                @pl.when(core == 1)
                def _():
                    greet((to_band, to_sector[0], core))

            else:
                greet((to_band, to_sector[n], core))

    for copy in first_copies:
        copy.wait()
    obs = obs_ref[...]
    hidden = half_silu(0.5 * (dot(obs, in_w_ref[...]) + in_b_ref[...])).astype(BF16)
    embedded = (obs.astype(F32) + dot(hidden, out_w_ref[...])).astype(BF16)
    owner = owner_ref[...]
    node = node_ref[...]
    live = iota((1, rows), 1) < count_ref[0] * (rows // PIECES)
    same = (owner == iota((geo, rows), 0)).astype(F32)
    span = rows // 4
    upto = (iota((span, span), 0) <= iota((span, span), 1)).astype(F32).astype(BF16)
    before = jnp.zeros((geo, 1), F32)
    ranks = []
    for n in range(4):
        some = same[:, n * span : (n + 1) * span]
        rank = dot(some.astype(BF16), upto) + before
        before = rank[:, span - 1 :]
        ranks.append(jnp.sum(rank * some, axis=0, keepdims=True))
    position = jnp.concatenate(ranks, axis=1).astype(jnp.int32) - 1
    further = (owner % sectors - sector + sectors) % sectors
    valid = jnp.logical_and(live, further % 2 == core)
    step = (owner // sectors - band + bands) % bands * columns + further // 2
    slot = jnp.where(valid, step * SLOTS + position, -1)
    lane = SLOTS * (step % GROUP) + position
    high = iota((2 * LANES, rows), 0) == lane
    low = iota((2 * LANES, rows), 0) == lane + LANES
    ids = jnp.where(
        high,
        (node // LOW + 1).astype(F32),
        jnp.where(low, (node % LOW).astype(F32), 0.0),
    ).astype(BF16)
    mine = (iota((pairs, rows), 0) == jnp.where(valid, step, -1)).astype(F32).astype(BF16)
    id_rows = lax.dot_general(
        mine, ids, (((1,), (1,)), ((), ())), preferred_element_type=F32
    ).astype(BF16)

    def block_copy(i, n):
        k = i * columns + n
        return pltpu.make_async_remote_copy(
            src_ref=send_buf.at[k],
            dst_ref=arrived.at[core, k],
            send_sem=send_sem.at[k // per_step],
            recv_sem=arrive_sem.at[k // per_step],
            device_id=(lax.rem(band + i, bands), to_sector[n], core),
            device_id_type=MESH,
        )

    def pack(g):
        first = g * per_step * SLOTS
        count = per_step * SLOTS
        place = (slot == first + iota((count, rows), 0)).astype(F32).astype(BF16)
        spread = first + iota((count, pairs), 0) == iota((count, pairs), 1) * SLOTS + ID_ROW
        block = dot(place, embedded) + dot(spread.astype(F32).astype(BF16), id_rows)
        send_buf[pl.ds(g * per_step, per_step)] = block.astype(BF16).reshape(per_step, SLOTS, -1)

    def send(g):
        for k in range(g * per_step, (g + 1) * per_step):
            i, n = k // columns, k % columns
            if k == 0:

                @pl.when(core == 1)
                def _():
                    block_copy(0, 0).start()

                @pl.when(core == 0)
                def _():
                    pltpu.make_async_copy(
                        send_buf.at[0], arrived.at[core, 0], arrive_sem.at[0]
                    ).start()

            else:
                block_copy(i, n).start()

    pack(0)
    pl.semaphore_wait(barrier, pairs - 1 + core + len(sides) + 1)
    send(0)
    for g in range(1, STEPS):
        pack(g)
        send(g)

    def weight_copy(n, source, target):
        return pltpu.make_async_remote_copy(
            src_ref=source,
            dst_ref=target,
            send_sem=weight_sem.at[n],
            recv_sem=weight_in_sem.at[n],
            device_id=partner,
            device_id_type=MESH,
        )

    weights = [
        weight_copy(0, send_hbm, send_w.at[core]),
        weight_copy(1, recv_hbm, recv_w.at[core]),
    ] + [
        weight_copy(2 + n, ref, vectors.at[n, core])
        for n, ref in enumerate((edge_b_ref, scale_ref, gain_ref))
    ]
    for copy in weights:
        copy.start()
    for n, ref in enumerate((edge_b_ref, scale_ref, gain_ref)):
        vectors[n, core] = ref[...]

    def blocks_of(g):
        return pl.ds(g * per_step, per_step)

    def pass_on(g, side):
        block = arrived.at[side, blocks_of(g)]
        return pltpu.make_async_remote_copy(
            src_ref=block,
            dst_ref=block,
            send_sem=pass_sem.at[g],
            recv_sem=pass_in_sem.at[g],
            device_id=partner,
            device_id_type=MESH,
        )

    def group_wait(g, first=0):
        span = pl.ds(g * per_step + first, per_step - first)
        return pltpu.make_async_remote_copy(
            src_ref=send_buf.at[span],
            dst_ref=arrived.at[core, span],
            send_sem=send_sem.at[g],
            recv_sem=arrive_sem.at[g],
            device_id=partner,
            device_id_type=MESH,
        )

    def encode(side, g):
        block = arrived[side, blocks_of(g)].reshape(per_step * SLOTS, -1)
        content = half_silu(0.5 * (dot(block, enc_w_ref[...]) + enc_b_ref[...])).astype(BF16)
        first = pl.multiple_of((side * pairs + g * per_step) * SLOTS, per_step * SLOTS)
        message[pl.ds(first, per_step * SLOTS), :] = content

    enc_copy.wait()
    for g in range(STEPS):
        group_wait(g).wait_recv()
        pass_on(g, core).start()
        encode(core, g)
    for g in range(STEPS):
        pass_on(g, other).wait_recv()
        encode(other, g)

    slots = geo * SLOTS
    at = iota((groups, slots), 1)
    chosen = jnp.logical_and(
        at // (GROUP * SLOTS) == iota((groups, slots), 0), at % SLOTS == ID_ROW
    )
    found = dot(chosen.astype(F32).astype(BF16), arrived[...].reshape(slots, -1))
    slot_ids = ((found[:, :LANES] - 1.0) * LOW + found[:, LANES:]).astype(jnp.int32)

    def latent_copy(q):
        return pltpu.make_async_remote_copy(
            src_ref=latent.at[q, other],
            dst_ref=latent_in.at[q],
            send_sem=latent_sem.at[q],
            recv_sem=latent_in_sem.at[q],
            device_id=partner,
            device_id_type=MESH,
        )

    def make_latent(q):
        names = iota((run, LANES), 0) + q * run
        count = jnp.zeros((run, LANES), F32)
        for g in range(groups):
            hit = (names == slot_ids[g : g + 1, :]).astype(F32)
            count = count + hit
            picks[:, g * LANES : (g + 1) * LANES] = hit.astype(BF16)
        total = dot(picks[...], message[...])
        scale = 1.0 / jnp.maximum(jnp.sum(count, axis=1, keepdims=True), 1.0)
        base = node_base[pl.ds(pl.multiple_of(q * run, run), run), :].astype(F32)
        latent[q] = (base + total * scale).astype(BF16).reshape(2, mine_rows, width)
        latent_copy(q).start()

    def project(q, weight):
        return dot(latent[q, core], weight[core]) + dot(latent_in[q], weight[other])

    def tile(t):
        return slice(t * LANES, (t + 1) * LANES)

    def sent_copy(q):
        return pltpu.make_async_remote_copy(
            src_ref=sent.at[q],
            dst_ref=sent_in.at[q],
            send_sem=sent_sem.at[q],
            recv_sem=sent_in_sem.at[q],
            device_id=partner,
            device_id_type=MESH,
        )

    def project_send(q):
        value = (0.5 * project(q, send_w)).astype(BF16)
        wide = value.astype(F32)
        for t in range(tiles):
            for h in range(2):
                sent[q, h, t] = value[h * piece : (h + 1) * piece, tile(t)]
            table[pl.ds(t * table_rows + q * run + core * mine_rows, mine_rows), :] = wide[
                :, tile(t)
            ]
        sent_copy(q).start()

    def project_recv(q):
        value = project(q, recv_w).astype(BF16).astype(F32)
        for t in range(tiles):
            bias = vectors[0, t // (tiles // 2), :, tile(t % (tiles // 2))]
            recv_base[pl.ds(t * base_rows + q * mine_rows, mine_rows), :] = 0.5 * (
                value[:, tile(t)] + bias
            )

    def widen(first, source):
        for t in range(tiles):
            table[pl.ds(t * table_rows + first, piece), :] = source[t].astype(F32)

    base_copy.wait()
    make_latent(0)
    send_w_copy.wait()
    weights[0].wait_recv()
    latent_copy(0).wait_recv()
    project_send(0)

    turns = [(d, e) for d in sides for e in sides if (d[0] == 0) != (e[0] == 0)]

    def group_of(i, j):
        return (1 - i) * 3 + 1 - j

    def halo_copy(half, d):
        n = half * 4 + sides.index(d)
        return pltpu.make_async_remote_copy(
            src_ref=sent.at[0, half],
            dst_ref=halo.at[group_of(*d), core, half],
            send_sem=halo_sem.at[n],
            recv_sem=halo_in_sem.at[n],
            device_id=neighbour(*d),
            device_id_type=MESH,
        )

    def corner_copy(d, e):
        half = 0 if d[0] == 0 else 1
        n = 8 + turns.index((d, e))
        return pltpu.make_async_remote_copy(
            src_ref=halo.at[group_of(*d), core, half],
            dst_ref=halo.at[group_of(d[0] + e[0], d[1] + e[1]), core, half],
            send_sem=halo_sem.at[n],
            recv_sem=halo_in_sem.at[n],
            device_id=neighbour(*e),
            device_id_type=MESH,
        )

    def share(group, half, side):
        block = halo.at[group, side, half]
        return pltpu.make_async_remote_copy(
            src_ref=block,
            dst_ref=block,
            send_sem=share_sem.at[group * 2 + half],
            recv_sem=share_in_sem.at[group * 2 + half],
            device_id=partner,
            device_id_type=MESH,
        )

    def widen_halo(group, half, side):
        widen(
            node_rows + group * run + half * piece + side * mine_rows,
            halo.at[group, side, half],
        )

    for first in (True, False):
        for d in sides:
            halo_copy(0 if (d[0] == 0) == first else 1, d).start()

    make_latent(1)
    for d in sides:
        half = 0 if d[0] == 0 else 1
        halo_copy(half, d).wait_recv()
        for e in sides:
            if (d, e) in turns:
                corner_copy(d, e).start()
        share(group_of(*d), half, core).start()

    def later_latent(q, carry):
        make_latent(q)
        return carry

    lax.fori_loop(2, PARTS, later_latent, 0)
    recv_w_copy.wait()
    for copy in weights[1:]:
        copy.wait_recv()
    project_recv(0)

    def later_project(q, carry):
        latent_copy(q).wait_recv()
        project_send(q)
        project_recv(q)
        return carry

    lax.fori_loop(1, PARTS, later_project, 0)

    def widen_sent(q, carry):
        sent_copy(q).wait_recv()
        for h in range(2):
            widen(q * run + h * piece + other * mine_rows, sent_in.at[q, h])
        return carry

    lax.fori_loop(0, PARTS, widen_sent, 0)

    straight = [(d, 0 if d[0] == 0 else 1) for d in sides]
    for d, half in straight:
        halo_copy(1 - half, d).wait_recv()
        share(group_of(*d), 1 - half, core).start()
        widen_halo(group_of(*d), half, core)
        widen_halo(group_of(*d), 1 - half, core)
    for d, half in straight:
        for h in (half, 1 - half):
            share(group_of(*d), h, other).wait_recv()
            widen_halo(group_of(*d), h, other)
    corners = [(group_of(d[0] + e[0], d[1] + e[1]), 0 if d[0] == 0 else 1) for d, e in turns]
    for n, (d, e) in enumerate(turns):
        corner_copy(d, e).wait_recv()
        share(*corners[n], core).start()
        widen_halo(*corners[n], core)
    for group, half in corners:
        share(group, half, other).wait_recv()
        widen_halo(group, half, other)

    unroll = 16

    def one_node(q, r):
        place = q * mine_rows + r
        base = recv_base[pl.ds(place, tiles, stride=base_rows), :]
        first = (q * run + core * mine_rows + r) * DEGREE
        total = None
        for k in range(DEGREE):
            sender = table[pl.ds(sender_ref[first + k], tiles, stride=table_rows), :]
            term = half_silu(base + sender)
            total = term if total is None else total + term
        agg[pl.ds(place, tiles, stride=base_rows), :] = total

    def out_rows(q):
        return out_hbm.at[pl.ds(pl.multiple_of(q * run + core * mine_rows, mine_rows), mine_rows)]

    def out_keep(q):
        return pltpu.make_async_copy(out_buf.at[q, core], out_rows(q), out_sem.at[q])

    def out_send(q):
        return pltpu.make_async_remote_copy(
            src_ref=out_buf.at[q, other],
            dst_ref=out_rows(q),
            send_sem=out_send_sem.at[q],
            recv_sem=out_in_sem.at[q],
            device_id=partner,
            device_id_type=MESH,
        )

    def edges(q, carry):
        def some(m, inner):
            for u in range(unroll):
                one_node(q, m * unroll + u)
            return inner

        lax.fori_loop(0, mine_rows // unroll, some, 0)

        def scaled(t):
            bias = vectors[1, t // (tiles // 2), :, tile(t % (tiles // 2))]
            return agg[pl.ds(t * base_rows + q * mine_rows, mine_rows), :] * bias

        square = jnp.zeros((mine_rows, LANES), F32)
        for t in range(tiles):
            value = scaled(t)
            square = square + value * value
        mean = jnp.sum(square, axis=1, keepdims=True) / (2 * width)
        factor = lax.rsqrt(mean + 1e-05)

        def finish(side, held):
            for t in range(tiles // 2):
                gain = vectors[2, side, :, tile(t)]
                normed = scaled(side * (tiles // 2) + t) * factor * gain
                out_buf[q, side, :, tile(t)] = (held[:, tile(t)].astype(F32) + normed).astype(
                    BF16
                )

        for side in range(2):

            @pl.when(core == side)
            def _():
                finish(side, latent[q, side])
                finish(1 - side, latent_in[q])

        out_send(q).start()
        out_keep(q).start()
        return carry

    lax.fori_loop(0, PARTS, edges, 0)

    @pl.when(core == 0)
    def _():
        group_wait(0, 1).wait_send()

    @pl.when(core == 1)
    def _():
        group_wait(0).wait_send()

    for g in range(1, STEPS):
        group_wait(g).wait_send()
    for g in range(STEPS):
        pass_on(g, core).wait_send()
    for copy in weights:
        copy.wait_send()
    for q in range(PARTS):
        latent_copy(q).wait_send()
        sent_copy(q).wait_send()
    for d in sides:
        halo_copy(0, d).wait_send()
        halo_copy(1, d).wait_send()
        for half in range(2):
            share(group_of(*d), half, core).wait_send()
    for n, (d, e) in enumerate(turns):
        corner_copy(d, e).wait_send()
        share(*corners[n], core).wait_send()
    for q in range(PARTS):
        out_keep(q).wait()
        out_send(q).wait()


def local(
    obs_features,
    obs_owner,
    obs_node,
    obs_count,
    edge_senders,
    obs_in_w,
    obs_in_b,
    obs_out_w,
    enc_w,
    enc_b,
    node_base,
    recv_w,
    send_w,
    edge_b,
    channel_scale,
    norm_gain,
):
    bands = lax.axis_size("band")
    sectors = lax.axis_size("sector")
    geo = bands * sectors
    pairs = geo // 2
    rows, embed = obs_features.shape
    node_rows, width = node_base.shape
    tiles = 2 * width // LANES
    run = node_rows // PARTS
    mine_rows = run // 2
    piece = mine_rows // 2
    slots = geo * SLOTS
    vmem = pl.BlockSpec(memory_space=pltpu.VMEM)
    smem = pl.BlockSpec(memory_space=pltpu.SMEM)
    hbm = pl.BlockSpec(memory_space=pl.ANY)
    dma = pltpu.SemaphoreType.DMA
    return pl.pallas_call(
        functools.partial(kernel, bands, sectors),
        out_shape=jax.ShapeDtypeStruct((node_rows, width), BF16),
        in_specs=[vmem, vmem, smem, smem] + [vmem] * 5 + [hbm] * 7,
        out_specs=hbm,
        scratch_shapes=[
            pltpu.VMEM((rows, embed), BF16),
            pltpu.VMEM((embed, embed), BF16),
            pltpu.VMEM((embed, embed), BF16),
            pltpu.VMEM((embed, width), BF16),
            pltpu.VMEM((3, 2, 1, width), F32),
            pltpu.VMEM((pairs, SLOTS, embed), BF16),
            pltpu.VMEM((2, pairs, SLOTS, embed), BF16),
            pltpu.VMEM((slots, width), BF16),
            pltpu.VMEM((node_rows, width), BF16),
            pltpu.VMEM((2, width, 2 * width), BF16),
            pltpu.VMEM((2, width, 2 * width), BF16),
            pltpu.VMEM((run, slots), BF16),
            pltpu.VMEM((PARTS, 2, mine_rows, width), BF16),
            pltpu.VMEM((PARTS, mine_rows, width), BF16),
            pltpu.VMEM((tiles * (node_rows + 9 * run + SKEW), LANES), F32),
            pltpu.VMEM((tiles * (PARTS * mine_rows + SKEW), LANES), F32),
            pltpu.VMEM((PARTS, 2, tiles, piece, LANES), BF16),
            pltpu.VMEM((PARTS, 2, tiles, piece, LANES), BF16),
            pltpu.VMEM((9, 2, 2, tiles, piece, LANES), BF16),
            pltpu.VMEM((tiles * (PARTS * mine_rows + SKEW), LANES), F32),
            pltpu.VMEM((PARTS, 2, mine_rows, width), BF16),
            dma((7,)),
            dma((5,)),
            dma((5,)),
            dma((STEPS,)),
            dma((STEPS,)),
            dma((STEPS,)),
            dma((STEPS,)),
            dma((PARTS,)),
            dma((PARTS,)),
            dma((PARTS,)),
            dma((PARTS,)),
            dma((16,)),
            dma((16,)),
            dma((18,)),
            dma((18,)),
            dma((PARTS,)),
            dma((PARTS,)),
            dma((PARTS,)),
        ],
        compiler_params=pltpu.CompilerParams(
            collective_id=0, has_side_effects=True, vmem_limit_bytes=58 * 2**20
        ),
        name="encode_and_pass",
    )(
        obs_owner.reshape(1, rows),
        obs_node.reshape(1, rows),
        obs_count,
        edge_senders,
        obs_in_b.reshape(1, -1),
        enc_b.reshape(1, -1),
        edge_b.reshape(1, -1),
        channel_scale.reshape(1, -1),
        norm_gain.reshape(1, -1),
        obs_features,
        obs_in_w,
        obs_out_w,
        enc_w,
        node_base,
        recv_w,
        send_w,
    )


def solution(mesh):
    in_specs = (
        P(("band", "sector"), None),
        P(("band", "sector"), None),
        P(("band", "sector")),
        P(("band", "sector")),
        P(("band", "sector")),
        P(),
        P(),
        P(),
        P(None, "chan"),
        P("chan"),
        P(("band", "sector"), "chan"),
        P("chan", None),
        P("chan", None),
        P("chan"),
        P("chan"),
        P("chan"),
    )
    out_specs = P(("band", "sector"), "chan")
    return jax.shard_map(local, mesh=mesh, in_specs=in_specs, out_specs=out_specs, check_vma=False)
```

```python
import functools

import jax
import jax.numpy as jnp
from jax import lax
from jax.experimental import pallas as pl
from jax.experimental.pallas import tpu as pltpu
from jax.sharding import PartitionSpec as P

PIECES = 8
DEGREE = 6
SLOTS = 16
ID_ROW = 12
GROUP = 8
LANES = 128
LOW = 64
SKEW = 4
PARTS = 4
STEPS = 4
SIDE = 4
ORDER = (2, 1, 3, 0)
MESH = pl.DeviceIdType.MESH
F32 = jnp.float32
BF16 = jnp.bfloat16


def dot(a, b):
    return jnp.dot(a, b, preferred_element_type=F32)


def iota(shape, axis):
    return lax.broadcasted_iota(jnp.int32, shape, axis)


def half_silu(h):
    return h + h * jnp.tanh(h)


def kernel(
    bands,
    sectors,
    owner_ref,
    node_ref,
    count_ref,
    sender_ref,
    in_b_ref,
    enc_b_ref,
    edge_b_ref,
    scale_ref,
    gain_ref,
    obs_hbm,
    in_w_hbm,
    out_w_hbm,
    enc_w_hbm,
    base_hbm,
    recv_hbm,
    send_hbm,
    out_ref,
    obs_ref,
    in_w_ref,
    out_w_ref,
    enc_w_ref,
    vectors,
    slot_ids,
    rim_sum,
    rim_count,
    send_buf,
    arrived,
    message,
    node_base,
    recv_w,
    send_w,
    picks,
    latent,
    latent_in,
    table,
    recv_base,
    sent,
    sent_in,
    halo,
    agg,
    out_buf,
    local_sem,
    weight_sem,
    weight_in_sem,
    send_sem,
    arrive_sem,
    pass_sem,
    pass_in_sem,
    latent_sem,
    latent_in_sem,
    sent_sem,
    sent_in_sem,
    halo_sem,
    halo_in_sem,
    share_sem,
    share_in_sem,
    out_send_sem,
    out_in_sem,
):
    band = lax.axis_index("band")
    sector = lax.axis_index("sector")
    core = lax.axis_index("chan")
    other = 1 - core
    geo = bands * sectors
    pairs = geo // 2
    partner = (band, sector, other)
    rows = obs_ref.shape[0]
    node_rows, width = node_base.shape
    tiles = 2 * width // LANES
    run = node_rows // PARTS
    mine_rows = run // 2
    piece = mine_rows // 2
    table_rows = table.shape[0] // tiles
    base_rows = recv_base.shape[0] // tiles
    groups = geo // GROUP
    per_step = pairs // STEPS

    sides = [(0, 1), (1, 0), (0, -1), (-1, 0)]

    def neighbour(i, j):
        return (
            lax.rem(band + (i + bands), bands),
            lax.rem(sector + (j + sectors), sectors),
            core,
        )

    row, column = lax.div(band, SIDE), lax.rem(band, SIDE)
    to_row = [lax.rem(row + n, SIDE) * SIDE for n in range(SIDE)]
    to_column = [lax.rem(column + n, SIDE) for n in range(SIDE)]
    to_sector = [lax.rem(sector + (2 * n + core), sectors) for n in range(SIDE)]

    def target_of(k):
        n, i, j = ORDER[k // SIDE**2], ORDER[k // SIDE % SIDE], ORDER[k % SIDE]
        return to_row[i] + to_column[j], to_sector[n], core

    barrier = pltpu.get_barrier_semaphore()

    def greet(device):
        pl.semaphore_signal(barrier, inc=1, device_id=device, device_id_type=MESH)

    for k in range(pairs - 1):
        greet(target_of(k))

    @pl.when(core == 1)
    def _():
        greet(target_of(pairs - 1))

    greet(partner)
    for d in sides:
        greet(neighbour(*d))

    def local_copy(n, source, target):
        return pltpu.make_async_copy(source, target, local_sem.at[n])

    first_copies = [
        local_copy(0, obs_hbm, obs_ref),
        local_copy(1, in_w_hbm, in_w_ref),
        local_copy(2, out_w_hbm, out_w_ref),
    ]
    enc_copy = local_copy(3, enc_w_hbm, enc_w_ref)
    base_copy = local_copy(4, base_hbm, node_base)
    send_w_copy = local_copy(5, send_hbm, send_w.at[core])
    recv_w_copy = local_copy(6, recv_hbm, recv_w.at[core])
    for copy in first_copies + [enc_copy, base_copy, send_w_copy, recv_w_copy]:
        copy.start()

    for copy in first_copies:
        copy.wait()
    obs = obs_ref[...]
    hidden = half_silu(0.5 * (dot(obs, in_w_ref[...]) + in_b_ref[...])).astype(BF16)
    embedded = (obs.astype(F32) + dot(hidden, out_w_ref[...])).astype(BF16)
    owner = owner_ref[...]
    node = node_ref[...]
    live = iota((1, rows), 1) < count_ref[0] * (rows // PIECES)
    same = (owner == iota((geo, rows), 0)).astype(F32)
    span = rows // 4
    upto = (iota((span, span), 0) <= iota((span, span), 1)).astype(F32).astype(BF16)
    before = jnp.zeros((geo, 1), F32)
    ranks = []
    for n in range(4):
        some = same[:, n * span : (n + 1) * span]
        rank = dot(some.astype(BF16), upto) + before
        before = rank[:, span - 1 :]
        ranks.append(jnp.sum(rank * some, axis=0, keepdims=True))
    position = jnp.concatenate(ranks, axis=1).astype(jnp.int32) - 1
    further = (owner % sectors - sector + sectors) % sectors
    valid = jnp.logical_and(live, further % 2 == core)
    owner_band = owner // sectors

    def place_of(distance):
        return jnp.where(
            distance == 2, 0, jnp.where(distance == 1, 1, jnp.where(distance == 3, 2, 3))
        )

    step = (
        place_of(further // 2) * SIDE**2
        + place_of((owner_band // SIDE - row + SIDE) % SIDE) * SIDE
        + place_of((owner_band % SIDE - column + SIDE) % SIDE)
    )
    slot = jnp.where(valid, step * SLOTS + position, -1)
    lane = SLOTS * (step % GROUP) + position
    high = iota((2 * LANES, rows), 0) == lane
    low = iota((2 * LANES, rows), 0) == lane + LANES
    ids = jnp.where(
        high,
        (node // LOW + 1).astype(F32),
        jnp.where(low, (node % LOW).astype(F32), 0.0),
    ).astype(BF16)
    mine = (iota((pairs, rows), 0) == jnp.where(valid, step, -1)).astype(F32).astype(BF16)
    id_rows = lax.dot_general(
        mine, ids, (((1,), (1,)), ((), ())), preferred_element_type=F32
    ).astype(BF16)

    def block_copy(k):
        return pltpu.make_async_remote_copy(
            src_ref=send_buf.at[k],
            dst_ref=arrived.at[core, k],
            send_sem=send_sem.at[k // per_step],
            recv_sem=arrive_sem.at[k // per_step],
            device_id=target_of(k),
            device_id_type=MESH,
        )

    def pack(g):
        first = g * per_step * SLOTS
        count = per_step * SLOTS
        place = (slot == first + iota((count, rows), 0)).astype(F32).astype(BF16)
        spread = first + iota((count, pairs), 0) == iota((count, pairs), 1) * SLOTS + ID_ROW
        block = dot(place, embedded) + dot(spread.astype(F32).astype(BF16), id_rows)
        send_buf[pl.ds(g * per_step, per_step)] = block.astype(BF16).reshape(per_step, SLOTS, -1)

    def send(g):
        for k in range(g * per_step, (g + 1) * per_step):
            if k < pairs - 1:
                block_copy(k).start()
                continue

            @pl.when(core == 1)
            def _():
                block_copy(k).start()

            @pl.when(core == 0)
            def _():
                pltpu.make_async_copy(
                    send_buf.at[k], arrived.at[core, k], arrive_sem.at[k // per_step]
                ).start()

    pack(0)
    pl.semaphore_wait(barrier, pairs - 1 + core + len(sides) + 1)
    send(0)
    for g in range(1, STEPS):
        pack(g)
        send(g)

    def weight_copy(n, source, target):
        return pltpu.make_async_remote_copy(
            src_ref=source,
            dst_ref=target,
            send_sem=weight_sem.at[n],
            recv_sem=weight_in_sem.at[n],
            device_id=partner,
            device_id_type=MESH,
        )

    weights = [
        weight_copy(0, send_hbm, send_w.at[core]),
        weight_copy(1, recv_hbm, recv_w.at[core]),
    ] + [
        weight_copy(2 + n, ref, vectors.at[n, core])
        for n, ref in enumerate((edge_b_ref, scale_ref, gain_ref))
    ]
    for copy in weights:
        copy.start()
    for n, ref in enumerate((edge_b_ref, scale_ref, gain_ref)):
        vectors[n, core] = ref[...]

    def blocks_of(g):
        return pl.ds(g * per_step, per_step)

    def pass_on(g, side):
        block = arrived.at[side, blocks_of(g)]
        return pltpu.make_async_remote_copy(
            src_ref=block,
            dst_ref=block,
            send_sem=pass_sem.at[g],
            recv_sem=pass_in_sem.at[g],
            device_id=partner,
            device_id_type=MESH,
        )

    def group_wait(g, less=0):
        span = pl.ds(g * per_step, per_step - less)
        return pltpu.make_async_remote_copy(
            src_ref=send_buf.at[span],
            dst_ref=arrived.at[core, span],
            send_sem=send_sem.at[g],
            recv_sem=arrive_sem.at[g],
            device_id=partner,
            device_id_type=MESH,
        )

    count = per_step * SLOTS
    id_groups = per_step // GROUP
    at = iota((8, count), 1)
    chosen = jnp.logical_and(at // (GROUP * SLOTS) == iota((8, count), 0), at % SLOTS == ID_ROW)
    chosen = chosen.astype(F32).astype(BF16)

    def hits(q, names):
        return (iota((run, LANES), 0) + q * run == names).astype(F32)

    def take(side, g):
        block = arrived[side, blocks_of(g)].reshape(count, -1)
        content = half_silu(0.5 * (dot(block, enc_w_ref[...]) + enc_b_ref[...])).astype(BF16)
        start = pl.multiple_of((side * pairs + g * per_step) * SLOTS, count)
        message[pl.ds(start, count), :] = content
        found = dot(chosen, block)
        names = ((found[:, :LANES] - 1.0) * LOW + found[:, LANES:]).astype(jnp.int32)
        slot_ids[side * STEPS + g] = names
        some = [hits(0, names[n : n + 1, :]) for n in range(id_groups)]
        value = dot(jnp.concatenate(some, axis=1).astype(BF16), content)
        return value, sum(some[1:], some[0])

    enc_copy.wait()
    for g in range(STEPS + 1):
        if g < STEPS:
            group_wait(g).wait_recv()
            pass_on(g, core).start()
        if g > 0:
            pass_on(g - 1, other).wait_recv()
        taken = []
        if g < STEPS:
            taken.append(take(core, g))
        if g > 0:
            taken.append(take(other, g - 1))
            taken.append((rim_sum[...], rim_count[...]))
        value, number = taken[0]
        for more in taken[1:]:
            value, number = value + more[0], number + more[1]
        rim_sum[...] = value
        rim_count[...] = number

    def latent_copy(q):
        return pltpu.make_async_remote_copy(
            src_ref=latent.at[q, other],
            dst_ref=latent_in.at[q],
            send_sem=latent_sem.at[q],
            recv_sem=latent_in_sem.at[q],
            device_id=partner,
            device_id_type=MESH,
        )

    def end_latent(q, total, number):
        scale = 1.0 / jnp.maximum(jnp.sum(number, axis=1, keepdims=True), 1.0)
        base = node_base[pl.ds(pl.multiple_of(q * run, run), run), :].astype(F32)
        latent[q] = (base + total * scale).astype(BF16).reshape(2, mine_rows, width)
        latent_copy(q).start()

    def make_latent(q):
        number = jnp.zeros((run, LANES), F32)
        for g in range(groups):
            n = g % id_groups
            hit = hits(q, slot_ids[g // id_groups, n : n + 1, :])
            number = number + hit
            picks[:, g * LANES : (g + 1) * LANES] = hit.astype(BF16)
        end_latent(q, dot(picks[...], message[...]), number)

    def project(q, weight, arrival=None):
        own = dot(latent[q, core], weight[core])
        if arrival is not None:
            arrival()
        return own + dot(latent_in[q], weight[other])

    def tile(t):
        return slice(t * LANES, (t + 1) * LANES)

    def sent_copy(q):
        return pltpu.make_async_remote_copy(
            src_ref=sent.at[q],
            dst_ref=sent_in.at[q],
            send_sem=sent_sem.at[q],
            recv_sem=sent_in_sem.at[q],
            device_id=partner,
            device_id_type=MESH,
        )

    def project_send(q, arrival=None):
        value = (0.5 * project(q, send_w, arrival)).astype(BF16)
        wide = value.astype(F32)
        for t in range(tiles):
            for h in range(2):
                sent[q, h, t] = value[h * piece : (h + 1) * piece, tile(t)]
            table[pl.ds(t * table_rows + q * run + core * mine_rows, mine_rows), :] = wide[
                :, tile(t)
            ]
        sent_copy(q).start()

    def project_recv(q):
        value = project(q, recv_w).astype(BF16).astype(F32)
        for t in range(tiles):
            bias = vectors[0, t // (tiles // 2), :, tile(t % (tiles // 2))]
            recv_base[pl.ds(t * base_rows + q * mine_rows, mine_rows), :] = 0.5 * (
                value[:, tile(t)] + bias
            )

    def widen(first, source):
        for t in range(tiles):
            table[pl.ds(t * table_rows + first, piece), :] = source[t].astype(F32)

    def first_arrival():
        weights[0].wait_recv()
        latent_copy(0).wait_recv()

    base_copy.wait()
    end_latent(0, rim_sum[...], rim_count[...])
    send_w_copy.wait()
    project_send(0, first_arrival)

    turns = [(d, e) for d in sides for e in sides if (d[0] == 0) != (e[0] == 0)]

    def group_of(i, j):
        return (1 - i) * 3 + 1 - j

    def halo_copy(half, d):
        n = half * 4 + sides.index(d)
        return pltpu.make_async_remote_copy(
            src_ref=sent.at[0, half],
            dst_ref=halo.at[group_of(*d), core, half],
            send_sem=halo_sem.at[n],
            recv_sem=halo_in_sem.at[n],
            device_id=neighbour(*d),
            device_id_type=MESH,
        )

    def corner_copy(d, e):
        half = 0 if d[0] == 0 else 1
        n = 8 + turns.index((d, e))
        return pltpu.make_async_remote_copy(
            src_ref=halo.at[group_of(*d), core, half],
            dst_ref=halo.at[group_of(d[0] + e[0], d[1] + e[1]), core, half],
            send_sem=halo_sem.at[n],
            recv_sem=halo_in_sem.at[n],
            device_id=neighbour(*e),
            device_id_type=MESH,
        )

    def share(group, half, side):
        block = halo.at[group, side, half]
        return pltpu.make_async_remote_copy(
            src_ref=block,
            dst_ref=block,
            send_sem=share_sem.at[group * 2 + half],
            recv_sem=share_in_sem.at[group * 2 + half],
            device_id=partner,
            device_id_type=MESH,
        )

    def widen_halo(group, half, side):
        widen(
            node_rows + group * run + half * piece + side * mine_rows,
            halo.at[group, side, half],
        )

    early = {d: 0 if d[0] == 0 else 1 for d in sides}
    first_turns, second_turns = turns[: len(sides)], turns[len(sides) :]

    def corner_of(d, e):
        return group_of(d[0] + e[0], d[1] + e[1]), early[d]

    def comes(d):
        return {1: band > 0, 0: None, -1: band < bands - 1}[d[0]]

    def goes(d):
        return comes((-d[0], 0))

    def when(condition, act):
        if condition is None:
            act()
        else:
            pl.when(condition)(act)

    def comes_corner(d, e):
        return comes((d[0] + e[0], 0))

    def goes_corner(d, e):
        return comes(d) if d[0] else goes(e)

    for d in sides:
        when(goes(d), lambda: halo_copy(early[d], d).start())

    make_latent(1)
    for d in sides:

        def second_half():
            halo_copy(early[d], d).wait_send()
            halo_copy(1 - early[d], d).start()

        when(goes(d), second_half)
    for d in sides:
        when(comes(d), lambda: halo_copy(early[d], d).wait_recv())
        for t in first_turns:
            if t[0] == d:
                when(goes_corner(*t), lambda: corner_copy(*t).start())
    for d in sides:
        when(comes(d), lambda: share(group_of(*d), early[d], core).start())

    def later_latent(q, carry):
        make_latent(q)
        return carry

    lax.fori_loop(2, PARTS, later_latent, 0)
    recv_w_copy.wait()
    for copy in weights[1:]:
        copy.wait_recv()
    project_recv(0)

    def later_project(q, carry):
        latent_copy(q).wait_recv()
        project_send(q)
        project_recv(q)
        return carry

    lax.fori_loop(1, PARTS, later_project, 0)
    for e in sides:
        for t in first_turns:
            if t[1] == e:
                when(goes_corner(*t), lambda: corner_copy(*t).wait_send())
        for t in second_turns:
            if t[1] == e:
                when(goes_corner(*t), lambda: corner_copy(*t).start())

    def widen_sent(q, carry):
        sent_copy(q).wait_recv()
        for h in range(2):
            widen(q * run + h * piece + other * mine_rows, sent_in.at[q, h])
        return carry

    lax.fori_loop(0, PARTS, widen_sent, 0)

    def widen_both(group, half):
        widen_halo(group, half, core)
        share(group, half, other).wait_recv()
        widen_halo(group, half, other)

    for d in sides:
        when(comes(d), lambda: widen_both(group_of(*d), early[d]))

    @pl.when(core == 0)
    def _():
        group_wait(STEPS - 1, 1).wait_send()

    @pl.when(core == 1)
    def _():
        group_wait(STEPS - 1).wait_send()

    for g in range(STEPS - 1):
        group_wait(g).wait_send()
    for g in range(STEPS):
        pass_on(g, core).wait_send()
    for copy in weights:
        copy.wait_send()
    for q in range(PARTS):
        latent_copy(q).wait_send()
        sent_copy(q).wait_send()

    for d in sides:

        def second_arrival():
            halo_copy(1 - early[d], d).wait_recv()
            share(group_of(*d), 1 - early[d], core).start()

        when(comes(d), second_arrival)

    def corner_arrival(t):
        corner_copy(*t).wait_recv()
        share(*corner_of(*t), core).start()

    for t in first_turns:
        when(comes_corner(*t), lambda: corner_arrival(t))
    for d in sides:
        when(comes(d), lambda: widen_both(group_of(*d), 1 - early[d]))
    for t in first_turns:
        when(comes_corner(*t), lambda: widen_both(*corner_of(*t)))
    for t in second_turns:
        when(comes_corner(*t), lambda: corner_arrival(t))
    for t in second_turns:
        when(comes_corner(*t), lambda: widen_both(*corner_of(*t)))

    unroll = 16

    def one_node(q, r):
        place = q * mine_rows + r
        base = recv_base[pl.ds(place, tiles, stride=base_rows), :]
        first = (q * run + core * mine_rows + r) * DEGREE
        total = None
        for k in range(DEGREE):
            sender = table[pl.ds(sender_ref[first + k], tiles, stride=table_rows), :]
            term = half_silu(base + sender)
            total = term if total is None else total + term
        agg[pl.ds(place, tiles, stride=base_rows), :] = total

    def out_rows(q):
        return pl.ds(pl.multiple_of(q * run + core * mine_rows, mine_rows), mine_rows)

    def out_send(q):
        return pltpu.make_async_remote_copy(
            src_ref=out_buf.at[q],
            dst_ref=out_ref.at[out_rows(q)],
            send_sem=out_send_sem.at[q],
            recv_sem=out_in_sem.at[q],
            device_id=partner,
            device_id_type=MESH,
        )

    def edges(q, carry):
        def some(m, inner):
            for u in range(unroll):
                one_node(q, m * unroll + u)
            return inner

        lax.fori_loop(0, mine_rows // unroll, some, 0)

        def scaled(t):
            bias = vectors[1, t // (tiles // 2), :, tile(t % (tiles // 2))]
            return agg[pl.ds(t * base_rows + q * mine_rows, mine_rows), :] * bias

        square = jnp.zeros((mine_rows, LANES), F32)
        for t in range(tiles):
            value = scaled(t)
            square = square + value * value
        mean = jnp.sum(square, axis=1, keepdims=True) / (2 * width)
        factor = lax.rsqrt(mean + 1e-05)

        def finish(side, held, target):
            for t in range(tiles // 2):
                gain = vectors[2, side, :, tile(t)]
                normed = scaled(side * (tiles // 2) + t) * factor * gain
                target[:, tile(t)] = (held[:, tile(t)].astype(F32) + normed).astype(BF16)

        for side in range(2):

            @pl.when(core == side)
            def _():
                finish(1 - side, latent_in[q], out_buf.at[q])
                finish(side, latent[q, side], out_ref.at[out_rows(q)])

        out_send(q).start()
        return carry

    lax.fori_loop(0, PARTS, edges, 0)

    def drain_side(d):
        for half in range(2):
            share(group_of(*d), half, core).wait_send()

    for d in sides:
        when(goes(d), lambda: halo_copy(1 - early[d], d).wait_send())
        when(comes(d), lambda: drain_side(d))
    for t in second_turns:
        when(goes_corner(*t), lambda: corner_copy(*t).wait_send())
    for t in turns:
        when(comes_corner(*t), lambda: share(*corner_of(*t), core).wait_send())
    for q in range(PARTS):
        out_send(q).wait()


def local(
    obs_features,
    obs_owner,
    obs_node,
    obs_count,
    edge_senders,
    obs_in_w,
    obs_in_b,
    obs_out_w,
    enc_w,
    enc_b,
    node_base,
    recv_w,
    send_w,
    edge_b,
    channel_scale,
    norm_gain,
):
    bands = lax.axis_size("band")
    sectors = lax.axis_size("sector")
    geo = bands * sectors
    pairs = geo // 2
    rows, embed = obs_features.shape
    node_rows, width = node_base.shape
    tiles = 2 * width // LANES
    run = node_rows // PARTS
    mine_rows = run // 2
    piece = mine_rows // 2
    slots = geo * SLOTS
    vmem = pl.BlockSpec(memory_space=pltpu.VMEM)
    smem = pl.BlockSpec(memory_space=pltpu.SMEM)
    hbm = pl.BlockSpec(memory_space=pl.ANY)
    dma = pltpu.SemaphoreType.DMA
    return pl.pallas_call(
        functools.partial(kernel, bands, sectors),
        out_shape=pltpu.VMEM((node_rows, width), BF16),
        in_specs=[vmem, vmem, smem, smem] + [vmem] * 5 + [hbm] * 7,
        out_specs=vmem,
        scratch_shapes=[
            pltpu.VMEM((rows, embed), BF16),
            pltpu.VMEM((embed, embed), BF16),
            pltpu.VMEM((embed, embed), BF16),
            pltpu.VMEM((embed, width), BF16),
            pltpu.VMEM((3, 2, 1, width), F32),
            pltpu.VMEM((2 * STEPS, 8, LANES), jnp.int32),
            pltpu.VMEM((run, width), F32),
            pltpu.VMEM((run, LANES), F32),
            pltpu.VMEM((pairs, SLOTS, embed), BF16),
            pltpu.VMEM((2, pairs, SLOTS, embed), BF16),
            pltpu.VMEM((slots, width), BF16),
            pltpu.VMEM((node_rows, width), BF16),
            pltpu.VMEM((2, width, 2 * width), BF16),
            pltpu.VMEM((2, width, 2 * width), BF16),
            pltpu.VMEM((run, slots), BF16),
            pltpu.VMEM((PARTS, 2, mine_rows, width), BF16),
            pltpu.VMEM((PARTS, mine_rows, width), BF16),
            pltpu.VMEM((tiles * (node_rows + 9 * run + SKEW), LANES), F32),
            pltpu.VMEM((tiles * (PARTS * mine_rows + SKEW), LANES), F32),
            pltpu.VMEM((PARTS, 2, tiles, piece, LANES), BF16),
            pltpu.VMEM((PARTS, 2, tiles, piece, LANES), BF16),
            pltpu.VMEM((9, 2, 2, tiles, piece, LANES), BF16),
            pltpu.VMEM((tiles * (PARTS * mine_rows + SKEW), LANES), F32),
            pltpu.VMEM((PARTS, mine_rows, width), BF16),
            dma((7,)),
            dma((5,)),
            dma((5,)),
            dma((STEPS,)),
            dma((STEPS,)),
            dma((STEPS,)),
            dma((STEPS,)),
            dma((PARTS,)),
            dma((PARTS,)),
            dma((PARTS,)),
            dma((PARTS,)),
            dma((16,)),
            dma((16,)),
            dma((18,)),
            dma((18,)),
            dma((PARTS,)),
            dma((PARTS,)),
        ],
        compiler_params=pltpu.CompilerParams(
            collective_id=0, has_side_effects=True, vmem_limit_bytes=56 * 2**20
        ),
        name="encode_and_pass",
    )(
        obs_owner.reshape(1, rows),
        obs_node.reshape(1, rows),
        obs_count,
        edge_senders,
        obs_in_b.reshape(1, -1),
        enc_b.reshape(1, -1),
        edge_b.reshape(1, -1),
        channel_scale.reshape(1, -1),
        norm_gain.reshape(1, -1),
        obs_features,
        obs_in_w,
        obs_out_w,
        enc_w,
        node_base,
        recv_w,
        send_w,
    )


def solution(mesh):
    in_specs = (
        P(("band", "sector"), None),
        P(("band", "sector"), None),
        P(("band", "sector")),
        P(("band", "sector")),
        P(("band", "sector")),
        P(),
        P(),
        P(),
        P(None, "chan"),
        P("chan"),
        P(("band", "sector"), "chan"),
        P("chan", None),
        P("chan", None),
        P("chan"),
        P("chan"),
        P("chan"),
    )
    out_specs = P(("band", "sector"), "chan")
    return jax.shard_map(local, mesh=mesh, in_specs=in_specs, out_specs=out_specs, check_vma=False)
```

```python
import functools

import jax
import jax.numpy as jnp
from jax import lax
from jax.experimental import pallas as pl
from jax.experimental.pallas import tpu as pltpu
from jax.sharding import PartitionSpec as P

PIECES = 8
DEGREE = 6
SLOTS = 16
ID_ROW = 12
GROUP = 8
LANES = 128
LOW = 64
SKEW = 4
PARTS = 4
STEPS = 4
SIDE = 4
ORDER = (2, 1, 3, 0)
MESH = pl.DeviceIdType.MESH
F32 = jnp.float32
BF16 = jnp.bfloat16


def dot(a, b):
    return jnp.dot(a, b, preferred_element_type=F32)


def iota(shape, axis):
    return lax.broadcasted_iota(jnp.int32, shape, axis)


def half_silu(h):
    return h + h * jnp.tanh(h)


def kernel(
    bands,
    sectors,
    count_ref,
    owner_hbm,
    node_hbm,
    sender_hbm,
    in_b_hbm,
    enc_b_hbm,
    edge_b_hbm,
    scale_hbm,
    gain_hbm,
    obs_hbm,
    in_w_hbm,
    out_w_hbm,
    enc_w_hbm,
    base_hbm,
    recv_hbm,
    send_hbm,
    out_ref,
    owner_ref,
    node_ref,
    sender_ref,
    in_b_ref,
    enc_b_ref,
    obs_ref,
    in_w_ref,
    out_w_ref,
    enc_w_ref,
    vectors,
    slot_ids,
    rim_sum,
    rim_count,
    send_buf,
    arrived,
    message,
    node_base,
    recv_w,
    send_w,
    picks,
    latent,
    latent_in,
    table,
    recv_base,
    sent,
    sent_in,
    halo,
    agg,
    out_buf,
    local_sem,
    weight_sem,
    weight_in_sem,
    send_sem,
    arrive_sem,
    pass_sem,
    pass_in_sem,
    latent_sem,
    latent_in_sem,
    sent_sem,
    sent_in_sem,
    halo_sem,
    halo_in_sem,
    share_sem,
    share_in_sem,
    out_send_sem,
    out_in_sem,
):
    band = lax.axis_index("band")
    sector = lax.axis_index("sector")
    core = lax.axis_index("chan")
    other = 1 - core
    geo = bands * sectors
    pairs = geo // 2
    partner = (band, sector, other)
    rows = obs_ref.shape[0]
    node_rows, width = node_base.shape
    tiles = 2 * width // LANES
    run = node_rows // PARTS
    mine_rows = run // 2
    piece = mine_rows // 2
    table_rows = table.shape[0] // tiles
    base_rows = recv_base.shape[0] // tiles
    groups = geo // GROUP
    per_step = pairs // STEPS

    def local_copy(n, source, target):
        return pltpu.make_async_copy(source, target, local_sem.at[n])

    first_copies = [
        local_copy(0, obs_hbm, obs_ref),
        local_copy(1, in_w_hbm, in_w_ref),
        local_copy(2, out_w_hbm, out_w_ref),
        local_copy(7, owner_hbm, owner_ref),
        local_copy(8, node_hbm, node_ref),
        local_copy(9, in_b_hbm, in_b_ref),
    ]
    sender_copy = local_copy(10, sender_hbm, sender_ref)
    enc_copies = [local_copy(3, enc_w_hbm, enc_w_ref), local_copy(11, enc_b_hbm, enc_b_ref)]
    vector_copies = [
        local_copy(12 + n, ref, vectors.at[n, core])
        for n, ref in enumerate((edge_b_hbm, scale_hbm, gain_hbm))
    ]
    base_copy = local_copy(4, base_hbm, node_base)
    send_w_copy = local_copy(5, send_hbm, send_w.at[core])
    recv_w_copy = local_copy(6, recv_hbm, recv_w.at[core])
    for copy in first_copies:
        copy.start()

    sides = [(0, 1), (1, 0), (0, -1), (-1, 0)]

    def neighbour(i, j):
        return (
            lax.rem(band + (i + bands), bands),
            lax.rem(sector + (j + sectors), sectors),
            core,
        )

    row, column = lax.div(band, SIDE), lax.rem(band, SIDE)
    to_row = [lax.rem(row + n, SIDE) * SIDE for n in range(SIDE)]
    to_column = [lax.rem(column + n, SIDE) for n in range(SIDE)]
    to_sector = [lax.rem(sector + (2 * n + core), sectors) for n in range(SIDE)]

    def target_of(k):
        n, i, j = ORDER[k // SIDE**2], ORDER[k // SIDE % SIDE], ORDER[k % SIDE]
        return to_row[i] + to_column[j], to_sector[n], core

    barrier = pltpu.get_barrier_semaphore()

    def greet(device):
        pl.semaphore_signal(barrier, inc=1, device_id=device, device_id_type=MESH)

    for k in range(pairs - 1):
        greet(target_of(k))

    @pl.when(core == 1)
    def _():
        greet(target_of(pairs - 1))

    greet(partner)
    for d in sides:
        greet(neighbour(*d))

    for copy in first_copies:
        copy.wait()
    for copy in enc_copies + [base_copy, send_w_copy, recv_w_copy, sender_copy] + vector_copies:
        copy.start()
    obs = obs_ref[...]
    hidden = half_silu(0.5 * (dot(obs, in_w_ref[...]) + in_b_ref[...])).astype(BF16)
    embedded = (obs.astype(F32) + dot(hidden, out_w_ref[...])).astype(BF16)
    owner = owner_ref[...]
    node = node_ref[...]
    live = iota((1, rows), 1) < count_ref[0] * (rows // PIECES)
    same = (owner == iota((geo, rows), 0)).astype(F32)
    span = rows // 4
    upto = (iota((span, span), 0) <= iota((span, span), 1)).astype(F32).astype(BF16)
    before = jnp.zeros((geo, 1), F32)
    ranks = []
    for n in range(4):
        some = same[:, n * span : (n + 1) * span]
        rank = dot(some.astype(BF16), upto) + before
        before = rank[:, span - 1 :]
        ranks.append(jnp.sum(rank * some, axis=0, keepdims=True))
    position = jnp.concatenate(ranks, axis=1).astype(jnp.int32) - 1
    further = (owner % sectors - sector + sectors) % sectors
    valid = jnp.logical_and(live, further % 2 == core)
    owner_band = owner // sectors

    def place_of(distance):
        return jnp.where(
            distance == 2, 0, jnp.where(distance == 1, 1, jnp.where(distance == 3, 2, 3))
        )

    step = (
        place_of(further // 2) * SIDE**2
        + place_of((owner_band // SIDE - row + SIDE) % SIDE) * SIDE
        + place_of((owner_band % SIDE - column + SIDE) % SIDE)
    )
    slot = jnp.where(valid, step * SLOTS + position, -1)
    lane = SLOTS * (step % GROUP) + position
    high = iota((2 * LANES, rows), 0) == lane
    low = iota((2 * LANES, rows), 0) == lane + LANES
    ids = jnp.where(
        high,
        (node // LOW + 1).astype(F32),
        jnp.where(low, (node % LOW).astype(F32), 0.0),
    ).astype(BF16)
    mine = (iota((pairs, rows), 0) == jnp.where(valid, step, -1)).astype(F32).astype(BF16)
    id_rows = lax.dot_general(
        mine, ids, (((1,), (1,)), ((), ())), preferred_element_type=F32
    ).astype(BF16)

    def block_copy(k):
        return pltpu.make_async_remote_copy(
            src_ref=send_buf.at[k],
            dst_ref=arrived.at[core, k],
            send_sem=send_sem.at[k // per_step],
            recv_sem=arrive_sem.at[k // per_step],
            device_id=target_of(k),
            device_id_type=MESH,
        )

    def pack(g):
        first = g * per_step * SLOTS
        count = per_step * SLOTS
        place = (slot == first + iota((count, rows), 0)).astype(F32).astype(BF16)
        spread = first + iota((count, pairs), 0) == iota((count, pairs), 1) * SLOTS + ID_ROW
        block = dot(place, embedded) + dot(spread.astype(F32).astype(BF16), id_rows)
        send_buf[pl.ds(g * per_step, per_step)] = block.astype(BF16).reshape(per_step, SLOTS, -1)

    def send(g):
        for k in range(g * per_step, (g + 1) * per_step):
            if k < pairs - 1:
                block_copy(k).start()
                continue

            @pl.when(core == 1)
            def _():
                block_copy(k).start()

            @pl.when(core == 0)
            def _():
                pltpu.make_async_copy(
                    send_buf.at[k], arrived.at[core, k], arrive_sem.at[k // per_step]
                ).start()

    pack(0)
    pl.semaphore_wait(barrier, pairs - 1 + core + len(sides) + 1)
    send(0)
    for g in range(1, STEPS):
        pack(g)
        send(g)

    def weight_copy(n, source, target):
        return pltpu.make_async_remote_copy(
            src_ref=source,
            dst_ref=target,
            send_sem=weight_sem.at[n],
            recv_sem=weight_in_sem.at[n],
            device_id=partner,
            device_id_type=MESH,
        )

    weights = [
        weight_copy(0, send_hbm, send_w.at[core]),
        weight_copy(1, recv_hbm, recv_w.at[core]),
    ] + [
        weight_copy(2 + n, ref, vectors.at[n, core])
        for n, ref in enumerate((edge_b_hbm, scale_hbm, gain_hbm))
    ]
    for copy in weights:
        copy.start()

    def blocks_of(g):
        return pl.ds(g * per_step, per_step)

    def pass_on(g, side):
        block = arrived.at[side, blocks_of(g)]
        return pltpu.make_async_remote_copy(
            src_ref=block,
            dst_ref=block,
            send_sem=pass_sem.at[g],
            recv_sem=pass_in_sem.at[g],
            device_id=partner,
            device_id_type=MESH,
        )

    def group_wait(g, less=0):
        span = pl.ds(g * per_step, per_step - less)
        return pltpu.make_async_remote_copy(
            src_ref=send_buf.at[span],
            dst_ref=arrived.at[core, span],
            send_sem=send_sem.at[g],
            recv_sem=arrive_sem.at[g],
            device_id=partner,
            device_id_type=MESH,
        )

    count = pairs * SLOTS
    id_groups = pairs // GROUP
    at = iota((id_groups, count), 1)
    chosen = jnp.logical_and(
        at // (GROUP * SLOTS) == iota((id_groups, count), 0), at % SLOTS == ID_ROW
    )
    chosen = chosen.astype(F32).astype(BF16)

    def hits(q, names):
        return (iota((run, LANES), 0) + q * run == names).astype(F32)

    def take(side):
        block = arrived[side].reshape(count, -1)
        content = half_silu(0.5 * (dot(block, enc_w_ref[...]) + enc_b_ref[...])).astype(BF16)
        message[pl.ds(pl.multiple_of(side * count, count), count), :] = content
        found = dot(chosen, block)
        names = ((found[:, :LANES] - 1.0) * LOW + found[:, LANES:]).astype(jnp.int32)
        slot_ids[side] = names
        some = [hits(0, names[n : n + 1, :]) for n in range(id_groups)]
        value = dot(jnp.concatenate(some, axis=1).astype(BF16), content)
        return value, sum(some[1:], some[0])

    for copy in enc_copies:
        copy.wait()
    for g in range(STEPS):
        group_wait(g).wait_recv()
        pass_on(g, core).start()
    rim_sum[...], rim_count[...] = take(core)
    for g in range(STEPS):
        pass_on(g, other).wait_recv()
    rim_rest, rim_more = take(other)

    def latent_copy(q):
        return pltpu.make_async_remote_copy(
            src_ref=latent.at[q, other],
            dst_ref=latent_in.at[q],
            send_sem=latent_sem.at[q],
            recv_sem=latent_in_sem.at[q],
            device_id=partner,
            device_id_type=MESH,
        )

    def end_latent(q, total, number):
        scale = 1.0 / jnp.maximum(jnp.sum(number, axis=1, keepdims=True), 1.0)
        base = node_base[pl.ds(pl.multiple_of(q * run, run), run), :].astype(F32)
        latent[q] = (base + total * scale).astype(BF16).reshape(2, mine_rows, width)
        latent_copy(q).start()

    def make_latent(q):
        number = jnp.zeros((run, LANES), F32)
        for g in range(groups):
            n = g % id_groups
            hit = hits(q, slot_ids[g // id_groups, n : n + 1, :])
            number = number + hit
            picks[:, g * LANES : (g + 1) * LANES] = hit.astype(BF16)
        end_latent(q, dot(picks[...], message[...]), number)

    def project(q, weight, arrival=None):
        own = dot(latent[q, core], weight[core])
        if arrival is not None:
            arrival()
        return own + dot(latent_in[q], weight[other])

    def tile(t):
        return slice(t * LANES, (t + 1) * LANES)

    def sent_copy(q):
        return pltpu.make_async_remote_copy(
            src_ref=sent.at[q],
            dst_ref=sent_in.at[q],
            send_sem=sent_sem.at[q],
            recv_sem=sent_in_sem.at[q],
            device_id=partner,
            device_id_type=MESH,
        )

    def project_send(q, arrival=None):
        value = (0.5 * project(q, send_w, arrival)).astype(BF16)
        wide = value.astype(F32)
        for t in range(tiles):
            for h in range(2):
                sent[q, h, t] = value[h * piece : (h + 1) * piece, tile(t)]
            table[pl.ds(t * table_rows + q * run + core * mine_rows, mine_rows), :] = wide[
                :, tile(t)
            ]
        sent_copy(q).start()

    def project_recv(q):
        value = project(q, recv_w).astype(BF16).astype(F32)
        for t in range(tiles):
            bias = vectors[0, t // (tiles // 2), :, tile(t % (tiles // 2))]
            recv_base[pl.ds(t * base_rows + q * mine_rows, mine_rows), :] = 0.5 * (
                value[:, tile(t)] + bias
            )

    def widen(first, source):
        for t in range(tiles):
            table[pl.ds(t * table_rows + first, source.shape[1]), :] = source[t].astype(F32)

    def first_arrival():
        weights[0].wait_recv()
        latent_copy(0).wait_recv()

    base_copy.wait()
    end_latent(0, rim_sum[...] + rim_rest, rim_count[...] + rim_more)
    send_w_copy.wait()
    project_send(0, first_arrival)

    turns = [(d, e) for d in sides for e in sides if (d[0] == 0) != (e[0] == 0)]

    def group_of(i, j):
        return (1 - i) * 3 + 1 - j

    def halo_copy(half, d):
        n = half * 4 + sides.index(d)
        return pltpu.make_async_remote_copy(
            src_ref=sent.at[0, half],
            dst_ref=halo.at[group_of(*d), core, half],
            send_sem=halo_sem.at[n],
            recv_sem=halo_in_sem.at[n],
            device_id=neighbour(*d),
            device_id_type=MESH,
        )

    split = piece * 3 // 5
    cuts = {None: pl.ds(0, piece), 0: pl.ds(0, split), 1: pl.ds(split, piece - split)}

    def corner_copy(d, e, cut=None):
        half = 0 if d[0] == 0 else 1
        n = 8 + turns.index((d, e)) + (8 if cut == 1 else 0)
        return pltpu.make_async_remote_copy(
            src_ref=halo.at[group_of(*d), core, half, :, cuts[cut]],
            dst_ref=halo.at[group_of(d[0] + e[0], d[1] + e[1]), core, half, :, cuts[cut]],
            send_sem=halo_sem.at[n],
            recv_sem=halo_in_sem.at[n],
            device_id=neighbour(*e),
            device_id_type=MESH,
        )

    def share(group, half, side, cut=None):
        block = halo.at[group, side, half, :, cuts[cut]]
        n = group * 2 + half + (18 if cut == 1 else 0)
        return pltpu.make_async_remote_copy(
            src_ref=block,
            dst_ref=block,
            send_sem=share_sem.at[n],
            recv_sem=share_in_sem.at[n],
            device_id=partner,
            device_id_type=MESH,
        )

    def widen_halo(group, half, side, cut=None):
        first = node_rows + group * run + half * piece + side * mine_rows
        widen(first + (split if cut == 1 else 0), halo.at[group, side, half, :, cuts[cut]])

    early = {d: 0 if d[0] == 0 else 1 for d in sides}
    first_turns, second_turns = turns[: len(sides)], turns[len(sides) :]

    def corner_of(d, e):
        return group_of(d[0] + e[0], d[1] + e[1]), early[d]

    def comes(d):
        return {1: band > 0, 0: None, -1: band < bands - 1}[d[0]]

    def goes(d):
        return comes((-d[0], 0))

    def when(condition, act):
        if condition is None:
            act()
        else:
            pl.when(condition)(act)

    def comes_corner(d, e):
        return comes((d[0] + e[0], 0))

    def goes_corner(d, e):
        return comes(d) if d[0] else goes(e)

    for d in sides:
        when(goes(d), lambda: halo_copy(early[d], d).start())

    make_latent(1)
    for d in sides:

        def second_half():
            halo_copy(early[d], d).wait_send()
            halo_copy(1 - early[d], d).start()

        when(goes(d), second_half)
    for d in sides:
        when(comes(d), lambda: halo_copy(early[d], d).wait_recv())
        for t in first_turns:
            if t[0] == d:
                when(goes_corner(*t), lambda: corner_copy(*t).start())
    for d in sides:
        when(comes(d), lambda: share(group_of(*d), early[d], core).start())

    def later_latent(q, carry):
        make_latent(q)
        return carry

    lax.fori_loop(2, PARTS, later_latent, 0)
    for copy in [recv_w_copy, sender_copy] + vector_copies:
        copy.wait()
    for copy in weights[1:]:
        copy.wait_recv()
    project_recv(0)

    def later_project(q, carry):
        latent_copy(q).wait_recv()
        project_send(q)
        project_recv(q)
        return carry

    lax.fori_loop(1, PARTS, later_project, 0)
    for e in sides:
        for t in first_turns:
            if t[1] == e:
                when(goes_corner(*t), lambda: corner_copy(*t).wait_send())
        for cut in range(2):
            for t in second_turns:
                if t[1] == e:
                    when(goes_corner(*t), lambda: corner_copy(*t, cut).start())

    def widen_sent(q, carry):
        sent_copy(q).wait_recv()
        for h in range(2):
            widen(q * run + h * piece + other * mine_rows, sent_in.at[q, h])
        return carry

    lax.fori_loop(0, PARTS, widen_sent, 0)

    def widen_both(group, half):
        widen_halo(group, half, core)
        share(group, half, other).wait_recv()
        widen_halo(group, half, other)

    for d in sides:
        when(comes(d), lambda: widen_both(group_of(*d), early[d]))

    @pl.when(core == 0)
    def _():
        group_wait(STEPS - 1, 1).wait_send()

    @pl.when(core == 1)
    def _():
        group_wait(STEPS - 1).wait_send()

    for g in range(STEPS - 1):
        group_wait(g).wait_send()
    for g in range(STEPS):
        pass_on(g, core).wait_send()
    for copy in weights:
        copy.wait_send()
    for q in range(PARTS):
        latent_copy(q).wait_send()
        sent_copy(q).wait_send()

    for d in sides:

        def second_arrival():
            halo_copy(1 - early[d], d).wait_recv()
            share(group_of(*d), 1 - early[d], core).start()

        when(comes(d), second_arrival)

    def corner_arrival(t, cut=None):
        corner_copy(*t, cut).wait_recv()
        share(*corner_of(*t), core, cut).start()

    for t in first_turns:
        when(comes_corner(*t), lambda: corner_arrival(t))
    for d in sides:
        when(comes(d), lambda: widen_both(group_of(*d), 1 - early[d]))
    for t in first_turns:
        when(comes_corner(*t), lambda: widen_both(*corner_of(*t)))
    for cut in range(2):
        for t in second_turns:
            when(comes_corner(*t), lambda: corner_arrival(t, cut))
        for t in second_turns:
            when(comes_corner(*t), lambda: widen_halo(*corner_of(*t), core, cut))

    def widen_shared(t, cut):
        share(*corner_of(*t), other, cut).wait_recv()
        widen_halo(*corner_of(*t), other, cut)

    for cut in range(2):
        for t in second_turns:
            when(comes_corner(*t), lambda: widen_shared(t, cut))

    unroll = 32

    def one_node(q, r):
        place = q * mine_rows + r
        base = recv_base[pl.ds(place, tiles, stride=base_rows), :]
        first = (q * run + core * mine_rows + r) * DEGREE
        total = None
        for k in range(DEGREE):
            sender = table[pl.ds(sender_ref[first + k], tiles, stride=table_rows), :]
            term = half_silu(base + sender)
            total = term if total is None else total + term
        agg[pl.ds(place, tiles, stride=base_rows), :] = total

    def out_rows(q):
        return pl.ds(pl.multiple_of(q * run + core * mine_rows, mine_rows), mine_rows)

    def out_send(q):
        return pltpu.make_async_remote_copy(
            src_ref=out_buf.at[q],
            dst_ref=out_ref.at[out_rows(q)],
            send_sem=out_send_sem.at[q],
            recv_sem=out_in_sem.at[q],
            device_id=partner,
            device_id_type=MESH,
        )

    def edges(q, carry):
        def some(m, inner):
            for u in range(unroll):
                one_node(q, m * unroll + u)
            return inner

        lax.fori_loop(0, mine_rows // unroll, some, 0)

        def scaled(t):
            bias = vectors[1, t // (tiles // 2), :, tile(t % (tiles // 2))]
            return agg[pl.ds(t * base_rows + q * mine_rows, mine_rows), :] * bias

        square = jnp.zeros((mine_rows, LANES), F32)
        for t in range(tiles):
            value = scaled(t)
            square = square + value * value
        mean = jnp.sum(square, axis=1, keepdims=True) / (2 * width)
        factor = lax.rsqrt(mean + 1e-05)

        def finish(side, held, target):
            for t in range(tiles // 2):
                gain = vectors[2, side, :, tile(t)]
                normed = scaled(side * (tiles // 2) + t) * factor * gain
                target[:, tile(t)] = (held[:, tile(t)].astype(F32) + normed).astype(BF16)

        for side in range(2):

            @pl.when(core == side)
            def _():
                finish(1 - side, latent_in[q], out_buf.at[q])
                out_send(q).start()
                finish(side, latent[q, side], out_ref.at[out_rows(q)])

        return carry

    lax.fori_loop(0, PARTS, edges, 0)

    def drain_side(d):
        for half in range(2):
            share(group_of(*d), half, core).wait_send()

    for d in sides:
        when(goes(d), lambda: halo_copy(1 - early[d], d).wait_send())
        when(comes(d), lambda: drain_side(d))
    for t in first_turns:
        when(comes_corner(*t), lambda: share(*corner_of(*t), core).wait_send())
    for cut in range(2):
        for t in second_turns:
            when(goes_corner(*t), lambda: corner_copy(*t, cut).wait_send())
            when(comes_corner(*t), lambda: share(*corner_of(*t), core, cut).wait_send())
    for q in range(PARTS):
        out_send(q).wait()


def local(
    obs_features,
    obs_owner,
    obs_node,
    obs_count,
    edge_senders,
    obs_in_w,
    obs_in_b,
    obs_out_w,
    enc_w,
    enc_b,
    node_base,
    recv_w,
    send_w,
    edge_b,
    channel_scale,
    norm_gain,
):
    bands = lax.axis_size("band")
    sectors = lax.axis_size("sector")
    geo = bands * sectors
    pairs = geo // 2
    rows, embed = obs_features.shape
    node_rows, width = node_base.shape
    tiles = 2 * width // LANES
    run = node_rows // PARTS
    mine_rows = run // 2
    piece = mine_rows // 2
    slots = geo * SLOTS
    vmem = pl.BlockSpec(memory_space=pltpu.VMEM)
    smem = pl.BlockSpec(memory_space=pltpu.SMEM)
    hbm = pl.BlockSpec(memory_space=pl.ANY)
    dma = pltpu.SemaphoreType.DMA
    return pl.pallas_call(
        functools.partial(kernel, bands, sectors),
        out_shape=pltpu.VMEM((node_rows, width), BF16),
        in_specs=[smem] + [hbm] * 15,
        out_specs=vmem,
        scratch_shapes=[
            pltpu.VMEM((1, rows), jnp.int32),
            pltpu.VMEM((1, rows), jnp.int32),
            pltpu.SMEM((node_rows * DEGREE,), jnp.int32),
            pltpu.VMEM((1, embed), F32),
            pltpu.VMEM((1, width), F32),
            pltpu.VMEM((rows, embed), BF16),
            pltpu.VMEM((embed, embed), BF16),
            pltpu.VMEM((embed, embed), BF16),
            pltpu.VMEM((embed, width), BF16),
            pltpu.VMEM((3, 2, 1, width), F32),
            pltpu.VMEM((2, pairs // GROUP, LANES), jnp.int32),
            pltpu.VMEM((run, width), F32),
            pltpu.VMEM((run, LANES), F32),
            pltpu.VMEM((pairs, SLOTS, embed), BF16),
            pltpu.VMEM((2, pairs, SLOTS, embed), BF16),
            pltpu.VMEM((slots, width), BF16),
            pltpu.VMEM((node_rows, width), BF16),
            pltpu.VMEM((2, width, 2 * width), BF16),
            pltpu.VMEM((2, width, 2 * width), BF16),
            pltpu.VMEM((run, slots), BF16),
            pltpu.VMEM((PARTS, 2, mine_rows, width), BF16),
            pltpu.VMEM((PARTS, mine_rows, width), BF16),
            pltpu.VMEM((tiles * (node_rows + 9 * run + SKEW), LANES), F32),
            pltpu.VMEM((tiles * (PARTS * mine_rows + SKEW), LANES), F32),
            pltpu.VMEM((PARTS, 2, tiles, piece, LANES), BF16),
            pltpu.VMEM((PARTS, 2, tiles, piece, LANES), BF16),
            pltpu.VMEM((9, 2, 2, tiles, piece, LANES), BF16),
            pltpu.VMEM((tiles * (PARTS * mine_rows + SKEW), LANES), F32),
            pltpu.VMEM((PARTS, mine_rows, width), BF16),
            dma((15,)),
            dma((5,)),
            dma((5,)),
            dma((STEPS,)),
            dma((STEPS,)),
            dma((STEPS,)),
            dma((STEPS,)),
            dma((PARTS,)),
            dma((PARTS,)),
            dma((PARTS,)),
            dma((PARTS,)),
            dma((24,)),
            dma((24,)),
            dma((36,)),
            dma((36,)),
            dma((PARTS,)),
            dma((PARTS,)),
        ],
        compiler_params=pltpu.CompilerParams(
            collective_id=0, has_side_effects=True, vmem_limit_bytes=56 * 2**20
        ),
        name="encode_and_pass",
    )(
        obs_count,
        obs_owner.reshape(1, rows),
        obs_node.reshape(1, rows),
        edge_senders,
        obs_in_b.reshape(1, -1),
        enc_b.reshape(1, -1),
        edge_b.reshape(1, -1),
        channel_scale.reshape(1, -1),
        norm_gain.reshape(1, -1),
        obs_features,
        obs_in_w,
        obs_out_w,
        enc_w,
        node_base,
        recv_w,
        send_w,
    )


def solution(mesh):
    in_specs = (
        P(("band", "sector"), None),
        P(("band", "sector"), None),
        P(("band", "sector")),
        P(("band", "sector")),
        P(("band", "sector")),
        P(),
        P(),
        P(),
        P(None, "chan"),
        P("chan"),
        P(("band", "sector"), "chan"),
        P("chan", None),
        P("chan", None),
        P("chan"),
        P("chan"),
        P("chan"),
    )
    out_specs = P(("band", "sector"), "chan")
    return jax.shard_map(local, mesh=mesh, in_specs=in_specs, out_specs=out_specs, check_vma=False)
```

```python
import functools

import jax
import jax.numpy as jnp
from jax import lax
from jax.experimental import pallas as pl
from jax.experimental.pallas import tpu as pltpu
from jax.sharding import PartitionSpec as P

PIECES = 8
DEGREE = 6
SLOTS = 16
ID_ROW = 12
GROUP = 8
LANES = 128
LOW = 64
SKEW = 4
PARTS = 4
STEPS = 4
SIDE = 4
ORDER = (2, 1, 3, 0)
MESH = pl.DeviceIdType.MESH
F32 = jnp.float32
BF16 = jnp.bfloat16


def dot(a, b):
    return jnp.dot(a, b, preferred_element_type=F32)


def iota(shape, axis):
    return lax.broadcasted_iota(jnp.int32, shape, axis)


def half_silu(h):
    return h + h * jnp.tanh(h)


def kernel(
    bands,
    sectors,
    count_ref,
    owner_hbm,
    node_hbm,
    sender_hbm,
    in_b_hbm,
    enc_b_hbm,
    edge_b_hbm,
    scale_hbm,
    gain_hbm,
    obs_hbm,
    in_w_hbm,
    out_w_hbm,
    enc_w_hbm,
    base_hbm,
    recv_hbm,
    send_hbm,
    out_ref,
    owner_ref,
    node_ref,
    sender_ref,
    in_b_ref,
    enc_b_ref,
    obs_ref,
    in_w_ref,
    out_w_ref,
    enc_w_ref,
    vectors,
    slot_ids,
    rim_sum,
    rim_count,
    send_buf,
    arrived,
    message,
    node_base,
    recv_w,
    send_w,
    picks,
    latent,
    latent_in,
    table,
    recv_base,
    sent,
    sent_in,
    halo,
    agg_even,
    agg_odd,
    out_buf,
    local_sem,
    weight_sem,
    weight_in_sem,
    send_sem,
    arrive_sem,
    pass_sem,
    pass_in_sem,
    latent_sem,
    latent_in_sem,
    sent_sem,
    sent_in_sem,
    halo_sem,
    halo_in_sem,
    share_sem,
    share_in_sem,
    out_send_sem,
    out_in_sem,
):
    band = lax.axis_index("band")
    sector = lax.axis_index("sector")
    core = lax.axis_index("chan")
    other = 1 - core
    geo = bands * sectors
    pairs = geo // 2
    partner = (band, sector, other)
    rows = obs_ref.shape[0]
    node_rows, width = node_base.shape
    tiles = 2 * width // LANES
    run = node_rows // PARTS
    mine_rows = run // 2
    piece = mine_rows // 2
    table_rows = table.shape[0] // tiles
    base_rows = recv_base.shape[0] // tiles
    groups = geo // GROUP
    per_step = pairs // STEPS

    def local_copy(n, source, target):
        return pltpu.make_async_copy(source, target, local_sem.at[n])

    first_copies = [
        local_copy(0, obs_hbm, obs_ref),
        local_copy(1, in_w_hbm, in_w_ref),
        local_copy(2, out_w_hbm, out_w_ref),
        local_copy(7, owner_hbm, owner_ref),
        local_copy(8, node_hbm, node_ref),
        local_copy(9, in_b_hbm, in_b_ref),
    ]
    sender_copy = local_copy(10, sender_hbm, sender_ref)
    enc_copies = [local_copy(3, enc_w_hbm, enc_w_ref), local_copy(11, enc_b_hbm, enc_b_ref)]
    vector_copies = [
        local_copy(12 + n, ref, vectors.at[n, core])
        for n, ref in enumerate((edge_b_hbm, scale_hbm, gain_hbm))
    ]
    base_copy = local_copy(4, base_hbm, node_base)
    send_w_copy = local_copy(5, send_hbm, send_w.at[core])
    recv_w_copy = local_copy(6, recv_hbm, recv_w.at[core])
    for copy in first_copies:
        copy.start()

    sides = [(0, 1), (1, 0), (0, -1), (-1, 0)]

    def neighbour(i, j):
        return (
            lax.rem(band + (i + bands), bands),
            lax.rem(sector + (j + sectors), sectors),
            core,
        )

    row, column = lax.div(band, SIDE), lax.rem(band, SIDE)
    to_row = [lax.rem(row + n, SIDE) * SIDE for n in range(SIDE)]
    to_column = [lax.rem(column + n, SIDE) for n in range(SIDE)]
    to_sector = [lax.rem(sector + (2 * n + core), sectors) for n in range(SIDE)]

    def target_of(k):
        n, i, j = ORDER[k // SIDE**2], ORDER[k // SIDE % SIDE], ORDER[k % SIDE]
        return to_row[i] + to_column[j], to_sector[n], core

    barrier = pltpu.get_barrier_semaphore()

    def greet(device):
        pl.semaphore_signal(barrier, inc=1, device_id=device, device_id_type=MESH)

    for k in range(pairs - 1):
        greet(target_of(k))

    @pl.when(core == 1)
    def _():
        greet(target_of(pairs - 1))

    greet(partner)
    for d in sides:
        greet(neighbour(*d))

    for copy in first_copies:
        copy.wait()
    for copy in enc_copies + [base_copy, send_w_copy, recv_w_copy, sender_copy] + vector_copies:
        copy.start()
    obs = obs_ref[...]
    hidden = half_silu(0.5 * (dot(obs, in_w_ref[...]) + in_b_ref[...])).astype(BF16)
    embedded = (obs.astype(F32) + dot(hidden, out_w_ref[...])).astype(BF16)
    owner = owner_ref[...]
    node = node_ref[...]
    live = iota((1, rows), 1) < count_ref[0] * (rows // PIECES)
    same = (owner == iota((geo, rows), 0)).astype(F32)
    span = rows // 4
    upto = (iota((span, span), 0) <= iota((span, span), 1)).astype(F32).astype(BF16)
    before = jnp.zeros((geo, 1), F32)
    ranks = []
    for n in range(4):
        some = same[:, n * span : (n + 1) * span]
        rank = dot(some.astype(BF16), upto) + before
        before = rank[:, span - 1 :]
        ranks.append(jnp.sum(rank * some, axis=0, keepdims=True))
    position = jnp.concatenate(ranks, axis=1).astype(jnp.int32) - 1
    further = (owner % sectors - sector + sectors) % sectors
    valid = jnp.logical_and(live, further % 2 == core)
    owner_band = owner // sectors

    def place_of(distance):
        return jnp.where(
            distance == 2, 0, jnp.where(distance == 1, 1, jnp.where(distance == 3, 2, 3))
        )

    step = (
        place_of(further // 2) * SIDE**2
        + place_of((owner_band // SIDE - row + SIDE) % SIDE) * SIDE
        + place_of((owner_band % SIDE - column + SIDE) % SIDE)
    )
    slot = jnp.where(valid, step * SLOTS + position, -1)
    lane = SLOTS * (step % GROUP) + position
    high = iota((2 * LANES, rows), 0) == lane
    low = iota((2 * LANES, rows), 0) == lane + LANES
    ids = jnp.where(
        high,
        (node // LOW + 1).astype(F32),
        jnp.where(low, (node % LOW).astype(F32), 0.0),
    ).astype(BF16)
    mine = (iota((pairs, rows), 0) == jnp.where(valid, step, -1)).astype(F32).astype(BF16)
    id_rows = lax.dot_general(
        mine, ids, (((1,), (1,)), ((), ())), preferred_element_type=F32
    ).astype(BF16)

    def block_copy(k):
        return pltpu.make_async_remote_copy(
            src_ref=send_buf.at[k],
            dst_ref=arrived.at[core, k],
            send_sem=send_sem.at[k // per_step],
            recv_sem=arrive_sem.at[k // per_step],
            device_id=target_of(k),
            device_id_type=MESH,
        )

    def pack(g):
        first = g * per_step * SLOTS
        count = per_step * SLOTS
        place = (slot == first + iota((count, rows), 0)).astype(F32).astype(BF16)
        spread = first + iota((count, pairs), 0) == iota((count, pairs), 1) * SLOTS + ID_ROW
        block = dot(place, embedded) + dot(spread.astype(F32).astype(BF16), id_rows)
        send_buf[pl.ds(g * per_step, per_step)] = block.astype(BF16).reshape(per_step, SLOTS, -1)

    def send(g):
        for k in range(g * per_step, (g + 1) * per_step):
            if k < pairs - 1:
                block_copy(k).start()
                continue

            @pl.when(core == 1)
            def _():
                block_copy(k).start()

            @pl.when(core == 0)
            def _():
                pltpu.make_async_copy(
                    send_buf.at[k], arrived.at[core, k], arrive_sem.at[k // per_step]
                ).start()

    for g in range(STEPS):
        pack(g)
    pl.semaphore_wait(barrier, pairs - 1 + core + len(sides) + 1)
    for g in range(STEPS):
        send(g)

    def weight_copy(n, source, target):
        return pltpu.make_async_remote_copy(
            src_ref=source,
            dst_ref=target,
            send_sem=weight_sem.at[n],
            recv_sem=weight_in_sem.at[n],
            device_id=partner,
            device_id_type=MESH,
        )

    weights = [
        weight_copy(0, send_hbm, send_w.at[core]),
        weight_copy(1, recv_hbm, recv_w.at[core]),
    ] + [
        weight_copy(2 + n, ref, vectors.at[n, core])
        for n, ref in enumerate((edge_b_hbm, scale_hbm, gain_hbm))
    ]
    for copy in weights:
        copy.start()

    def blocks_of(g):
        return pl.ds(g * per_step, per_step)

    def pass_on(g, side):
        block = arrived.at[side, blocks_of(g)]
        return pltpu.make_async_remote_copy(
            src_ref=block,
            dst_ref=block,
            send_sem=pass_sem.at[g],
            recv_sem=pass_in_sem.at[g],
            device_id=partner,
            device_id_type=MESH,
        )

    def group_wait(g, less=0):
        span = pl.ds(g * per_step, per_step - less)
        return pltpu.make_async_remote_copy(
            src_ref=send_buf.at[span],
            dst_ref=arrived.at[core, span],
            send_sem=send_sem.at[g],
            recv_sem=arrive_sem.at[g],
            device_id=partner,
            device_id_type=MESH,
        )

    count = pairs * SLOTS
    id_groups = pairs // GROUP
    at = iota((id_groups, count), 1)
    chosen = jnp.logical_and(
        at // (GROUP * SLOTS) == iota((id_groups, count), 0), at % SLOTS == ID_ROW
    )
    chosen = chosen.astype(F32).astype(BF16)

    def hits(q, names):
        return (iota((run, LANES), 0) + q * run == names).astype(F32)

    def take(side):
        block = arrived[side].reshape(count, -1)
        content = half_silu(0.5 * (dot(block, enc_w_ref[...]) + enc_b_ref[...])).astype(BF16)
        message[pl.ds(pl.multiple_of(side * count, count), count), :] = content
        found = dot(chosen, block)
        names = ((found[:, :LANES] - 1.0) * LOW + found[:, LANES:]).astype(jnp.int32)
        slot_ids[side] = names
        some = [hits(0, names[n : n + 1, :]) for n in range(id_groups)]
        value = dot(jnp.concatenate(some, axis=1).astype(BF16), content)
        return value, sum(some[1:], some[0])

    for copy in enc_copies:
        copy.wait()
    for g in range(STEPS):
        group_wait(g).wait_recv()
        pass_on(g, core).start()
    rim_sum[...], rim_count[...] = take(core)
    for g in range(STEPS):
        pass_on(g, other).wait_recv()
    rim_rest, rim_more = take(other)

    def latent_copy(q):
        return pltpu.make_async_remote_copy(
            src_ref=latent.at[q, other],
            dst_ref=latent_in.at[q],
            send_sem=latent_sem.at[q],
            recv_sem=latent_in_sem.at[q],
            device_id=partner,
            device_id_type=MESH,
        )

    def end_latent(q, total, number):
        scale = 1.0 / jnp.maximum(jnp.sum(number, axis=1, keepdims=True), 1.0)
        base = node_base[pl.ds(pl.multiple_of(q * run, run), run), :].astype(F32)
        latent[q] = (base + total * scale).astype(BF16).reshape(2, mine_rows, width)
        latent_copy(q).start()

    def make_latent(q):
        number = jnp.zeros((run, LANES), F32)
        for g in range(groups):
            n = g % id_groups
            hit = hits(q, slot_ids[g // id_groups, n : n + 1, :])
            number = number + hit
            picks[:, g * LANES : (g + 1) * LANES] = hit.astype(BF16)
        end_latent(q, dot(picks[...], message[...]), number)

    def project(q, weight, arrival=None):
        own = dot(latent[q, core], weight[core])
        if arrival is not None:
            arrival()
        return own + dot(latent_in[q], weight[other])

    def tile(t):
        return slice(t * LANES, (t + 1) * LANES)

    def sent_copy(q):
        return pltpu.make_async_remote_copy(
            src_ref=sent.at[q],
            dst_ref=sent_in.at[q],
            send_sem=sent_sem.at[q],
            recv_sem=sent_in_sem.at[q],
            device_id=partner,
            device_id_type=MESH,
        )

    def project_send(q, arrival=None):
        value = (0.5 * project(q, send_w, arrival)).astype(BF16)
        wide = value.astype(F32)
        for t in range(tiles):
            for h in range(2):
                sent[q, h, t] = value[h * piece : (h + 1) * piece, tile(t)]
            table[pl.ds(t * table_rows + q * run + core * mine_rows, mine_rows), :] = wide[
                :, tile(t)
            ]
        sent_copy(q).start()

    def project_recv(q):
        value = project(q, recv_w).astype(BF16).astype(F32)
        for t in range(tiles):
            bias = vectors[0, t // (tiles // 2), :, tile(t % (tiles // 2))]
            recv_base[pl.ds(t * base_rows + q * mine_rows, mine_rows), :] = 0.5 * (
                value[:, tile(t)] + bias
            )

    def widen(first, source):
        for t in range(tiles):
            table[pl.ds(t * table_rows + first, source.shape[1]), :] = source[t].astype(F32)

    def first_arrival():
        weights[0].wait_recv()
        latent_copy(0).wait_recv()

    base_copy.wait()
    end_latent(0, rim_sum[...] + rim_rest, rim_count[...] + rim_more)
    send_w_copy.wait()
    project_send(0, first_arrival)

    turns = [(d, e) for d in sides for e in sides if (d[0] == 0) != (e[0] == 0)]

    def group_of(i, j):
        return (1 - i) * 3 + 1 - j

    def halo_copy(half, d):
        n = half * 4 + sides.index(d)
        return pltpu.make_async_remote_copy(
            src_ref=sent.at[0, half],
            dst_ref=halo.at[group_of(*d), core, half],
            send_sem=halo_sem.at[n],
            recv_sem=halo_in_sem.at[n],
            device_id=neighbour(*d),
            device_id_type=MESH,
        )

    split = piece * 3 // 5
    cuts = {None: pl.ds(0, piece), 0: pl.ds(0, split), 1: pl.ds(split, piece - split)}

    def corner_copy(d, e, cut=None):
        half = 0 if d[0] == 0 else 1
        n = 8 + turns.index((d, e)) + (8 if cut == 1 else 0)
        return pltpu.make_async_remote_copy(
            src_ref=halo.at[group_of(*d), core, half, :, cuts[cut]],
            dst_ref=halo.at[group_of(d[0] + e[0], d[1] + e[1]), core, half, :, cuts[cut]],
            send_sem=halo_sem.at[n],
            recv_sem=halo_in_sem.at[n],
            device_id=neighbour(*e),
            device_id_type=MESH,
        )

    def share(group, half, side, cut=None):
        block = halo.at[group, side, half, :, cuts[cut]]
        n = group * 2 + half + (18 if cut == 1 else 0)
        return pltpu.make_async_remote_copy(
            src_ref=block,
            dst_ref=block,
            send_sem=share_sem.at[n],
            recv_sem=share_in_sem.at[n],
            device_id=partner,
            device_id_type=MESH,
        )

    def widen_halo(group, half, side, cut=None):
        first = node_rows + group * run + half * piece + side * mine_rows
        widen(first + (split if cut == 1 else 0), halo.at[group, side, half, :, cuts[cut]])

    early = {d: 0 if d[0] == 0 else 1 for d in sides}
    first_turns, second_turns = turns[: len(sides)], turns[len(sides) :]

    def corner_of(d, e):
        return group_of(d[0] + e[0], d[1] + e[1]), early[d]

    def comes(d):
        return {1: band > 0, 0: None, -1: band < bands - 1}[d[0]]

    def goes(d):
        return comes((-d[0], 0))

    def when(condition, act):
        if condition is None:
            act()
        else:
            pl.when(condition)(act)

    def comes_corner(d, e):
        return comes((d[0] + e[0], 0))

    def goes_corner(d, e):
        return comes(d) if d[0] else goes(e)

    for d in sides:
        when(goes(d), lambda: halo_copy(early[d], d).start())

    make_latent(1)
    for d in sides:

        def second_half():
            halo_copy(early[d], d).wait_send()
            halo_copy(1 - early[d], d).start()

        when(goes(d), second_half)
    for d in sides:
        when(comes(d), lambda: halo_copy(early[d], d).wait_recv())
        for t in first_turns:
            if t[0] == d:
                when(goes_corner(*t), lambda: corner_copy(*t).start())
    for d in sides:
        when(comes(d), lambda: share(group_of(*d), early[d], core).start())

    def later_latent(q, carry):
        make_latent(q)
        return carry

    lax.fori_loop(2, PARTS, later_latent, 0)
    for copy in [recv_w_copy, sender_copy] + vector_copies:
        copy.wait()
    for copy in weights[1:]:
        copy.wait_recv()
    project_recv(0)

    def later_project(q, carry):
        latent_copy(q).wait_recv()
        project_send(q)
        project_recv(q)
        return carry

    lax.fori_loop(1, PARTS, later_project, 0)
    for e in sides:
        for t in first_turns:
            if t[1] == e:
                when(goes_corner(*t), lambda: corner_copy(*t).wait_send())
        for cut in range(2):
            for t in second_turns:
                if t[1] == e:
                    when(goes_corner(*t), lambda: corner_copy(*t, cut).start())

    def widen_sent(q, carry):
        sent_copy(q).wait_recv()
        for h in range(2):
            widen(q * run + h * piece + other * mine_rows, sent_in.at[q, h])
        return carry

    lax.fori_loop(0, PARTS, widen_sent, 0)

    def widen_both(group, half):
        widen_halo(group, half, core)
        share(group, half, other).wait_recv()
        widen_halo(group, half, other)

    for d in sides:
        when(comes(d), lambda: widen_both(group_of(*d), early[d]))

    @pl.when(core == 0)
    def _():
        group_wait(STEPS - 1, 1).wait_send()

    @pl.when(core == 1)
    def _():
        group_wait(STEPS - 1).wait_send()

    for g in range(STEPS - 1):
        group_wait(g).wait_send()
    for g in range(STEPS):
        pass_on(g, core).wait_send()
    for copy in weights:
        copy.wait_send()
    for q in range(PARTS):
        latent_copy(q).wait_send()
        sent_copy(q).wait_send()

    for d in sides:

        def second_arrival():
            halo_copy(1 - early[d], d).wait_recv()
            share(group_of(*d), 1 - early[d], core).start()

        when(comes(d), second_arrival)

    def corner_arrival(t, cut=None):
        corner_copy(*t, cut).wait_recv()
        share(*corner_of(*t), core, cut).start()

    for t in first_turns:
        when(comes_corner(*t), lambda: corner_arrival(t))
    for d in sides:
        when(comes(d), lambda: widen_both(group_of(*d), 1 - early[d]))
    for t in first_turns:
        when(comes_corner(*t), lambda: widen_both(*corner_of(*t)))
    for cut in range(2):
        for t in second_turns:
            when(comes_corner(*t), lambda: corner_arrival(t, cut))
        for t in second_turns:
            when(comes_corner(*t), lambda: widen_halo(*corner_of(*t), core, cut))

    def widen_shared(t, cut):
        share(*corner_of(*t), other, cut).wait_recv()
        widen_halo(*corner_of(*t), other, cut)

    for cut in range(2):
        for t in second_turns:
            when(comes_corner(*t), lambda: widen_shared(t, cut))

    unroll = 32
    agg = (agg_even, agg_odd)

    agg_rows = agg[0].shape[0] // tiles

    def one_node(q, r):
        base = recv_base[pl.ds(q * mine_rows + r, tiles, stride=base_rows), :]
        first = (q * run + core * mine_rows + r) * DEGREE
        total = None
        for k in range(DEGREE):
            sender = table[pl.ds(sender_ref[first + k], tiles, stride=table_rows), :]
            term = half_silu(base + sender)
            total = term if total is None else total + term
        agg[q % 2][pl.ds(r, tiles, stride=agg_rows), :] = total

    def out_rows(q):
        return pl.ds(pl.multiple_of(q * run + core * mine_rows, mine_rows), mine_rows)

    def out_send(q):
        return pltpu.make_async_remote_copy(
            src_ref=out_buf.at[q],
            dst_ref=out_ref.at[out_rows(q)],
            send_sem=out_send_sem.at[q],
            recv_sem=out_in_sem.at[q],
            device_id=partner,
            device_id_type=MESH,
        )

    def finish(q, r, some, between=None):
        def scaled(side, t):
            value = agg[q % 2][pl.ds((side * (tiles // 2) + t) * agg_rows + r, some), :]
            return value * vectors[1, side, :, tile(t)]

        values = [(side, t, scaled(side, t)) for side in (other, core) for t in range(tiles // 2)]
        square = values[0][2] * values[0][2]
        for _, _, value in values[1:]:
            square = square + value * value
        mean = jnp.sum(square, axis=1, keepdims=True) / (2 * width)
        factor = lax.rsqrt(mean + 1e-05)
        span = pl.ds(pl.multiple_of(r, unroll), some)
        start = pl.multiple_of(q * run + core * mine_rows + r, unroll)
        for n, (side, t, value) in enumerate(values):
            if n == tiles // 2 and between is not None:
                between()
            held = latent_in[q, span, tile(t)] if side is other else latent[q, core, span, tile(t)]
            normed = value * factor * vectors[2, side, :, tile(t)]
            result = (held.astype(F32) + normed).astype(BF16)
            if side is other:
                out_buf[q, span, tile(t)] = result
            else:
                out_ref[pl.ds(start, some), tile(t)] = result

    for q in range(PARTS):

        def some_nodes(m, carry):
            for u in range(unroll):
                one_node(q, m * unroll + u)
            if q > 0:
                finish(q - 1, m * unroll, unroll)
            return carry

        lax.fori_loop(0, mine_rows // unroll, some_nodes, 0)
        if q > 0:
            out_send(q - 1).start()
    finish(PARTS - 1, 0, mine_rows, lambda: out_send(PARTS - 1).start())

    def drain_side(d):
        for half in range(2):
            share(group_of(*d), half, core).wait_send()

    for d in sides:
        when(goes(d), lambda: halo_copy(1 - early[d], d).wait_send())
        when(comes(d), lambda: drain_side(d))
    for t in first_turns:
        when(comes_corner(*t), lambda: share(*corner_of(*t), core).wait_send())
    for cut in range(2):
        for t in second_turns:
            when(goes_corner(*t), lambda: corner_copy(*t, cut).wait_send())
            when(comes_corner(*t), lambda: share(*corner_of(*t), core, cut).wait_send())
    for q in range(PARTS):
        out_send(q).wait()


def local(
    obs_features,
    obs_owner,
    obs_node,
    obs_count,
    edge_senders,
    obs_in_w,
    obs_in_b,
    obs_out_w,
    enc_w,
    enc_b,
    node_base,
    recv_w,
    send_w,
    edge_b,
    channel_scale,
    norm_gain,
):
    bands = lax.axis_size("band")
    sectors = lax.axis_size("sector")
    geo = bands * sectors
    pairs = geo // 2
    rows, embed = obs_features.shape
    node_rows, width = node_base.shape
    tiles = 2 * width // LANES
    run = node_rows // PARTS
    mine_rows = run // 2
    piece = mine_rows // 2
    slots = geo * SLOTS
    vmem = pl.BlockSpec(memory_space=pltpu.VMEM)
    smem = pl.BlockSpec(memory_space=pltpu.SMEM)
    hbm = pl.BlockSpec(memory_space=pl.ANY)
    dma = pltpu.SemaphoreType.DMA
    return pl.pallas_call(
        functools.partial(kernel, bands, sectors),
        out_shape=pltpu.VMEM((node_rows, width), BF16),
        in_specs=[smem] + [hbm] * 15,
        out_specs=vmem,
        scratch_shapes=[
            pltpu.VMEM((1, rows), jnp.int32),
            pltpu.VMEM((1, rows), jnp.int32),
            pltpu.SMEM((node_rows * DEGREE,), jnp.int32),
            pltpu.VMEM((1, embed), F32),
            pltpu.VMEM((1, width), F32),
            pltpu.VMEM((rows, embed), BF16),
            pltpu.VMEM((embed, embed), BF16),
            pltpu.VMEM((embed, embed), BF16),
            pltpu.VMEM((embed, width), BF16),
            pltpu.VMEM((3, 2, 1, width), F32),
            pltpu.VMEM((2, pairs // GROUP, LANES), jnp.int32),
            pltpu.VMEM((run, width), F32),
            pltpu.VMEM((run, LANES), F32),
            pltpu.VMEM((pairs, SLOTS, embed), BF16),
            pltpu.VMEM((2, pairs, SLOTS, embed), BF16),
            pltpu.VMEM((slots, width), BF16),
            pltpu.VMEM((node_rows, width), BF16),
            pltpu.VMEM((2, width, 2 * width), BF16),
            pltpu.VMEM((2, width, 2 * width), BF16),
            pltpu.VMEM((run, slots), BF16),
            pltpu.VMEM((PARTS, 2, mine_rows, width), BF16),
            pltpu.VMEM((PARTS, mine_rows, width), BF16),
            pltpu.VMEM((tiles * (node_rows + 9 * run + SKEW), LANES), F32),
            pltpu.VMEM((tiles * (PARTS * mine_rows + SKEW), LANES), F32),
            pltpu.VMEM((PARTS, 2, tiles, piece, LANES), BF16),
            pltpu.VMEM((PARTS, 2, tiles, piece, LANES), BF16),
            pltpu.VMEM((9, 2, 2, tiles, piece, LANES), BF16),
            pltpu.VMEM((tiles * (mine_rows + SKEW), LANES), F32),
            pltpu.VMEM((tiles * (mine_rows + SKEW), LANES), F32),
            pltpu.VMEM((PARTS, mine_rows, width), BF16),
            dma((15,)),
            dma((5,)),
            dma((5,)),
            dma((STEPS,)),
            dma((STEPS,)),
            dma((STEPS,)),
            dma((STEPS,)),
            dma((PARTS,)),
            dma((PARTS,)),
            dma((PARTS,)),
            dma((PARTS,)),
            dma((24,)),
            dma((24,)),
            dma((36,)),
            dma((36,)),
            dma((PARTS,)),
            dma((PARTS,)),
        ],
        compiler_params=pltpu.CompilerParams(
            collective_id=0, has_side_effects=True, vmem_limit_bytes=56 * 2**20
        ),
        name="encode_and_pass",
    )(
        obs_count,
        obs_owner.reshape(1, rows),
        obs_node.reshape(1, rows),
        edge_senders,
        obs_in_b.reshape(1, -1),
        enc_b.reshape(1, -1),
        edge_b.reshape(1, -1),
        channel_scale.reshape(1, -1),
        norm_gain.reshape(1, -1),
        obs_features,
        obs_in_w,
        obs_out_w,
        enc_w,
        node_base,
        recv_w,
        send_w,
    )


def solution(mesh):
    in_specs = (
        P(("band", "sector"), None),
        P(("band", "sector"), None),
        P(("band", "sector")),
        P(("band", "sector")),
        P(("band", "sector")),
        P(),
        P(),
        P(),
        P(None, "chan"),
        P("chan"),
        P(("band", "sector"), "chan"),
        P("chan", None),
        P("chan", None),
        P("chan"),
        P("chan"),
        P("chan"),
    )
    out_specs = P(("band", "sector"), "chan")
    return jax.shard_map(local, mesh=mesh, in_specs=in_specs, out_specs=out_specs, check_vma=False)
```

```python
import functools

import jax
import jax.numpy as jnp
from jax import lax
from jax.experimental import pallas as pl
from jax.experimental.pallas import tpu as pltpu
from jax.sharding import PartitionSpec as P

PIECES = 8
DEGREE = 6
SLOTS = 16
ID_ROW = 12
GROUP = 8
LANES = 128
LOW = 64
SKEW = 4
PARTS = 4
STEPS = 4
SIDE = 4
ORDER = (2, 1, 3, 0)
MESH = pl.DeviceIdType.MESH
F32 = jnp.float32
BF16 = jnp.bfloat16


def dot(a, b):
    return jnp.dot(a, b, preferred_element_type=F32)


def iota(shape, axis):
    return lax.broadcasted_iota(jnp.int32, shape, axis)


def half_silu(h):
    return h + h * jnp.tanh(h)


def kernel(
    bands,
    sectors,
    count_ref,
    owner_hbm,
    node_hbm,
    sender_hbm,
    in_b_hbm,
    enc_b_hbm,
    edge_b_hbm,
    scale_hbm,
    gain_hbm,
    obs_hbm,
    in_w_hbm,
    out_w_hbm,
    enc_w_hbm,
    base_hbm,
    recv_hbm,
    send_hbm,
    out_ref,
    owner_ref,
    node_ref,
    sender_ref,
    in_b_ref,
    enc_b_ref,
    obs_ref,
    in_w_ref,
    out_w_ref,
    enc_w_ref,
    vectors,
    slot_ids,
    rim_sum,
    rim_count,
    send_buf,
    arrived,
    message,
    node_base,
    recv_w,
    send_w,
    picks,
    latent,
    latent_in,
    table,
    recv_base,
    sent,
    sent_in,
    halo,
    agg_even,
    agg_odd,
    out_buf,
    local_sem,
    weight_sem,
    weight_in_sem,
    send_sem,
    arrive_sem,
    pass_sem,
    pass_in_sem,
    latent_sem,
    latent_in_sem,
    sent_sem,
    sent_in_sem,
    halo_sem,
    halo_in_sem,
    share_sem,
    share_in_sem,
    out_send_sem,
    out_in_sem,
):
    band = lax.axis_index("band")
    sector = lax.axis_index("sector")
    core = lax.axis_index("chan")
    other = 1 - core
    geo = bands * sectors
    pairs = geo // 2
    partner = (band, sector, other)
    rows = obs_ref.shape[0]
    node_rows, width = node_base.shape
    tiles = 2 * width // LANES
    run = node_rows // PARTS
    mine_rows = run // 2
    piece = mine_rows // 2
    table_rows = table.shape[0] // tiles
    base_rows = recv_base.shape[0] // tiles
    groups = geo // GROUP
    per_step = pairs // STEPS

    def local_copy(n, source, target):
        return pltpu.make_async_copy(source, target, local_sem.at[n])

    first_copies = [
        local_copy(0, obs_hbm, obs_ref),
        local_copy(1, in_w_hbm, in_w_ref),
        local_copy(2, out_w_hbm, out_w_ref),
        local_copy(7, owner_hbm, owner_ref),
        local_copy(8, node_hbm, node_ref),
        local_copy(9, in_b_hbm, in_b_ref),
    ]
    sender_copy = local_copy(10, sender_hbm, sender_ref)
    enc_copies = [local_copy(3, enc_w_hbm, enc_w_ref), local_copy(11, enc_b_hbm, enc_b_ref)]
    vector_copies = [
        local_copy(12 + n, ref, vectors.at[n, core])
        for n, ref in enumerate((edge_b_hbm, scale_hbm, gain_hbm))
    ]
    base_copy = local_copy(4, base_hbm, node_base)
    send_w_copy = local_copy(5, send_hbm, send_w.at[core])
    recv_w_copy = local_copy(6, recv_hbm, recv_w.at[core])
    for copy in first_copies:
        copy.start()

    sides = [(0, 1), (1, 0), (0, -1), (-1, 0)]

    def neighbour(i, j):
        return (
            lax.rem(band + (i + bands), bands),
            lax.rem(sector + (j + sectors), sectors),
            core,
        )

    row, column = lax.div(band, SIDE), lax.rem(band, SIDE)
    to_row = [lax.rem(row + n, SIDE) * SIDE for n in range(SIDE)]
    to_column = [lax.rem(column + n, SIDE) for n in range(SIDE)]
    to_sector = [lax.rem(sector + (2 * n + core), sectors) for n in range(SIDE)]

    def target_of(k):
        n, i, j = ORDER[k // SIDE**2], ORDER[k // SIDE % SIDE], ORDER[k % SIDE]
        return to_row[i] + to_column[j], to_sector[n], core

    barrier = pltpu.get_barrier_semaphore()

    def greet(device):
        pl.semaphore_signal(barrier, inc=1, device_id=device, device_id_type=MESH)

    for k in range(pairs - 1):
        greet(target_of(k))

    @pl.when(core == 1)
    def _():
        greet(target_of(pairs - 1))

    greet(partner)
    for d in sides:
        greet(neighbour(*d))

    for copy in first_copies:
        copy.wait()
    for copy in enc_copies + [base_copy, send_w_copy, recv_w_copy, sender_copy] + vector_copies:
        copy.start()
    obs = obs_ref[...]
    hidden = half_silu(0.5 * (dot(obs, in_w_ref[...]) + in_b_ref[...])).astype(BF16)
    embedded = (obs.astype(F32) + dot(hidden, out_w_ref[...])).astype(BF16)
    owner = owner_ref[...]
    node = node_ref[...]
    live = iota((1, rows), 1) < count_ref[0] * (rows // PIECES)
    same = (owner == iota((geo, rows), 0)).astype(F32)
    span = rows // 4
    upto = (iota((span, span), 0) <= iota((span, span), 1)).astype(F32).astype(BF16)
    before = jnp.zeros((geo, 1), F32)
    ranks = []
    for n in range(4):
        some = same[:, n * span : (n + 1) * span]
        rank = dot(some.astype(BF16), upto) + before
        before = rank[:, span - 1 :]
        ranks.append(jnp.sum(rank * some, axis=0, keepdims=True))
    position = jnp.concatenate(ranks, axis=1).astype(jnp.int32) - 1
    further = (owner % sectors - sector + sectors) % sectors
    valid = jnp.logical_and(live, further % 2 == core)
    owner_band = owner // sectors

    def place_of(distance):
        return jnp.where(
            distance == 2, 0, jnp.where(distance == 1, 1, jnp.where(distance == 3, 2, 3))
        )

    step = (
        place_of(further // 2) * SIDE**2
        + place_of((owner_band // SIDE - row + SIDE) % SIDE) * SIDE
        + place_of((owner_band % SIDE - column + SIDE) % SIDE)
    )
    slot = jnp.where(valid, step * SLOTS + position, -1)
    lane = SLOTS * (step % GROUP) + position
    high = iota((2 * LANES, rows), 0) == lane
    low = iota((2 * LANES, rows), 0) == lane + LANES
    ids = jnp.where(
        high,
        (node // LOW + 1).astype(F32),
        jnp.where(low, (node % LOW).astype(F32), 0.0),
    ).astype(BF16)
    mine = (iota((pairs, rows), 0) == jnp.where(valid, step, -1)).astype(F32).astype(BF16)
    id_rows = lax.dot_general(
        mine, ids, (((1,), (1,)), ((), ())), preferred_element_type=F32
    ).astype(BF16)

    def block_copy(k):
        return pltpu.make_async_remote_copy(
            src_ref=send_buf.at[k],
            dst_ref=arrived.at[core, k],
            send_sem=send_sem.at[k // per_step],
            recv_sem=arrive_sem.at[k // per_step],
            device_id=target_of(k),
            device_id_type=MESH,
        )

    def pack(g):
        first = g * per_step * SLOTS
        count = per_step * SLOTS
        place = (slot == first + iota((count, rows), 0)).astype(F32).astype(BF16)
        spread = first + iota((count, pairs), 0) == iota((count, pairs), 1) * SLOTS + ID_ROW
        block = dot(place, embedded) + dot(spread.astype(F32).astype(BF16), id_rows)
        send_buf[pl.ds(g * per_step, per_step)] = block.astype(BF16).reshape(per_step, SLOTS, -1)

    def send(g):
        for k in range(g * per_step, (g + 1) * per_step):
            if k < pairs - 1:
                block_copy(k).start()
                continue

            @pl.when(core == 1)
            def _():
                block_copy(k).start()

            @pl.when(core == 0)
            def _():
                pltpu.make_async_copy(
                    send_buf.at[k], arrived.at[core, k], arrive_sem.at[k // per_step]
                ).start()

    for g in range(STEPS):
        pack(g)
    pl.semaphore_wait(barrier, pairs - 1 + core + len(sides) + 1)
    for g in range(STEPS):
        send(g)

    def weight_copy(n, source, target):
        return pltpu.make_async_remote_copy(
            src_ref=source,
            dst_ref=target,
            send_sem=weight_sem.at[n],
            recv_sem=weight_in_sem.at[n],
            device_id=partner,
            device_id_type=MESH,
        )

    weights = [
        weight_copy(0, send_hbm, send_w.at[core]),
        weight_copy(1, recv_hbm, recv_w.at[core]),
    ] + [
        weight_copy(2 + n, ref, vectors.at[n, core])
        for n, ref in enumerate((edge_b_hbm, scale_hbm, gain_hbm))
    ]
    for copy in weights:
        copy.start()

    def blocks_of(g):
        return pl.ds(g * per_step, per_step)

    def pass_on(g, side):
        block = arrived.at[side, blocks_of(g)]
        return pltpu.make_async_remote_copy(
            src_ref=block,
            dst_ref=block,
            send_sem=pass_sem.at[g],
            recv_sem=pass_in_sem.at[g],
            device_id=partner,
            device_id_type=MESH,
        )

    def group_wait(g, less=0):
        span = pl.ds(g * per_step, per_step - less)
        return pltpu.make_async_remote_copy(
            src_ref=send_buf.at[span],
            dst_ref=arrived.at[core, span],
            send_sem=send_sem.at[g],
            recv_sem=arrive_sem.at[g],
            device_id=partner,
            device_id_type=MESH,
        )

    count = pairs * SLOTS
    id_groups = pairs // GROUP
    at = iota((id_groups, count), 1)
    chosen = jnp.logical_and(
        at // (GROUP * SLOTS) == iota((id_groups, count), 0), at % SLOTS == ID_ROW
    )
    chosen = chosen.astype(F32).astype(BF16)

    def hits(q, names):
        return (iota((run, LANES), 0) + q * run == names).astype(F32)

    def take(side):
        block = arrived[side].reshape(count, -1)
        content = half_silu(0.5 * (dot(block, enc_w_ref[...]) + enc_b_ref[...])).astype(BF16)
        message[pl.ds(pl.multiple_of(side * count, count), count), :] = content
        found = dot(chosen, block)
        names = ((found[:, :LANES] - 1.0) * LOW + found[:, LANES:]).astype(jnp.int32)
        slot_ids[side] = names
        some = [hits(0, names[n : n + 1, :]) for n in range(id_groups)]
        value = dot(jnp.concatenate(some, axis=1).astype(BF16), content)
        return value, sum(some[1:], some[0])

    for copy in enc_copies:
        copy.wait()
    for g in range(STEPS):
        group_wait(g).wait_recv()
        pass_on(g, core).start()
    rim_sum[...], rim_count[...] = take(core)
    for g in range(STEPS):
        pass_on(g, other).wait_recv()
    rim_rest, rim_more = take(other)

    def latent_copy(q):
        return pltpu.make_async_remote_copy(
            src_ref=latent.at[q, other],
            dst_ref=latent_in.at[q],
            send_sem=latent_sem.at[q],
            recv_sem=latent_in_sem.at[q],
            device_id=partner,
            device_id_type=MESH,
        )

    def end_latent(q, total, number):
        scale = 1.0 / jnp.maximum(jnp.sum(number, axis=1, keepdims=True), 1.0)
        base = node_base[pl.ds(pl.multiple_of(q * run, run), run), :].astype(F32)
        latent[q] = (base + total * scale).astype(BF16).reshape(2, mine_rows, width)
        latent_copy(q).start()

    def make_latent(q):
        number = jnp.zeros((run, LANES), F32)
        for g in range(groups):
            n = g % id_groups
            hit = hits(q, slot_ids[g // id_groups, n : n + 1, :])
            number = number + hit
            picks[:, g * LANES : (g + 1) * LANES] = hit.astype(BF16)
        end_latent(q, dot(picks[...], message[...]), number)

    def project(q, weight, arrival=None):
        own = dot(latent[q, core], weight[core])
        if arrival is not None:
            arrival()
        return own + dot(latent_in[q], weight[other])

    def tile(t):
        return slice(t * LANES, (t + 1) * LANES)

    def sent_copy(q):
        return pltpu.make_async_remote_copy(
            src_ref=sent.at[q],
            dst_ref=sent_in.at[q],
            send_sem=sent_sem.at[q],
            recv_sem=sent_in_sem.at[q],
            device_id=partner,
            device_id_type=MESH,
        )

    def project_send(q, arrival=None):
        value = (0.5 * project(q, send_w, arrival)).astype(BF16)
        wide = value.astype(F32)
        for t in range(tiles):
            for h in range(2):
                sent[q, h, t] = value[h * piece : (h + 1) * piece, tile(t)]
            table[pl.ds(t * table_rows + q * run + core * mine_rows, mine_rows), :] = wide[
                :, tile(t)
            ]
        sent_copy(q).start()

    def project_recv(q):
        value = project(q, recv_w).astype(BF16).astype(F32)
        for t in range(tiles):
            bias = vectors[0, t // (tiles // 2), :, tile(t % (tiles // 2))]
            recv_base[pl.ds(t * base_rows + q * mine_rows, mine_rows), :] = 0.5 * (
                value[:, tile(t)] + bias
            )

    def widen(first, source):
        for t in range(tiles):
            table[pl.ds(t * table_rows + first, source.shape[1]), :] = source[t].astype(F32)

    def first_arrival():
        weights[0].wait_recv()
        latent_copy(0).wait_recv()

    base_copy.wait()
    end_latent(0, rim_sum[...] + rim_rest, rim_count[...] + rim_more)
    send_w_copy.wait()
    project_send(0, first_arrival)

    turns = [(d, e) for d in sides for e in sides if (d[0] == 0) != (e[0] == 0)]

    def group_of(i, j):
        return (1 - i) * 3 + 1 - j

    def halo_copy(half, d):
        n = half * 4 + sides.index(d)
        return pltpu.make_async_remote_copy(
            src_ref=sent.at[0, half],
            dst_ref=halo.at[group_of(*d), core, half],
            send_sem=halo_sem.at[n],
            recv_sem=halo_in_sem.at[n],
            device_id=neighbour(*d),
            device_id_type=MESH,
        )

    split = piece * 3 // 5
    cuts = {None: pl.ds(0, piece), 0: pl.ds(0, split), 1: pl.ds(split, piece - split)}

    def corner_copy(d, e, cut=None):
        half = 0 if d[0] == 0 else 1
        n = 8 + turns.index((d, e)) + (8 if cut == 1 else 0)
        return pltpu.make_async_remote_copy(
            src_ref=halo.at[group_of(*d), core, half, :, cuts[cut]],
            dst_ref=halo.at[group_of(d[0] + e[0], d[1] + e[1]), core, half, :, cuts[cut]],
            send_sem=halo_sem.at[n],
            recv_sem=halo_in_sem.at[n],
            device_id=neighbour(*e),
            device_id_type=MESH,
        )

    def share(group, half, side, cut=None):
        block = halo.at[group, side, half, :, cuts[cut]]
        n = group * 2 + half + (18 if cut == 1 else 0)
        return pltpu.make_async_remote_copy(
            src_ref=block,
            dst_ref=block,
            send_sem=share_sem.at[n],
            recv_sem=share_in_sem.at[n],
            device_id=partner,
            device_id_type=MESH,
        )

    def widen_halo(group, half, side, cut=None):
        first = node_rows + group * run + half * piece + side * mine_rows
        widen(first + (split if cut == 1 else 0), halo.at[group, side, half, :, cuts[cut]])

    early = {d: 0 if d[0] == 0 else 1 for d in sides}
    first_turns, second_turns = turns[: len(sides)], turns[len(sides) :]

    def corner_of(d, e):
        return group_of(d[0] + e[0], d[1] + e[1]), early[d]

    def comes(d):
        return {1: band > 0, 0: None, -1: band < bands - 1}[d[0]]

    def goes(d):
        return comes((-d[0], 0))

    def when(condition, act):
        if condition is None:
            act()
        else:
            pl.when(condition)(act)

    def comes_corner(d, e):
        return comes((d[0] + e[0], 0))

    def goes_corner(d, e):
        return comes(d) if d[0] else goes(e)

    for d in sides:
        when(goes(d), lambda: halo_copy(early[d], d).start())

    make_latent(1)
    for d in sides:

        def second_half():
            halo_copy(early[d], d).wait_send()
            halo_copy(1 - early[d], d).start()

        when(goes(d), second_half)
    for d in sides:
        when(comes(d), lambda: halo_copy(early[d], d).wait_recv())
        for t in first_turns:
            if t[0] == d:
                when(goes_corner(*t), lambda: corner_copy(*t).start())
    for d in sides:
        when(comes(d), lambda: share(group_of(*d), early[d], core).start())

    for cut in range(2):
        for t in second_turns:
            when(goes_corner(*t), lambda: corner_copy(*t, cut).start())

    def later_latent(q, carry):
        make_latent(q)
        return carry

    lax.fori_loop(2, PARTS, later_latent, 0)
    for copy in [recv_w_copy, sender_copy] + vector_copies:
        copy.wait()
    for copy in weights[1:]:
        copy.wait_recv()
    project_recv(0)

    def later_project(q, carry):
        latent_copy(q).wait_recv()
        project_send(q)
        project_recv(q)
        return carry

    lax.fori_loop(1, PARTS, later_project, 0)
    for t in first_turns:
        when(goes_corner(*t), lambda: corner_copy(*t).wait_send())

    def widen_sent(q, carry):
        sent_copy(q).wait_recv()
        for h in range(2):
            widen(q * run + h * piece + other * mine_rows, sent_in.at[q, h])
        return carry

    lax.fori_loop(0, PARTS, widen_sent, 0)

    def widen_both(group, half):
        widen_halo(group, half, core)
        share(group, half, other).wait_recv()
        widen_halo(group, half, other)

    for d in sides:
        when(comes(d), lambda: widen_both(group_of(*d), early[d]))

    @pl.when(core == 0)
    def _():
        group_wait(STEPS - 1, 1).wait_send()

    @pl.when(core == 1)
    def _():
        group_wait(STEPS - 1).wait_send()

    for g in range(STEPS - 1):
        group_wait(g).wait_send()
    for g in range(STEPS):
        pass_on(g, core).wait_send()
    for copy in weights:
        copy.wait_send()
    for q in range(PARTS):
        latent_copy(q).wait_send()
        sent_copy(q).wait_send()

    for d in sides:

        def second_arrival():
            halo_copy(1 - early[d], d).wait_recv()
            share(group_of(*d), 1 - early[d], core).start()

        when(comes(d), second_arrival)

    def corner_arrival(t, cut=None):
        corner_copy(*t, cut).wait_recv()
        share(*corner_of(*t), core, cut).start()

    for t in first_turns:
        when(comes_corner(*t), lambda: corner_arrival(t))
    for d in sides:
        when(comes(d), lambda: widen_both(group_of(*d), 1 - early[d]))
    for t in first_turns:
        when(comes_corner(*t), lambda: widen_both(*corner_of(*t)))
    for cut in range(2):
        for t in second_turns:
            when(comes_corner(*t), lambda: corner_arrival(t, cut))
        for t in second_turns:
            when(comes_corner(*t), lambda: widen_halo(*corner_of(*t), core, cut))

    def widen_shared(t, cut):
        share(*corner_of(*t), other, cut).wait_recv()
        widen_halo(*corner_of(*t), other, cut)

    for cut in range(2):
        for t in second_turns:
            when(comes_corner(*t), lambda: widen_shared(t, cut))

    unroll = 32
    agg = (agg_even, agg_odd)

    agg_rows = agg[0].shape[0] // tiles

    def one_node(q, r):
        base = recv_base[pl.ds(q * mine_rows + r, tiles, stride=base_rows), :]
        first = (q * run + core * mine_rows + r) * DEGREE
        total = None
        for k in range(DEGREE):
            sender = table[pl.ds(sender_ref[first + k], tiles, stride=table_rows), :]
            term = half_silu(base + sender)
            total = term if total is None else total + term
        agg[q % 2][pl.ds(r, tiles, stride=agg_rows), :] = total

    def out_rows(q):
        return pl.ds(pl.multiple_of(q * run + core * mine_rows, mine_rows), mine_rows)

    def out_send(q):
        return pltpu.make_async_remote_copy(
            src_ref=out_buf.at[q],
            dst_ref=out_ref.at[out_rows(q)],
            send_sem=out_send_sem.at[q],
            recv_sem=out_in_sem.at[q],
            device_id=partner,
            device_id_type=MESH,
        )

    def finish(q, r, some, between=None):
        def scaled(side, t):
            value = agg[q % 2][pl.ds((side * (tiles // 2) + t) * agg_rows + r, some), :]
            return value * vectors[1, side, :, tile(t)]

        values = [(side, t, scaled(side, t)) for side in (other, core) for t in range(tiles // 2)]
        square = values[0][2] * values[0][2]
        for _, _, value in values[1:]:
            square = square + value * value
        mean = jnp.sum(square, axis=1, keepdims=True) / (2 * width)
        factor = lax.rsqrt(mean + 1e-05)
        span = pl.ds(pl.multiple_of(r, unroll), some)
        start = pl.multiple_of(q * run + core * mine_rows + r, unroll)
        for n, (side, t, value) in enumerate(values):
            if n == tiles // 2 and between is not None:
                between()
            held = latent_in[q, span, tile(t)] if side is other else latent[q, core, span, tile(t)]
            normed = value * factor * vectors[2, side, :, tile(t)]
            result = (held.astype(F32) + normed).astype(BF16)
            if side is other:
                out_buf[q, span, tile(t)] = result
            else:
                out_ref[pl.ds(start, some), tile(t)] = result

    for q in range(PARTS):

        def some_nodes(m, carry):
            for u in range(unroll):
                one_node(q, m * unroll + u)
            if q > 0:
                finish(q - 1, m * unroll, unroll)
            return carry

        lax.fori_loop(0, mine_rows // unroll, some_nodes, 0)
        if q > 0:
            out_send(q - 1).start()
    finish(PARTS - 1, 0, mine_rows, lambda: out_send(PARTS - 1).start())

    def drain_side(d):
        for half in range(2):
            share(group_of(*d), half, core).wait_send()

    for d in sides:
        when(goes(d), lambda: halo_copy(1 - early[d], d).wait_send())
        when(comes(d), lambda: drain_side(d))
    for t in first_turns:
        when(comes_corner(*t), lambda: share(*corner_of(*t), core).wait_send())
    for cut in range(2):
        for t in second_turns:
            when(goes_corner(*t), lambda: corner_copy(*t, cut).wait_send())
            when(comes_corner(*t), lambda: share(*corner_of(*t), core, cut).wait_send())
    for q in range(PARTS):
        out_send(q).wait()


def local(
    obs_features,
    obs_owner,
    obs_node,
    obs_count,
    edge_senders,
    obs_in_w,
    obs_in_b,
    obs_out_w,
    enc_w,
    enc_b,
    node_base,
    recv_w,
    send_w,
    edge_b,
    channel_scale,
    norm_gain,
):
    bands = lax.axis_size("band")
    sectors = lax.axis_size("sector")
    geo = bands * sectors
    pairs = geo // 2
    rows, embed = obs_features.shape
    node_rows, width = node_base.shape
    tiles = 2 * width // LANES
    run = node_rows // PARTS
    mine_rows = run // 2
    piece = mine_rows // 2
    slots = geo * SLOTS
    vmem = pl.BlockSpec(memory_space=pltpu.VMEM)
    smem = pl.BlockSpec(memory_space=pltpu.SMEM)
    hbm = pl.BlockSpec(memory_space=pl.ANY)
    dma = pltpu.SemaphoreType.DMA
    return pl.pallas_call(
        functools.partial(kernel, bands, sectors),
        out_shape=pltpu.VMEM((node_rows, width), BF16),
        in_specs=[smem] + [hbm] * 15,
        out_specs=vmem,
        scratch_shapes=[
            pltpu.VMEM((1, rows), jnp.int32),
            pltpu.VMEM((1, rows), jnp.int32),
            pltpu.SMEM((node_rows * DEGREE,), jnp.int32),
            pltpu.VMEM((1, embed), F32),
            pltpu.VMEM((1, width), F32),
            pltpu.VMEM((rows, embed), BF16),
            pltpu.VMEM((embed, embed), BF16),
            pltpu.VMEM((embed, embed), BF16),
            pltpu.VMEM((embed, width), BF16),
            pltpu.VMEM((3, 2, 1, width), F32),
            pltpu.VMEM((2, pairs // GROUP, LANES), jnp.int32),
            pltpu.VMEM((run, width), F32),
            pltpu.VMEM((run, LANES), F32),
            pltpu.VMEM((pairs, SLOTS, embed), BF16),
            pltpu.VMEM((2, pairs, SLOTS, embed), BF16),
            pltpu.VMEM((slots, width), BF16),
            pltpu.VMEM((node_rows, width), BF16),
            pltpu.VMEM((2, width, 2 * width), BF16),
            pltpu.VMEM((2, width, 2 * width), BF16),
            pltpu.VMEM((run, slots), BF16),
            pltpu.VMEM((PARTS, 2, mine_rows, width), BF16),
            pltpu.VMEM((PARTS, mine_rows, width), BF16),
            pltpu.VMEM((tiles * (node_rows + 9 * run + SKEW), LANES), F32),
            pltpu.VMEM((tiles * (PARTS * mine_rows + SKEW), LANES), F32),
            pltpu.VMEM((PARTS, 2, tiles, piece, LANES), BF16),
            pltpu.VMEM((PARTS, 2, tiles, piece, LANES), BF16),
            pltpu.VMEM((9, 2, 2, tiles, piece, LANES), BF16),
            pltpu.VMEM((tiles * (mine_rows + SKEW), LANES), F32),
            pltpu.VMEM((tiles * (mine_rows + SKEW), LANES), F32),
            pltpu.VMEM((PARTS, mine_rows, width), BF16),
            dma((15,)),
            dma((5,)),
            dma((5,)),
            dma((STEPS,)),
            dma((STEPS,)),
            dma((STEPS,)),
            dma((STEPS,)),
            dma((PARTS,)),
            dma((PARTS,)),
            dma((PARTS,)),
            dma((PARTS,)),
            dma((24,)),
            dma((24,)),
            dma((36,)),
            dma((36,)),
            dma((PARTS,)),
            dma((PARTS,)),
        ],
        compiler_params=pltpu.CompilerParams(
            collective_id=0, has_side_effects=True, vmem_limit_bytes=56 * 2**20
        ),
        name="encode_and_pass",
    )(
        obs_count,
        obs_owner.reshape(1, rows),
        obs_node.reshape(1, rows),
        edge_senders,
        obs_in_b.reshape(1, -1),
        enc_b.reshape(1, -1),
        edge_b.reshape(1, -1),
        channel_scale.reshape(1, -1),
        norm_gain.reshape(1, -1),
        obs_features,
        obs_in_w,
        obs_out_w,
        enc_w,
        node_base,
        recv_w,
        send_w,
    )


def solution(mesh):
    in_specs = (
        P(("band", "sector"), None),
        P(("band", "sector"), None),
        P(("band", "sector")),
        P(("band", "sector")),
        P(("band", "sector")),
        P(),
        P(),
        P(),
        P(None, "chan"),
        P("chan"),
        P(("band", "sector"), "chan"),
        P("chan", None),
        P("chan", None),
        P("chan"),
        P("chan"),
        P("chan"),
    )
    out_specs = P(("band", "sector"), "chan")
    return jax.shard_map(local, mesh=mesh, in_specs=in_specs, out_specs=out_specs, check_vma=False)
```

```python
import functools

import jax
import jax.numpy as jnp
from jax import lax
from jax.experimental import pallas as pl
from jax.experimental.pallas import tpu as pltpu
from jax.sharding import PartitionSpec as P

PIECES = 8
DEGREE = 6
SLOTS = 16
ID_ROW = 12
GROUP = 8
LANES = 128
LOW = 64
SKEW = 4
PARTS = 4
STEPS = 4
SIDE = 4
ORDER = (2, 1, 3, 0)
MESH = pl.DeviceIdType.MESH
F32 = jnp.float32
BF16 = jnp.bfloat16


def dot(a, b):
    return jnp.dot(a, b, preferred_element_type=F32)


def iota(shape, axis):
    return lax.broadcasted_iota(jnp.int32, shape, axis)


def half_silu(h):
    return h + h * jnp.tanh(h)


def kernel(
    bands,
    sectors,
    count_ref,
    owner_hbm,
    node_hbm,
    sender_hbm,
    in_b_hbm,
    enc_b_hbm,
    edge_b_hbm,
    scale_hbm,
    gain_hbm,
    obs_hbm,
    in_w_hbm,
    out_w_hbm,
    enc_w_hbm,
    base_hbm,
    recv_hbm,
    send_hbm,
    out_ref,
    owner_ref,
    node_ref,
    sender_ref,
    in_b_ref,
    enc_b_ref,
    obs_ref,
    in_w_ref,
    out_w_ref,
    enc_w_ref,
    vectors,
    slot_ids,
    rim_sum,
    rim_count,
    send_buf,
    arrived,
    message,
    node_base,
    recv_w,
    send_w,
    picks,
    latent,
    latent_in,
    table,
    recv_base,
    sent,
    sent_in,
    halo,
    agg_even,
    agg_odd,
    out_buf,
    local_sem,
    weight_sem,
    weight_in_sem,
    send_sem,
    arrive_sem,
    pass_sem,
    pass_in_sem,
    latent_sem,
    latent_in_sem,
    sent_sem,
    sent_in_sem,
    halo_sem,
    halo_in_sem,
    share_sem,
    share_in_sem,
    out_send_sem,
    out_in_sem,
):
    band = lax.axis_index("band")
    sector = lax.axis_index("sector")
    core = lax.axis_index("chan")
    other = 1 - core
    geo = bands * sectors
    pairs = geo // 2
    partner = (band, sector, other)
    rows = obs_ref.shape[0]
    node_rows, width = node_base.shape
    tiles = 2 * width // LANES
    run = node_rows // PARTS
    mine_rows = run // 2
    piece = mine_rows // 2
    table_rows = table.shape[0] // tiles
    base_rows = recv_base.shape[0] // tiles
    groups = geo // GROUP
    per_step = pairs // STEPS

    def local_copy(n, source, target):
        return pltpu.make_async_copy(source, target, local_sem.at[n])

    first_copies = [
        local_copy(0, obs_hbm, obs_ref),
        local_copy(1, in_w_hbm, in_w_ref),
        local_copy(2, out_w_hbm, out_w_ref),
        local_copy(7, owner_hbm, owner_ref),
        local_copy(8, node_hbm, node_ref),
        local_copy(9, in_b_hbm, in_b_ref),
    ]
    sender_copy = local_copy(10, sender_hbm, sender_ref)
    enc_copies = [local_copy(3, enc_w_hbm, enc_w_ref), local_copy(11, enc_b_hbm, enc_b_ref)]
    vector_copies = [
        local_copy(12 + n, ref, vectors.at[n, core])
        for n, ref in enumerate((edge_b_hbm, scale_hbm, gain_hbm))
    ]
    base_copy = local_copy(4, base_hbm, node_base)
    send_w_copy = local_copy(5, send_hbm, send_w.at[core])
    recv_w_copy = local_copy(6, recv_hbm, recv_w.at[core])
    for copy in first_copies:
        copy.start()

    sides = [(0, 1), (1, 0), (0, -1), (-1, 0)]

    def neighbour(i, j):
        return (
            lax.rem(band + (i + bands), bands),
            lax.rem(sector + (j + sectors), sectors),
            core,
        )

    row, column = lax.div(band, SIDE), lax.rem(band, SIDE)
    to_row = [lax.rem(row + n, SIDE) * SIDE for n in range(SIDE)]
    to_column = [lax.rem(column + n, SIDE) for n in range(SIDE)]
    to_sector = [lax.rem(sector + (2 * n + core), sectors) for n in range(SIDE)]

    def target_of(k):
        n, i, j = ORDER[k // SIDE**2], ORDER[k // SIDE % SIDE], ORDER[k % SIDE]
        return to_row[i] + to_column[j], to_sector[n], core

    barrier = pltpu.get_barrier_semaphore()

    def greet(device):
        pl.semaphore_signal(barrier, inc=1, device_id=device, device_id_type=MESH)

    for k in range(pairs - 1):
        greet(target_of(k))

    @pl.when(core == 1)
    def _():
        greet(target_of(pairs - 1))

    greet(partner)
    for d in sides:
        greet(neighbour(*d))

    for copy in first_copies:
        copy.wait()
    for copy in enc_copies + [base_copy, send_w_copy, recv_w_copy, sender_copy] + vector_copies:
        copy.start()
    obs = obs_ref[...]
    hidden = half_silu(0.5 * (dot(obs, in_w_ref[...]) + in_b_ref[...])).astype(BF16)
    embedded = (obs.astype(F32) + dot(hidden, out_w_ref[...])).astype(BF16)
    owner = owner_ref[...]
    node = node_ref[...]
    live = iota((1, rows), 1) < count_ref[0] * (rows // PIECES)
    same = (owner == iota((geo, rows), 0)).astype(F32)
    span = rows // 4
    upto = (iota((span, span), 0) <= iota((span, span), 1)).astype(F32).astype(BF16)
    before = jnp.zeros((geo, 1), F32)
    ranks = []
    for n in range(4):
        some = same[:, n * span : (n + 1) * span]
        rank = dot(some.astype(BF16), upto) + before
        before = rank[:, span - 1 :]
        ranks.append(jnp.sum(rank * some, axis=0, keepdims=True))
    position = jnp.concatenate(ranks, axis=1).astype(jnp.int32) - 1
    further = (owner % sectors - sector + sectors) % sectors
    valid = jnp.logical_and(live, further % 2 == core)
    owner_band = owner // sectors

    def place_of(distance):
        return jnp.where(
            distance == 2, 0, jnp.where(distance == 1, 1, jnp.where(distance == 3, 2, 3))
        )

    step = (
        place_of(further // 2) * SIDE**2
        + place_of((owner_band // SIDE - row + SIDE) % SIDE) * SIDE
        + place_of((owner_band % SIDE - column + SIDE) % SIDE)
    )
    slot = jnp.where(valid, step * SLOTS + position, -1)
    lane = SLOTS * (step % GROUP) + position
    high = iota((2 * LANES, rows), 0) == lane
    low = iota((2 * LANES, rows), 0) == lane + LANES
    ids = jnp.where(
        high,
        (node // LOW + 1).astype(F32),
        jnp.where(low, (node % LOW).astype(F32), 0.0),
    ).astype(BF16)
    mine = (iota((pairs, rows), 0) == jnp.where(valid, step, -1)).astype(F32).astype(BF16)
    id_rows = lax.dot_general(
        mine, ids, (((1,), (1,)), ((), ())), preferred_element_type=F32
    ).astype(BF16)

    def block_copy(k):
        return pltpu.make_async_remote_copy(
            src_ref=send_buf.at[k],
            dst_ref=arrived.at[core, k],
            send_sem=send_sem.at[k // per_step],
            recv_sem=arrive_sem.at[k // per_step],
            device_id=target_of(k),
            device_id_type=MESH,
        )

    def pack(g):
        first = g * per_step * SLOTS
        count = per_step * SLOTS
        place = (slot == first + iota((count, rows), 0)).astype(F32).astype(BF16)
        spread = first + iota((count, pairs), 0) == iota((count, pairs), 1) * SLOTS + ID_ROW
        block = dot(place, embedded) + dot(spread.astype(F32).astype(BF16), id_rows)
        send_buf[pl.ds(g * per_step, per_step)] = block.astype(BF16).reshape(per_step, SLOTS, -1)

    def send(g):
        for k in range(g * per_step, (g + 1) * per_step):
            if k < pairs - 1:
                block_copy(k).start()
                continue

            @pl.when(core == 1)
            def _():
                block_copy(k).start()

            @pl.when(core == 0)
            def _():
                pltpu.make_async_copy(
                    send_buf.at[k], arrived.at[core, k], arrive_sem.at[k // per_step]
                ).start()

    for g in range(STEPS):
        pack(g)
    pl.semaphore_wait(barrier, pairs - 1 + core + len(sides) + 1)
    for g in range(STEPS):
        send(g)

    def weight_copy(n, source, target):
        return pltpu.make_async_remote_copy(
            src_ref=source,
            dst_ref=target,
            send_sem=weight_sem.at[n],
            recv_sem=weight_in_sem.at[n],
            device_id=partner,
            device_id_type=MESH,
        )

    weights = [
        weight_copy(0, send_hbm, send_w.at[core]),
        weight_copy(1, recv_hbm, recv_w.at[core]),
    ] + [
        weight_copy(2 + n, ref, vectors.at[n, core])
        for n, ref in enumerate((edge_b_hbm, scale_hbm, gain_hbm))
    ]
    for copy in weights:
        copy.start()

    def blocks_of(g):
        return pl.ds(g * per_step, per_step)

    def pass_on(g, side):
        block = arrived.at[side, blocks_of(g)]
        return pltpu.make_async_remote_copy(
            src_ref=block,
            dst_ref=block,
            send_sem=pass_sem.at[g],
            recv_sem=pass_in_sem.at[g],
            device_id=partner,
            device_id_type=MESH,
        )

    def group_wait(g, less=0):
        span = pl.ds(g * per_step, per_step - less)
        return pltpu.make_async_remote_copy(
            src_ref=send_buf.at[span],
            dst_ref=arrived.at[core, span],
            send_sem=send_sem.at[g],
            recv_sem=arrive_sem.at[g],
            device_id=partner,
            device_id_type=MESH,
        )

    count = pairs * SLOTS
    id_groups = pairs // GROUP
    at = iota((id_groups, count), 1)
    chosen = jnp.logical_and(
        at // (GROUP * SLOTS) == iota((id_groups, count), 0), at % SLOTS == ID_ROW
    )
    chosen = chosen.astype(F32).astype(BF16)

    def hits(q, names):
        return (iota((run, LANES), 0) + q * run == names).astype(F32)

    def take(side):
        block = arrived[side].reshape(count, -1)
        content = half_silu(0.5 * (dot(block, enc_w_ref[...]) + enc_b_ref[...])).astype(BF16)
        message[pl.ds(pl.multiple_of(side * count, count), count), :] = content
        found = dot(chosen, block)
        names = ((found[:, :LANES] - 1.0) * LOW + found[:, LANES:]).astype(jnp.int32)
        slot_ids[side] = names
        some = [hits(0, names[n : n + 1, :]) for n in range(id_groups)]
        value = dot(jnp.concatenate(some, axis=1).astype(BF16), content)
        return value, sum(some[1:], some[0])

    for copy in enc_copies:
        copy.wait()
    for g in range(STEPS):
        group_wait(g).wait_recv()
        pass_on(g, core).start()
    rim_sum[...], rim_count[...] = take(core)
    for g in range(STEPS):
        pass_on(g, other).wait_recv()
    rim_rest, rim_more = take(other)

    def latent_copy(q):
        return pltpu.make_async_remote_copy(
            src_ref=latent.at[q, other],
            dst_ref=latent_in.at[q],
            send_sem=latent_sem.at[q],
            recv_sem=latent_in_sem.at[q],
            device_id=partner,
            device_id_type=MESH,
        )

    def end_latent(q, total, number):
        scale = 1.0 / jnp.maximum(jnp.sum(number, axis=1, keepdims=True), 1.0)
        base = node_base[pl.ds(pl.multiple_of(q * run, run), run), :].astype(F32)
        latent[q] = (base + total * scale).astype(BF16).reshape(2, mine_rows, width)
        latent_copy(q).start()

    def make_latent(q):
        number = jnp.zeros((run, LANES), F32)
        for g in range(groups):
            n = g % id_groups
            hit = hits(q, slot_ids[g // id_groups, n : n + 1, :])
            number = number + hit
            picks[:, g * LANES : (g + 1) * LANES] = hit.astype(BF16)
        end_latent(q, dot(picks[...], message[...]), number)

    def project(q, weight, arrival=None):
        own = dot(latent[q, core], weight[core])
        if arrival is not None:
            arrival()
        return own + dot(latent_in[q], weight[other])

    def tile(t):
        return slice(t * LANES, (t + 1) * LANES)

    def sent_copy(q):
        return pltpu.make_async_remote_copy(
            src_ref=sent.at[q],
            dst_ref=sent_in.at[q],
            send_sem=sent_sem.at[q],
            recv_sem=sent_in_sem.at[q],
            device_id=partner,
            device_id_type=MESH,
        )

    def project_send(q, arrival=None):
        value = (0.5 * project(q, send_w, arrival)).astype(BF16)
        wide = value.astype(F32)
        for t in range(tiles):
            for h in range(2):
                sent[q, h, t] = value[h * piece : (h + 1) * piece, tile(t)]
            table[pl.ds(t * table_rows + q * run + core * mine_rows, mine_rows), :] = wide[
                :, tile(t)
            ]
        sent_copy(q).start()

    def project_recv(q):
        value = project(q, recv_w).astype(BF16).astype(F32)
        for t in range(tiles):
            bias = vectors[0, t // (tiles // 2), :, tile(t % (tiles // 2))]
            recv_base[pl.ds(t * base_rows + q * mine_rows, mine_rows), :] = 0.5 * (
                value[:, tile(t)] + bias
            )

    def widen(first, source):
        for t in range(tiles):
            table[pl.ds(t * table_rows + first, source.shape[1]), :] = source[t].astype(F32)

    def first_arrival():
        weights[0].wait_recv()
        latent_copy(0).wait_recv()

    base_copy.wait()
    end_latent(0, rim_sum[...] + rim_rest, rim_count[...] + rim_more)
    send_w_copy.wait()
    project_send(0, first_arrival)

    turns = [(d, e) for d in sides for e in sides if (d[0] == 0) != (e[0] == 0)]

    def group_of(i, j):
        return (1 - i) * 3 + 1 - j

    def halo_copy(half, d):
        n = half * 4 + sides.index(d)
        return pltpu.make_async_remote_copy(
            src_ref=sent.at[0, half],
            dst_ref=halo.at[group_of(*d), core, half],
            send_sem=halo_sem.at[n],
            recv_sem=halo_in_sem.at[n],
            device_id=neighbour(*d),
            device_id_type=MESH,
        )

    split = piece * 3 // 5
    cuts = {None: pl.ds(0, piece), 0: pl.ds(0, split), 1: pl.ds(split, piece - split)}

    def corner_copy(d, e, cut=None):
        half = 0 if d[0] == 0 else 1
        n = 8 + turns.index((d, e)) + (8 if cut == 1 else 0)
        return pltpu.make_async_remote_copy(
            src_ref=halo.at[group_of(*d), core, half, :, cuts[cut]],
            dst_ref=halo.at[group_of(d[0] + e[0], d[1] + e[1]), core, half, :, cuts[cut]],
            send_sem=halo_sem.at[n],
            recv_sem=halo_in_sem.at[n],
            device_id=neighbour(*e),
            device_id_type=MESH,
        )

    def share(group, half, side, cut=None):
        block = halo.at[group, side, half, :, cuts[cut]]
        n = group * 2 + half + (18 if cut == 1 else 0)
        return pltpu.make_async_remote_copy(
            src_ref=block,
            dst_ref=block,
            send_sem=share_sem.at[n],
            recv_sem=share_in_sem.at[n],
            device_id=partner,
            device_id_type=MESH,
        )

    def widen_halo(group, half, side, cut=None):
        first = node_rows + group * run + half * piece + side * mine_rows
        widen(first + (split if cut == 1 else 0), halo.at[group, side, half, :, cuts[cut]])

    early = {d: 0 if d[0] == 0 else 1 for d in sides}
    first_turns, second_turns = turns[: len(sides)], turns[len(sides) :]

    def corner_of(d, e):
        return group_of(d[0] + e[0], d[1] + e[1]), early[d]

    def comes(d):
        return {1: band > 0, 0: None, -1: band < bands - 1}[d[0]]

    def goes(d):
        return comes((-d[0], 0))

    def when(condition, act):
        if condition is None:
            act()
        else:
            pl.when(condition)(act)

    def comes_corner(d, e):
        return comes((d[0] + e[0], 0))

    def goes_corner(d, e):
        return comes(d) if d[0] else goes(e)

    for d in sides:
        when(goes(d), lambda: halo_copy(early[d], d).start())

    make_latent(1)
    for d in sides:

        def second_half():
            halo_copy(early[d], d).wait_send()
            halo_copy(1 - early[d], d).start()

        when(goes(d), second_half)
    for d in sides:
        when(comes(d), lambda: halo_copy(early[d], d).wait_recv())
        for t in first_turns:
            if t[0] == d:
                when(goes_corner(*t), lambda: corner_copy(*t).start())
        for cut in range(2):
            for t in second_turns:
                if t[0] == d:
                    when(goes_corner(*t), lambda: corner_copy(*t, cut).start())
    for d in sides:
        when(comes(d), lambda: share(group_of(*d), early[d], core).start())

    def later_latent(q, carry):
        make_latent(q)
        return carry

    lax.fori_loop(2, PARTS, later_latent, 0)
    for copy in [recv_w_copy, sender_copy] + vector_copies:
        copy.wait()
    for copy in weights[1:]:
        copy.wait_recv()
    project_recv(0)

    def later_project(q, carry):
        latent_copy(q).wait_recv()
        project_send(q)
        project_recv(q)
        return carry

    lax.fori_loop(1, PARTS, later_project, 0)
    for t in first_turns:
        when(goes_corner(*t), lambda: corner_copy(*t).wait_send())

    def widen_sent(q, carry):
        sent_copy(q).wait_recv()
        for h in range(2):
            widen(q * run + h * piece + other * mine_rows, sent_in.at[q, h])
        return carry

    lax.fori_loop(0, PARTS, widen_sent, 0)

    def widen_both(group, half):
        widen_halo(group, half, core)
        share(group, half, other).wait_recv()
        widen_halo(group, half, other)

    for d in sides:
        when(comes(d), lambda: widen_both(group_of(*d), early[d]))

    @pl.when(core == 0)
    def _():
        group_wait(STEPS - 1, 1).wait_send()

    @pl.when(core == 1)
    def _():
        group_wait(STEPS - 1).wait_send()

    for g in range(STEPS - 1):
        group_wait(g).wait_send()
    for g in range(STEPS):
        pass_on(g, core).wait_send()
    for copy in weights:
        copy.wait_send()
    for q in range(PARTS):
        latent_copy(q).wait_send()
        sent_copy(q).wait_send()

    for d in sides:

        def second_arrival():
            halo_copy(1 - early[d], d).wait_recv()
            share(group_of(*d), 1 - early[d], core).start()

        when(comes(d), second_arrival)

    def corner_arrival(t, cut=None):
        corner_copy(*t, cut).wait_recv()
        share(*corner_of(*t), core, cut).start()

    for t in first_turns:
        when(comes_corner(*t), lambda: corner_arrival(t))
    for d in sides:
        when(comes(d), lambda: widen_both(group_of(*d), 1 - early[d]))
    for t in first_turns:
        when(comes_corner(*t), lambda: widen_both(*corner_of(*t)))
    for cut in range(2):
        for t in second_turns:
            when(comes_corner(*t), lambda: corner_arrival(t, cut))
        for t in second_turns:
            when(comes_corner(*t), lambda: widen_halo(*corner_of(*t), core, cut))

    def widen_shared(t, cut):
        share(*corner_of(*t), other, cut).wait_recv()
        widen_halo(*corner_of(*t), other, cut)

    for cut in range(2):
        for t in second_turns:
            when(comes_corner(*t), lambda: widen_shared(t, cut))

    unroll = 32
    agg = (agg_even, agg_odd)

    agg_rows = agg[0].shape[0] // tiles

    def one_node(q, r):
        base = recv_base[pl.ds(q * mine_rows + r, tiles, stride=base_rows), :]
        first = (q * run + core * mine_rows + r) * DEGREE
        total = None
        for k in range(DEGREE):
            sender = table[pl.ds(sender_ref[first + k], tiles, stride=table_rows), :]
            term = half_silu(base + sender)
            total = term if total is None else total + term
        agg[q % 2][pl.ds(r, tiles, stride=agg_rows), :] = total

    def out_rows(q):
        return pl.ds(pl.multiple_of(q * run + core * mine_rows, mine_rows), mine_rows)

    def out_send(q):
        return pltpu.make_async_remote_copy(
            src_ref=out_buf.at[q],
            dst_ref=out_ref.at[out_rows(q)],
            send_sem=out_send_sem.at[q],
            recv_sem=out_in_sem.at[q],
            device_id=partner,
            device_id_type=MESH,
        )

    def finish(q, r, some, between=None):
        def scaled(side, t):
            value = agg[q % 2][pl.ds((side * (tiles // 2) + t) * agg_rows + r, some), :]
            return value * vectors[1, side, :, tile(t)]

        values = [(side, t, scaled(side, t)) for side in (other, core) for t in range(tiles // 2)]
        square = values[0][2] * values[0][2]
        for _, _, value in values[1:]:
            square = square + value * value
        mean = jnp.sum(square, axis=1, keepdims=True) / (2 * width)
        factor = lax.rsqrt(mean + 1e-05)
        span = pl.ds(pl.multiple_of(r, unroll), some)
        start = pl.multiple_of(q * run + core * mine_rows + r, unroll)
        for n, (side, t, value) in enumerate(values):
            if n == tiles // 2 and between is not None:
                between()
            held = latent_in[q, span, tile(t)] if side is other else latent[q, core, span, tile(t)]
            normed = value * factor * vectors[2, side, :, tile(t)]
            result = (held.astype(F32) + normed).astype(BF16)
            if side is other:
                out_buf[q, span, tile(t)] = result
            else:
                out_ref[pl.ds(start, some), tile(t)] = result

    for q in range(PARTS):

        def some_nodes(m, carry):
            for u in range(unroll):
                one_node(q, m * unroll + u)
            if q > 0:
                finish(q - 1, m * unroll, unroll)
            return carry

        lax.fori_loop(0, mine_rows // unroll, some_nodes, 0)
        if q > 0:
            out_send(q - 1).start()
    finish(PARTS - 1, 0, mine_rows, lambda: out_send(PARTS - 1).start())

    def drain_side(d):
        for half in range(2):
            share(group_of(*d), half, core).wait_send()

    for d in sides:
        when(goes(d), lambda: halo_copy(1 - early[d], d).wait_send())
        when(comes(d), lambda: drain_side(d))
    for t in first_turns:
        when(comes_corner(*t), lambda: share(*corner_of(*t), core).wait_send())
    for cut in range(2):
        for t in second_turns:
            when(goes_corner(*t), lambda: corner_copy(*t, cut).wait_send())
            when(comes_corner(*t), lambda: share(*corner_of(*t), core, cut).wait_send())
    for q in range(PARTS):
        out_send(q).wait()


def local(
    obs_features,
    obs_owner,
    obs_node,
    obs_count,
    edge_senders,
    obs_in_w,
    obs_in_b,
    obs_out_w,
    enc_w,
    enc_b,
    node_base,
    recv_w,
    send_w,
    edge_b,
    channel_scale,
    norm_gain,
):
    bands = lax.axis_size("band")
    sectors = lax.axis_size("sector")
    geo = bands * sectors
    pairs = geo // 2
    rows, embed = obs_features.shape
    node_rows, width = node_base.shape
    tiles = 2 * width // LANES
    run = node_rows // PARTS
    mine_rows = run // 2
    piece = mine_rows // 2
    slots = geo * SLOTS
    vmem = pl.BlockSpec(memory_space=pltpu.VMEM)
    smem = pl.BlockSpec(memory_space=pltpu.SMEM)
    hbm = pl.BlockSpec(memory_space=pl.ANY)
    dma = pltpu.SemaphoreType.DMA
    return pl.pallas_call(
        functools.partial(kernel, bands, sectors),
        out_shape=pltpu.VMEM((node_rows, width), BF16),
        in_specs=[smem] + [hbm] * 15,
        out_specs=vmem,
        scratch_shapes=[
            pltpu.VMEM((1, rows), jnp.int32),
            pltpu.VMEM((1, rows), jnp.int32),
            pltpu.SMEM((node_rows * DEGREE,), jnp.int32),
            pltpu.VMEM((1, embed), F32),
            pltpu.VMEM((1, width), F32),
            pltpu.VMEM((rows, embed), BF16),
            pltpu.VMEM((embed, embed), BF16),
            pltpu.VMEM((embed, embed), BF16),
            pltpu.VMEM((embed, width), BF16),
            pltpu.VMEM((3, 2, 1, width), F32),
            pltpu.VMEM((2, pairs // GROUP, LANES), jnp.int32),
            pltpu.VMEM((run, width), F32),
            pltpu.VMEM((run, LANES), F32),
            pltpu.VMEM((pairs, SLOTS, embed), BF16),
            pltpu.VMEM((2, pairs, SLOTS, embed), BF16),
            pltpu.VMEM((slots, width), BF16),
            pltpu.VMEM((node_rows, width), BF16),
            pltpu.VMEM((2, width, 2 * width), BF16),
            pltpu.VMEM((2, width, 2 * width), BF16),
            pltpu.VMEM((run, slots), BF16),
            pltpu.VMEM((PARTS, 2, mine_rows, width), BF16),
            pltpu.VMEM((PARTS, mine_rows, width), BF16),
            pltpu.VMEM((tiles * (node_rows + 9 * run + SKEW), LANES), F32),
            pltpu.VMEM((tiles * (PARTS * mine_rows + SKEW), LANES), F32),
            pltpu.VMEM((PARTS, 2, tiles, piece, LANES), BF16),
            pltpu.VMEM((PARTS, 2, tiles, piece, LANES), BF16),
            pltpu.VMEM((9, 2, 2, tiles, piece, LANES), BF16),
            pltpu.VMEM((tiles * (mine_rows + SKEW), LANES), F32),
            pltpu.VMEM((tiles * (mine_rows + SKEW), LANES), F32),
            pltpu.VMEM((PARTS, mine_rows, width), BF16),
            dma((15,)),
            dma((5,)),
            dma((5,)),
            dma((STEPS,)),
            dma((STEPS,)),
            dma((STEPS,)),
            dma((STEPS,)),
            dma((PARTS,)),
            dma((PARTS,)),
            dma((PARTS,)),
            dma((PARTS,)),
            dma((24,)),
            dma((24,)),
            dma((36,)),
            dma((36,)),
            dma((PARTS,)),
            dma((PARTS,)),
        ],
        compiler_params=pltpu.CompilerParams(
            collective_id=0, has_side_effects=True, vmem_limit_bytes=56 * 2**20
        ),
        name="encode_and_pass",
    )(
        obs_count,
        obs_owner.reshape(1, rows),
        obs_node.reshape(1, rows),
        edge_senders,
        obs_in_b.reshape(1, -1),
        enc_b.reshape(1, -1),
        edge_b.reshape(1, -1),
        channel_scale.reshape(1, -1),
        norm_gain.reshape(1, -1),
        obs_features,
        obs_in_w,
        obs_out_w,
        enc_w,
        node_base,
        recv_w,
        send_w,
    )


def solution(mesh):
    in_specs = (
        P(("band", "sector"), None),
        P(("band", "sector"), None),
        P(("band", "sector")),
        P(("band", "sector")),
        P(("band", "sector")),
        P(),
        P(),
        P(),
        P(None, "chan"),
        P("chan"),
        P(("band", "sector"), "chan"),
        P("chan", None),
        P("chan", None),
        P("chan"),
        P("chan"),
        P("chan"),
    )
    out_specs = P(("band", "sector"), "chan")
    return jax.shard_map(local, mesh=mesh, in_specs=in_specs, out_specs=out_specs, check_vma=False)
```
